32 devices in a mesh: dp: 2 (over x), ep: 16 (over z, y, core).
Axes of the slice: x: 2, y: 2, z: 4, core: 2. Of those that a mesh axis runs over, the one named last changes fastest.
Arguments:
- layer_input: bfloat16 [4096, 2048], P(('dp', 'ep')), may hold values from -6 to 6
- lengths: int32 [32], P(('dp', 'ep')), may hold values from 32 to 128, as said below
- routes: int32 [4096, 4], P(('dp', 'ep')), may hold values from 0 to 7, all different within a row; in each aligned block of 128 rows (0 to 127, 128 to 255, ...) at most 128 rows name the same one
- route_weight: bfloat16 [4096, 4], P(('dp', 'ep')), may hold values from 0.19921875 to 0.796875
- cotangent: bfloat16 [4096, 2048], P(('dp', 'ep')), may hold values from -6 to 6
- norm_gain: bfloat16 [2048], P(('dp', 'ep')), may hold values from 0.5 to 1.5
- w_qkv: bfloat16 [2048, 6144], P(('dp', 'ep')), may hold values from -0.125 to 0.125
- b_qkv: bfloat16 [6144], P(('dp', 'ep')), may hold values from -3 to 3
- w_out: bfloat16 [2048, 2048], P(('dp', 'ep')), may hold values from -0.5 to 0.5
- post_gain: bfloat16 [2048], P(('dp', 'ep')), may hold values from 0.5 to 1.5
- w_gate: bfloat16 [16, 2048, 704], P('ep'), may hold values from -0.125 to 0.125
- w_up: bfloat16 [16, 2048, 704], P('ep'), may hold values from -0.125 to 0.125
- w_down: bfloat16 [16, 704, 2048], P('ep'), may hold values from -0.3125 to 0.3125
- shared_gate: bfloat16 [2048, 5632], P(None, 'ep'), may hold values from -0.125 to 0.125
- shared_up: bfloat16 [2048, 5632], P(None, 'ep'), may hold values from -0.125 to 0.125
- shared_down: bfloat16 [5632, 2048], P('ep'), may hold values from -0.078125 to 0.078125
- shared_vector: bfloat16 [2048], P(('dp', 'ep')), may hold values from -0.125 to 0.125
Outputs:
- layer_output: bfloat16 [4096, 2048], P(('dp', 'ep'))
- input_grad: bfloat16 [4096, 2048], P(('dp', 'ep'))
- norm_gain_grad: float32 [2048], P(('dp', 'ep'))
- w_qkv_grad: float32 [2048, 6144], P(('dp', 'ep'))
- b_qkv_grad: float32 [6144], P(('dp', 'ep'))
- w_out_grad: float32 [2048, 2048], P(('dp', 'ep'))
- post_gain_grad: float32 [2048], P(('dp', 'ep'))
- w_gate_grad: float32 [16, 2048, 704], P('ep')
- w_up_grad: float32 [16, 2048, 704], P('ep')
- w_down_grad: float32 [16, 704, 2048], P('ep')
- shared_gate_grad: float32 [2048, 5632], P(None, 'ep')
- shared_up_grad: float32 [2048, 5632], P(None, 'ep')
- shared_down_grad: float32 [5632, 2048], P('ep')
- shared_vector_grad: float32 [2048], P(('dp', 'ep'))
The draws below stay inside these ranges and needn't reach their ends.
Inputs may be any that keep to these rules, and one draw needn't show every extreme that they name: `routes`: each row names 4 different experts. In the rows of one device no expert is named by more than 128 rows, a bound that some block reaches. `lengths`: some sequence uses all 128 slots.
All inputs are finite; a program needn't handle non-finite values.
Results may differ from the reference program's by a relative error of at most 0.018.
Values may be sent and summed in bfloat16 or wider, within the bound.
No kernel may reach another device: no remote copies, remote signals or barrier semaphores. Data moves between devices by JAX's collectives and lax.ppermute only.
A program may use at most 448 MiB of HBM per device.

```python
import math
import jax
import jax.numpy as jnp
import numpy as np
from jax import lax

D = 2048
HEADS = 16
HEAD_DIM = 128
FF_EXP = 1408
SHARED_FF = 5632
TOP = 4
HALVES = 2
TOK_DEV = 128
EXPERTS = 8
CAP = 128
SEQS = 32
TOKENS = 4096


def draw_lengths(key, part):
    key = jax.random.fold_in(key, 11)
    first_key, second_key = jax.random.split(key)
    drawn = jax.random.randint(first_key, (SEQS,), TOK_DEV // 4, TOK_DEV + 1)
    longest = jax.random.randint(second_key, (), 0, SEQS)
    return jnp.where(jnp.arange(SEQS) == longest, TOK_DEV, drawn).astype(jnp.int32)


def level_of(key, shape, pieces, smallest, top_value):
    loudness, own = 1.0, jax.random.fold_in(key, 6)
    for dim, blocks in pieces:
        heights = jnp.exp(jax.random.uniform(jax.random.fold_in(own, dim), (blocks,), jnp.float32, smallest / len(pieces), top_value / len(pieces)))
        loudness = loudness * jnp.repeat(heights, shape[dim] // blocks).reshape([-1 if axis == dim else 1 for axis in range(len(shape))])
    return loudness


def shared_out(stream_key, own, number, rows, count, top, reach, skew):
    ranking = jax.random.permutation(stream_key, count)
    crowded, ordinary = portions_of(count, rows * top, reach, skew, True), portions_of(count, rows * top, reach, skew, False)
    places = jnp.arange(count)

    def named(tallies, turn):
        used = int((tallies > 0).sum())
        fixed = max(1, used // 4)
        shifted = fixed + (places - fixed + turn * (used - fixed)) % max(1, count - fixed)
        return jnp.zeros((count,), jnp.int32).at[ranking[jnp.where(places < fixed, places, shifted)]].set(jnp.asarray(tallies, jnp.int32))

    tallies = jnp.where(number % 4 == 0, named(crowded, number // 4), named(ordinary, number - number // 4 - 1))
    mixed = jax.random.permutation(jax.random.fold_in(own, 3), count)
    giver, taker = mixed[0:count // 2 * 2:2], mixed[1:count // 2 * 2:2]
    margin = jnp.minimum(tallies[giver] - 1, reach - tallies[taker]) // 2
    margin = jnp.where((giver == ranking[0]) | (taker == ranking[0]) | (tallies[taker] == 0), 0, jnp.maximum(margin, 0))
    shifted = jax.random.randint(jax.random.fold_in(own, 4), (count // 2,), 0, 1 << 20) % (margin + 1)
    tallies = tallies.at[giver].add(-shifted).at[taker].add(shifted)
    labels = jnp.searchsorted(jnp.cumsum(tallies), jnp.arange(rows * top), side="right").astype(jnp.int32)
    grid = labels.reshape(top, rows).T
    grid = grid[jax.random.permutation(jax.random.fold_in(own, 1), rows)]
    turn = jax.random.randint(jax.random.fold_in(own, 2), (rows, 1), 0, top)
    return jnp.take_along_axis(grid, (jnp.arange(top)[None, :] + turn) % top, axis=1)


def portions_of(count, total, limit, lean, full):
    weights = [(1 << 20) // math.isqrt(standing ** lean) + 1 for standing in range(1, count + 1)]
    largest = limit if full else min(limit, max(-(-total // count), total * weights[0] // sum(weights)))
    least = 1 if total - largest >= count - 1 else 0
    holding, rest = [largest] + [least] * (count - 1), total - largest - least * (count - 1)
    while rest > 0:
        free = [i for i in range(1, count) if holding[i] < largest] or [i for i in range(1, count) if holding[i] < limit]
        mass, left = sum([weights[i] for i in free]), rest
        for i in free:
            addition = min(limit - holding[i], max(1, left * weights[i] // mass), rest)
            holding[i] = holding[i] + addition
            rest = rest - addition
    return np.array(holding)


def gaussian(stream_key, shape, deviation, reach, shards=(), kind=jnp.bfloat16):
    values = jax.random.normal(stream_key, shape, jnp.float32) * deviation
    if len(shards) > 0:
        values = level_of(stream_key, shape, shards, -0.22, 0.18) * values
    return jnp.clip(values, min=-reach, max=reach).astype(kind)


def setup_inputs(seed: int = 0) -> dict:
    key_of = jax.random.split(jax.random.key(seed), 18)
    layer_input = gaussian(key_of[0], (TOKENS, D), 1.0, 6.0, ((0, 32),))
    lengths = draw_lengths(jax.random.fold_in(key_of[17], 71), 0)
    routes_keys = jax.random.split(jax.random.fold_in(key_of[2], 1), TOKENS // TOK_DEV)
    routes_turns = jax.random.permutation(jax.random.fold_in(key_of[2], 3), TOKENS // TOK_DEV)
    routes = jax.vmap(lambda own, number: shared_out(jax.random.fold_in(key_of[2], 2), own, number, TOK_DEV, EXPERTS, TOP, CAP, 2))(routes_keys, routes_turns).reshape((TOKENS, TOP))
    route_weight = jnp.clip(0.19921875 + 0.59765625 * jax.random.uniform(key_of[3], (TOKENS, TOP), jnp.float32) ** level_of(key_of[3], (TOKENS, TOP), ((0, 32),), -0.2, 0.2), 0.19921875, 0.796875).astype(jnp.bfloat16)
    cotangent = gaussian(key_of[4], (TOKENS, D), 1.0, 6.0, ((0, 32),))
    norm_gain = jnp.clip(1.0 + 0.1 * jax.random.normal(key_of[5], (D,), jnp.float32), 0.5, 1.5).astype(jnp.bfloat16)
    w_qkv = gaussian(key_of[6], (D, 3 * D), D ** -0.5, 0.125, ((0, 32),))
    b_qkv = gaussian(key_of[7], (3 * D,), 0.5, 3.0, ((0, 32),))
    w_out = gaussian(key_of[8], (D, D), (D // 16) ** -0.5, 0.5, ((0, 32),))
    post_gain = jnp.clip(1.0 + 0.1 * jax.random.normal(key_of[9], (D,), jnp.float32), 0.5, 1.5).astype(jnp.bfloat16)
    w_gate = gaussian(key_of[10], (EXPERTS * HALVES, D, FF_EXP // HALVES), D ** -0.5, 0.125, ((0, 16),))
    w_up = gaussian(key_of[11], (EXPERTS * HALVES, D, FF_EXP // HALVES), D ** -0.5, 0.125, ((0, 16),))
    w_down = gaussian(key_of[12], (EXPERTS * HALVES, FF_EXP // HALVES, D), (FF_EXP // 4) ** -0.5, 0.3125, ((0, 16),))
    shared_gate = gaussian(key_of[13], (D, SHARED_FF), D ** -0.5, 0.125, ((1, 16),))
    shared_up = gaussian(key_of[14], (D, SHARED_FF), D ** -0.5, 0.125, ((1, 16),))
    shared_down = gaussian(key_of[15], (SHARED_FF, D), SHARED_FF ** -0.5, 0.078125, ((0, 16),))
    shared_vector = gaussian(key_of[16], (D,), D ** -0.5, 0.125, ((0, 32),))
    return dict(layer_input=layer_input, lengths=lengths, routes=routes, route_weight=route_weight, cotangent=cotangent, norm_gain=norm_gain, w_qkv=w_qkv, b_qkv=b_qkv, w_out=w_out, post_gain=post_gain, w_gate=w_gate, w_up=w_up, w_down=w_down, shared_gate=shared_gate, shared_up=shared_up, shared_down=shared_down, shared_vector=shared_vector)


@jax.custom_vjp
def low(v):
    return lax.optimization_barrier(v.astype(jnp.bfloat16)).astype(jnp.float32)

@jax.custom_vjp
def low_back(v):
    return v

def low_keep(v):
    return (low(v), None)

def low_pass(kept, grad):
    return (grad,)

def back_keep(v):
    return (v, None)

def back_low(kept, grad):
    return (low(grad),)
low.defvjp(low_keep, low_pass)
low_back.defvjp(back_keep, back_low)
epsilon = 1e-06
rope_base = 1000000.0
highest = lax.Precision.HIGHEST

def rms_norm(values, gain_row):
    return values * lax.rsqrt(lax.optimization_barrier(jnp.mean(values * values, axis=-1, keepdims=True)) + epsilon) * gain_row

def rope_tables(row_count, head_size):
    inverse = rope_base ** (-jnp.arange(0, head_size, 2, dtype=jnp.float32) / head_size)
    angles = jnp.arange(row_count, dtype=jnp.float32)[:, None] * inverse[None, :]
    angles = jnp.concatenate([angles, angles], axis=-1)
    return (jnp.cos(angles)[:, None, :], jnp.sin(angles)[:, None, :])

def rotate(values, cosine_table, sine_table):
    middle_index = values.shape[-1] // 2
    turned = jnp.concatenate([-values[..., middle_index:], values[..., :middle_index]], axis=-1)
    return values * cosine_table + turned * sine_table

def block_forward(inputs, valid_rows, routes, route_weight, params):
    norm_gain, w_qkv, b_qkv, w_out, post_gain, w_gate, w_up, w_down, shared_gate, shared_up, shared_down, shared_vector = params
    seq_count, row_count, feature_count = inputs.shape
    normed = low(rms_norm(inputs, norm_gain))
    projected = low_back(jnp.einsum('std,de->ste', normed, w_qkv, precision=highest) + b_qkv)
    head_shape = (seq_count, row_count, HEADS, HEAD_DIM)
    cosine_table, sine_table = rope_tables(row_count, HEAD_DIM)
    query = low(rotate(projected[..., :feature_count].reshape(head_shape), cosine_table, sine_table))
    key_rows = low(rotate(projected[..., feature_count:2 * feature_count].reshape(head_shape), cosine_table, sine_table))
    value_rows = low(projected[..., 2 * feature_count:].reshape(head_shape))
    scores = low_back(jnp.einsum('sqhd,skhd->shqk', query, key_rows, precision=highest) / math.sqrt(HEAD_DIM))
    positions = jnp.arange(row_count, dtype=jnp.int32)
    causal = (positions[None, :] <= positions[:, None])[None, None]
    allowed = causal & (valid_rows[:, None, None, :] > 0)
    scores = jnp.where(allowed, scores, -1e+30)
    probabilities = low(jax.nn.softmax(scores, axis=-1))
    context = low(jnp.einsum('shqk,skhd->sqhd', probabilities, value_rows, precision=highest).reshape(seq_count, row_count, feature_count))
    attended = low_back(jnp.einsum('std,de->ste', context, w_out, precision=highest))
    residual = (inputs + attended).reshape(-1, feature_count)
    normed_second = low(rms_norm(residual, post_gain))

    @jax.checkpoint
    def one_part(carry, item):
        gate_weight, up_weight, down_weight, part_index = item
        gate_pre = low_back(jnp.dot(normed_second, gate_weight, precision=highest))
        up_pre = low_back(jnp.dot(normed_second, up_weight, precision=highest))
        middle = low(jax.nn.silu(gate_pre) * up_pre)
        result = low_back(low(jnp.dot(middle, down_weight, precision=highest)))
        coefficient = lax.optimization_barrier(jnp.sum(jnp.where(routes == part_index // HALVES, route_weight, 0.0), axis=1))
        return (carry + coefficient[:, None] * result, None)
    part_ids = jnp.arange(w_gate.shape[0], dtype=jnp.int32)
    routed, _ = lax.scan(one_part, jnp.zeros_like(residual), (w_gate, w_up, w_down, part_ids))
    shared_gate_pre = low_back(jnp.dot(normed_second, shared_gate, precision=highest))
    shared_up_pre = low_back(jnp.dot(normed_second, shared_up, precision=highest))
    shared_mid = low(jax.nn.silu(shared_gate_pre) * shared_up_pre)
    shared_result = low_back(jnp.dot(shared_mid, shared_down, precision=highest))
    gate_value = jax.nn.sigmoid(jnp.dot(normed_second, shared_vector, precision=highest))
    combined = residual + routed + gate_value[:, None] * shared_result
    kept = valid_rows.reshape(-1)[:, None] > 0
    return jnp.where(kept, combined, 0.0).reshape(seq_count, row_count, feature_count)

def reference(layer_input, lengths, routes, route_weight, cotangent, norm_gain, w_qkv, b_qkv, w_out, post_gain, w_gate, w_up, w_down, shared_gate, shared_up, shared_down, shared_vector):
    params = tuple((weight_array.astype(jnp.float32) for weight_array in (norm_gain, w_qkv, b_qkv, w_out, post_gain, w_gate, w_up, w_down, shared_gate, shared_up, shared_down, shared_vector)))
    per_block = math.gcd(SEQS, max(1, 4096 // TOK_DEV))
    block_count = SEQS // per_block
    valid = (jnp.arange(TOK_DEV, dtype=jnp.int32)[None, :] < lengths[:, None]).astype(jnp.int32)
    items = (layer_input.astype(jnp.float32).reshape(block_count, per_block, TOK_DEV, D), valid.reshape(block_count, per_block, TOK_DEV), routes.reshape(block_count, per_block * TOK_DEV, TOP), route_weight.astype(jnp.float32).reshape(block_count, per_block * TOK_DEV, TOP), cotangent.astype(jnp.float32).reshape(block_count, per_block, TOK_DEV, D))

    def block_step(totals, item):
        block_inputs, block_valid, block_routes, block_weight, block_grad = item

        def forward(inputs, weights):
            return block_forward(inputs, block_valid, block_routes, block_weight, weights)
        result, pullback = jax.vjp(forward, block_inputs, params)
        inputs_grad, weight_grads = pullback(block_grad)
        totals = jax.tree.map(jnp.add, totals, weight_grads)
        return (totals, (result.astype(jnp.bfloat16), inputs_grad.astype(jnp.bfloat16)))
    zero_grads = jax.tree.map(jnp.zeros_like, params)
    grads, (outputs, input_grads) = lax.scan(block_step, zero_grads, items)
    return (outputs.reshape(TOKENS, D), input_grads.reshape(TOKENS, D), grads[0], grads[1], grads[2], grads[3], grads[4], grads[5], grads[6], grads[7], grads[8], grads[9], grads[10], grads[11])
```

```python
import math

import jax
import jax.numpy as jnp
from jax import lax
from jax.sharding import PartitionSpec as P

HEADS = 16
HEAD_DIM = 128
TOP = 4
HALVES = 2
CORES = 2
LINE = 4


epsilon = 1e-06
rope_base = 1000000.0
bf16 = jnp.bfloat16
f32 = jnp.float32


def unit_norm(values):
    factor = lax.rsqrt(jnp.mean(values * values, axis=-1, keepdims=True) + epsilon)
    return (values * factor, factor)


def norm_backward(incoming, unit_rows, factor, gain_row):
    scaled = incoming * gain_row
    inner_mean = jnp.mean(scaled * unit_rows, axis=-1, keepdims=True)
    return factor * (scaled - unit_rows * inner_mean)


def rope_tables(row_count, head_size):
    inverse = rope_base ** (-jnp.arange(0, head_size, 2, dtype=f32) / head_size)
    angles = jnp.arange(row_count, dtype=f32)[:, None] * inverse[None, :]
    angles = jnp.concatenate([angles, angles], axis=-1)
    return (jnp.cos(angles)[:, None, :], jnp.sin(angles)[:, None, :])


def turn_half(values):
    middle_index = values.shape[-1] // 2
    return jnp.concatenate([-values[..., middle_index:], values[..., :middle_index]], axis=-1)


def rotate(values, cosine_table, sine_table):
    return values * cosine_table + turn_half(values) * sine_table


def rotate_back(incoming, cosine_table, sine_table):
    return incoming * cosine_table - turn_half(incoming * sine_table)


def dot(left, right, dims):
    return lax.dot_general(left, right, (dims, ((), ())), preferred_element_type=f32)


class Grid:
    def __init__(self):
        self.groups = lax.axis_size("dp")
        self.owners = lax.axis_size("ep")
        self.chips = self.owners // CORES
        self.na = math.gcd(LINE, self.chips)
        self.nb = self.chips // self.na
        self.group = lax.axis_index("dp")
        me = lax.axis_index("ep")
        self.chip = me // CORES
        self.core = me % CORES
        self.a = self.chip // self.nb
        self.b = self.chip % self.nb

    def place(self, a, b, c):
        return ((a % self.na) * self.nb + b % self.nb) * CORES + c % CORES

    def hop(self, values, da=0, db=0, dc=0):
        pairs = [
            (self.place(a, b, c), self.place(a + da, b + db, c + dc))
            for a in range(self.na)
            for b in range(self.nb)
            for c in range(CORES)
        ]
        return lax.ppermute(values, "ep", pairs)

    def cross(self, values, shift):
        pairs = [(g, (g + shift) % self.groups) for g in range(self.groups)]
        return lax.ppermute(values, "dp", pairs)

    def plane(self, block):
        slots = []
        for da in range(self.na):
            along = self.hop(block, da=-da) if da else block
            rows = [along]
            for db in range(1, self.nb):
                rows.append(self.hop(along, db=-db))
            slots.append(jnp.concatenate(rows, axis=0))
        return slots

    def both(self, slots):
        return [jnp.concatenate([rows, self.hop(rows, dc=1)], axis=0) for rows in slots]

    def plane_sum(self, slots):
        total = None
        for da in list(range(1, self.na)) + [0]:
            terms = slots[da]
            here = terms[0].astype(f32)
            for db in range(1, self.nb):
                here = here + self.hop(terms[db], db=db).astype(f32)
            if da:
                here = self.hop(here.astype(bf16), da=da).astype(f32)
            total = here if total is None else total + here
        return total

    def pair_sum(self, terms):
        return (terms[0].astype(f32) + self.hop(terms[1], dc=1).astype(f32)).astype(bf16)

    def absolute(self, relative):
        turned = jnp.roll(relative, self.a, axis=0)
        return jnp.roll(turned, self.b, axis=1)

    def relative(self, by_place):
        turned = jnp.roll(by_place, -self.a, axis=0)
        return jnp.roll(turned, -self.b, axis=1)

    def same_core(self):
        return [[k * CORES + c for k in range(self.chips)] for c in range(CORES)]

    def swap(self, blocks):
        return lax.all_to_all(
            blocks,
            "ep",
            split_axis=0,
            concat_axis=0,
            tiled=True,
            axis_index_groups=self.same_core(),
        )

    def scatter_core(self, terms, axis):
        mine = lax.dynamic_index_in_dim(terms, self.core, axis, keepdims=False)
        other = lax.dynamic_index_in_dim(terms, 1 - self.core, axis, keepdims=False)
        return mine.astype(f32) + self.hop(other, dc=1).astype(f32)

    def scatter_groups(self, terms):
        total = lax.dynamic_index_in_dim(terms, self.group, 0, keepdims=False).astype(f32)
        for shift in range(1, self.groups):
            there = (self.group + shift) % self.groups
            piece = lax.dynamic_index_in_dim(terms, there, 0, keepdims=False)
            total = total + self.cross(piece, shift).astype(f32)
        return total

    def scatter_rows(self, terms):
        total = lax.dynamic_index_in_dim(terms, self.b, 1, keepdims=False).astype(f32)
        for db in range(1, self.nb):
            there = (self.b + db) % self.nb
            piece = lax.dynamic_index_in_dim(terms, there, 1, keepdims=False)
            total = total + self.hop(piece, db=db).astype(f32)
        terms = total.astype(terms.dtype)
        total = lax.dynamic_index_in_dim(terms, self.a, 0, keepdims=False).astype(f32)
        for da in range(1, self.na):
            there = (self.a + da) % self.na
            piece = lax.dynamic_index_in_dim(terms, there, 0, keepdims=False)
            total = total + self.hop(piece, da=da).astype(f32)
        return total

    def everywhere(self, small):
        parts = [small] + [self.cross(small, -shift) for shift in range(1, self.groups)]
        level = jnp.stack(parts)
        parts = [level] + [self.hop(level, db=-db) for db in range(1, self.nb)]
        level = jnp.stack(parts, axis=1)
        parts = [level] + [self.hop(level, da=-da) for da in range(1, self.na)]
        level = jnp.stack(parts, axis=1)
        return jnp.stack([level, self.hop(level, dc=1)], axis=3)


def expert_rows(rows, grads, scale_routed, scale_shared, into, out_weights, routed_units):
    units = into.shape[1] // 2
    pre = dot(rows, into, ((1,), (0,)))
    gate_pre, up_pre = pre[:, :units], pre[:, units:]
    back = dot(grads, out_weights, ((1,), (1,)))
    is_routed = lax.broadcasted_iota(jnp.int32, (1, units), 1) < routed_units
    scale = jnp.where(is_routed, scale_routed[:, None], scale_shared[:, None])
    gate_sigmoid = jax.nn.sigmoid(gate_pre)
    silu = gate_pre * gate_sigmoid
    middle = silu * up_pre
    inner = jnp.sum(jnp.where(is_routed, 0.0, middle * back), axis=1)
    scaled_middle = (scale * middle).astype(bf16)
    back = scale * back
    grad_gate = (back * up_pre * gate_sigmoid * (1.0 + gate_pre * (1.0 - gate_sigmoid))).astype(
        bf16
    )
    grad_up = (back * silu).astype(bf16)
    return scaled_middle, jnp.concatenate([grad_gate, grad_up], axis=1), inner


def local(
    layer_input,
    lengths,
    routes,
    route_weight,
    cotangent,
    norm_gain,
    w_qkv,
    b_qkv,
    w_out,
    post_gain,
    w_gate,
    w_up,
    w_down,
    shared_gate,
    shared_up,
    shared_down,
    shared_vector,
):
    grid = Grid()
    row_count, feature_count = layer_input.shape
    groups, owners, chips, na, nb = grid.groups, grid.owners, grid.chips, grid.na, grid.nb
    devices = groups * owners
    heads_here = HEADS // chips
    width = heads_here * HEAD_DIM
    routed_units = w_gate.shape[2]
    shared_units = shared_gate.shape[1]
    units = routed_units + shared_units
    positions = jnp.arange(row_count, dtype=jnp.int32)

    x_slots = grid.plane(layer_input)
    small = jnp.concatenate([norm_gain, post_gain, shared_vector, b_qkv]).astype(f32)
    small_count = small.shape[0]
    small = jnp.pad(small, (0, -small_count % row_count))
    meta = jnp.concatenate(
        [
            routes.T.astype(f32),
            route_weight.T.astype(f32),
            jnp.broadcast_to(lengths.astype(f32)[:, None], (1, row_count)),
            small.reshape(-1, row_count),
        ],
        axis=0,
    )
    meta_all = grid.everywhere(meta)
    flat_meta = meta_all.reshape(devices, *meta.shape)
    index = jnp.arange(devices, dtype=jnp.int32)
    ig, ia, ib, ic = (
        index // owners,
        index // (nb * CORES) % na,
        index // CORES % nb,
        index % CORES,
    )
    from_here = (
        ((ig - grid.group) % groups * na + (ia - grid.a) % na) * nb + (ib - grid.b) % nb
    ) * CORES + (ic - grid.core) % CORES
    small_all = jnp.take(flat_meta[:, 2 * TOP + 1 :], from_here, axis=0).reshape(devices, -1)
    own_features = norm_gain.shape[0]
    gains_in = small_all[:, :own_features].reshape(-1)
    gains_post = small_all[:, own_features : 2 * own_features].reshape(-1)
    gate_vector = small_all[:, 2 * own_features : 3 * own_features].reshape(-1)
    qkv_bias = small_all[:, 3 * own_features : small_count].reshape(3, chips, width)
    bias_here = lax.dynamic_index_in_dim(qkv_bias, grid.chip, 1, keepdims=False).reshape(-1)

    own_rows = w_qkv.shape[0]
    sliced = jnp.transpose(w_qkv.reshape(own_rows, 3, chips, width), (2, 0, 1, 3))
    by_chip = grid.swap(sliced.reshape(chips, own_rows, 3 * width))
    by_core = jnp.zeros((chips, CORES, own_rows, 3 * width), bf16)
    by_core = lax.dynamic_update_slice(by_core, by_chip[:, None], (0, grid.core, 0, 0))
    by_core = lax.dynamic_update_slice(
        by_core, grid.hop(by_chip, dc=1)[:, None], (0, 1 - grid.core, 0, 0)
    )
    by_core = by_core.reshape(-1, 3 * width)
    heads_weight = jnp.zeros((groups, *by_core.shape), bf16)
    for shift in range(groups):
        piece = grid.cross(by_core, shift) if shift else by_core
        heads_weight = lax.dynamic_update_slice(
            heads_weight, piece[None], ((grid.group - shift) % groups, 0, 0)
        )
    heads_weight = heads_weight.reshape(feature_count, 3 * width)
    out_weight = lax.all_gather(w_out, ("dp", "ep"), axis=0, tiled=True)

    valid_rows = positions < lengths[0]
    grad_rows = jnp.where(valid_rows[:, None], cotangent, jnp.zeros_like(cotangent))
    grad_plane = grid.plane(grad_rows)
    grad_slots = grid.both(grad_plane)

    inputs = layer_input.astype(f32)
    plane_rows = jnp.concatenate(x_slots, axis=0).astype(f32)
    plane_unit, _ = unit_norm(plane_rows)
    normed_first = (plane_unit * gains_in).astype(bf16)
    projected = dot(normed_first, heads_weight, ((1,), (0,))) + bias_here
    cosine_table, sine_table = rope_tables(row_count, HEAD_DIM)
    head_shape = (chips, row_count, heads_here, HEAD_DIM)
    query_low = rotate(
        projected[:, :width].reshape(head_shape), cosine_table, sine_table
    ).astype(bf16)
    key_low = rotate(
        projected[:, width : 2 * width].reshape(head_shape), cosine_table, sine_table
    ).astype(bf16)
    value_low = projected[:, 2 * width :].reshape(head_shape).astype(bf16)
    plane_lengths = meta_all[0, :, :, 0, 2 * TOP, 0].reshape(chips, 1)
    plane_valid = positions[None, :] < plane_lengths.astype(jnp.int32)
    allowed = (positions[None, None, :] <= positions[None, :, None]) & plane_valid[:, None, :]
    root_size = math.sqrt(HEAD_DIM)
    scores = (
        jnp.einsum("nqhd,nkhd->nhqk", query_low, key_low, preferred_element_type=f32) / root_size
    )
    scores = jnp.where(allowed[:, None], scores, -1e30)
    probabilities = jax.nn.softmax(scores, axis=-1)
    probs_low = probabilities.astype(bf16)
    context_here = jnp.einsum("nhqk,nkhd->nqhd", probs_low, value_low, preferred_element_type=f32)
    context_here = context_here.astype(bf16).reshape(na, nb, row_count, width)
    sent = grid.absolute(context_here).reshape(chips, row_count, width)
    context = jnp.transpose(grid.swap(sent), (1, 0, 2)).reshape(row_count, feature_count)
    residual = inputs + dot(context, out_weight, ((1,), (0,)))
    unit_second, factor_second = unit_norm(residual)
    normed_second = (unit_second * gains_post).astype(bf16)

    expert = lax.axis_index("ep") // HALVES
    into = jnp.concatenate([w_gate[0], shared_gate, w_up[0], shared_up], axis=1)
    out_of = jnp.concatenate([w_down[0], shared_down], axis=0)
    hits = meta_all[..., :TOP, :] == expert.astype(f32)
    route_scale = jnp.sum(jnp.where(hits, meta_all[..., TOP : 2 * TOP, :], 0.0), axis=-2)
    route_scale = jnp.transpose(route_scale, (0, 1, 3, 2, 4)).reshape(groups, na, -1)

    def slot_work(rows, grads, scale):
        gate_logit = dot(rows, gate_vector.astype(bf16), ((1,), (0,)))
        group_sigmoid = jax.nn.sigmoid(gate_logit)
        middle, grad_pre, inner = expert_rows(
            rows, grads, scale, group_sigmoid, into, out_of, routed_units
        )
        return middle, grad_pre, inner * group_sigmoid * (1.0 - group_sigmoid)

    second_plane = grid.plane(normed_second)
    second_slots = grid.both(second_plane)
    slot_shape = (CORES, nb, row_count, feature_count)
    worked = [
        slot_work(second_slots[s], grad_slots[s], route_scale[0, s]) for s in range(na)
    ]
    back_terms, out_terms = [], []
    for middle, grad_pre, logit_grad in worked:
        term = dot(grad_pre, into, ((1,), (1,))) + logit_grad[:, None] * gate_vector
        back_terms.append(grid.pair_sum(term.astype(bf16).reshape(slot_shape)))
        out_term = dot(middle, out_of, ((1,), (0,)))
        out_terms.append(grid.pair_sum(out_term.astype(bf16).reshape(slot_shape)))
    second_grad = grid.plane_sum(back_terms)
    mixed = grid.plane_sum(out_terms)
    combined = residual + mixed
    output = jnp.where(valid_rows[:, None], combined, 0.0).astype(bf16)

    def weight_grads(rows, grads, middles, grad_pres):
        rows, grads = jnp.concatenate(rows), jnp.concatenate(grads)
        middles, grad_pres = jnp.concatenate(middles), jnp.concatenate(grad_pres)
        columns = (0, routed_units, units, units + routed_units, 2 * units)
        into_grads = [
            dot(rows, grad_pres[:, lo:hi], ((0,), (0,))) for lo, hi in zip(columns, columns[1:])
        ]
        out_grads = [
            dot(middles[:, lo:hi], grads, ((0,), (0,)))
            for lo, hi in ((0, routed_units), (routed_units, units))
        ]
        return into_grads + out_grads

    logit_all = jnp.concatenate([w[2] for w in worked])
    vector_grad = dot(logit_all[None], jnp.concatenate(second_slots).astype(f32), ((1,), (0,)))[0]
    totals = weight_grads(
        second_slots, grad_slots, [w[0] for w in worked], [w[1] for w in worked]
    )
    for shift in range(1, groups):
        if groups > 2:
            totals, second_plane, grad_plane = lax.optimization_barrier(
                (totals, second_plane, grad_plane)
            )
        far_rows = grid.both([grid.cross(rows, -shift) for rows in second_plane])
        far_grads = grid.both([grid.cross(rows, -shift) for rows in grad_plane])
        far = [slot_work(far_rows[s], far_grads[s], route_scale[shift, s]) for s in range(na)]
        more = weight_grads(far_rows, far_grads, [w[0] for w in far], [w[1] for w in far])
        totals = [total + extra for total, extra in zip(totals, more)]

    grad_float = grad_rows.astype(f32)
    post_gain_grad = jnp.sum(second_grad * unit_second, axis=0)
    residual_grad = grad_float + norm_backward(
        second_grad, unit_second, factor_second, gains_post
    )
    attended_grad = residual_grad.astype(bf16)
    context_grad = dot(attended_grad, out_weight, ((1,), (1,))).astype(bf16)
    sent = jnp.transpose(context_grad.reshape(row_count, chips, width), (1, 0, 2))
    arrived = grid.relative(grid.swap(sent).reshape(na, nb, row_count, width))
    context_grad = arrived.reshape(head_shape)
    probs_grad = jnp.einsum("nqhd,nkhd->nhqk", context_grad, value_low, preferred_element_type=f32)
    value_grad = jnp.einsum("nhqk,nqhd->nkhd", probs_low, context_grad, preferred_element_type=f32)
    score_grad = probabilities * (
        probs_grad - jnp.sum(probabilities * probs_grad, axis=-1, keepdims=True)
    )
    score_grad = score_grad.astype(bf16)
    query_grad = (
        jnp.einsum("nhqk,nkhd->nqhd", score_grad, key_low, preferred_element_type=f32) / root_size
    )
    key_grad = (
        jnp.einsum("nhqk,nqhd->nkhd", score_grad, query_low, preferred_element_type=f32)
        / root_size
    )
    plane_count = chips * row_count
    projected_grad = jnp.concatenate(
        [
            rotate_back(query_grad, cosine_table, sine_table).reshape(plane_count, width),
            rotate_back(key_grad, cosine_table, sine_table).reshape(plane_count, width),
            value_grad.reshape(plane_count, width),
        ],
        axis=1,
    ).astype(bf16)
    first_terms = dot(projected_grad, heads_weight, ((1,), (1,))).astype(bf16)
    slot_first = first_terms.reshape(na, nb, row_count, feature_count)
    first_grad = grid.plane_sum([slot_first[s] for s in range(na)])
    unit_first, factor_first = unit_norm(inputs)
    input_part = norm_backward(first_grad, unit_first, factor_first, gains_in)
    layer_grad = (residual_grad + input_part).astype(bf16)

    out_weight_grad = dot(context, attended_grad, ((0,), (0,))).astype(bf16)
    out_weight_grad = grid.scatter_core(
        out_weight_grad.reshape(groups, na, nb, CORES, own_rows, feature_count), 3
    )
    out_weight_grad = grid.scatter_groups(out_weight_grad.astype(bf16))
    out_weight_grad = grid.scatter_rows(out_weight_grad.astype(bf16))

    qkv_grad = dot(normed_first, projected_grad, ((0,), (0,))).astype(bf16)
    qkv_grad = grid.scatter_core(qkv_grad.reshape(groups, chips, CORES, own_rows, 3 * width), 2)
    qkv_grad = grid.scatter_groups(qkv_grad.astype(bf16)).astype(bf16)
    qkv_grad = grid.swap(qkv_grad).reshape(chips, own_rows, 3, width)
    qkv_weight_grad = jnp.transpose(qkv_grad, (1, 2, 0, 3)).reshape(own_rows, -1).astype(f32)

    gain_grad = jnp.sum(first_terms.astype(f32) * plane_unit, axis=0)
    bias_grad = jnp.zeros((3, chips, width), f32)
    bias_grad = lax.dynamic_update_slice(
        bias_grad,
        jnp.sum(projected_grad.astype(f32), axis=0).reshape(3, 1, width),
        (0, grid.chip, 0),
    )
    vectors = jnp.concatenate(
        [
            gain_grad.reshape(devices, -1),
            post_gain_grad.reshape(devices, -1),
            vector_grad.reshape(devices, -1),
            bias_grad.reshape(devices, -1),
        ],
        axis=1,
    ).reshape(groups, na, nb, CORES, -1)
    vectors = grid.scatter_core(vectors, 3)
    vectors = grid.scatter_groups(vectors)
    vectors = grid.scatter_rows(vectors)
    return (
        output,
        layer_grad,
        vectors[:own_features],
        qkv_weight_grad,
        vectors[3 * own_features :],
        out_weight_grad,
        vectors[own_features : 2 * own_features],
        totals[0][None],
        totals[2][None],
        totals[4][None],
        totals[1],
        totals[3],
        totals[5],
        vectors[2 * own_features : 3 * own_features],
    )


def solution(mesh):
    rows = P(("dp", "ep"), None)
    split = P(("dp", "ep"))
    parts = P("ep", None, None)
    return jax.shard_map(
        local,
        mesh=mesh,
        in_specs=(
            rows,
            split,
            rows,
            rows,
            rows,
            split,
            rows,
            split,
            rows,
            split,
            parts,
            parts,
            parts,
            P(None, "ep"),
            P(None, "ep"),
            P("ep", None),
            split,
        ),
        out_specs=(
            rows,
            rows,
            split,
            rows,
            split,
            rows,
            split,
            parts,
            parts,
            parts,
            P(None, "ep"),
            P(None, "ep"),
            P("ep", None),
            split,
        ),
        check_vma=False,
    )
```

```python
import functools
import math

import jax
import jax.numpy as jnp
from jax import lax
from jax.experimental import pallas as pl
from jax.experimental.pallas import tpu as pltpu
from jax.sharding import PartitionSpec as P

HEADS = 16
HEAD_DIM = 128
TOP = 4
HALVES = 2
CORES = 2
LINE = 4
LANES = 128
TILE = 512
VMEM = 56 << 20


epsilon = 1e-06
rope_base = 1000000.0
bf16 = jnp.bfloat16
f32 = jnp.float32


def unit_norm(values):
    factor = lax.rsqrt(jnp.mean(values * values, axis=-1, keepdims=True) + epsilon)
    return (values * factor, factor)


def norm_backward(incoming, unit_rows, factor, gain_row):
    scaled = incoming * gain_row
    inner_mean = jnp.mean(scaled * unit_rows, axis=-1, keepdims=True)
    return factor * (scaled - unit_rows * inner_mean)


def rope_tables(row_count, head_size):
    inverse = rope_base ** (-jnp.arange(0, head_size, 2, dtype=f32) / head_size)
    angles = jnp.arange(row_count, dtype=f32)[:, None] * inverse[None, :]
    angles = jnp.concatenate([angles, angles], axis=-1)
    return (jnp.cos(angles)[:, None, :], jnp.sin(angles)[:, None, :])


def dot(left, right, dims):
    return lax.dot_general(left, right, (dims, ((), ())), preferred_element_type=f32)


def tie(*values):
    return lax.optimization_barrier(values)


class Grid:
    def __init__(self):
        self.groups = lax.axis_size("dp")
        self.owners = lax.axis_size("ep")
        self.chips = self.owners // CORES
        self.na = math.gcd(LINE, self.chips)
        self.nb = self.chips // self.na
        self.group = lax.axis_index("dp")
        me = lax.axis_index("ep")
        self.chip = me // CORES
        self.core = me % CORES
        self.a = self.chip // self.nb
        self.b = self.chip % self.nb

    def place(self, a, b, c):
        return ((a % self.na) * self.nb + b % self.nb) * CORES + c % CORES

    def hop(self, values, da=0, db=0, dc=0):
        pairs = [
            (self.place(a, b, c), self.place(a + da, b + db, c + dc))
            for a in range(self.na)
            for b in range(self.nb)
            for c in range(CORES)
        ]
        return lax.ppermute(values, "ep", pairs)

    def cross(self, values, shift):
        pairs = [(g, (g + shift) % self.groups) for g in range(self.groups)]
        return lax.ppermute(values, "dp", pairs)

    def row(self, block):
        return [block] + [self.hop(block, db=db) for db in range(1, self.nb)]

    def row_sum(self, terms):
        total = terms[0].astype(f32)
        for db in range(1, self.nb):
            total = total + self.hop(terms[db], db=-db).astype(f32)
        return total

    def core_sum(self, terms):
        return (terms[0].astype(f32) + self.hop(terms[1], dc=1).astype(f32)).astype(bf16)

    def same_core(self):
        return [[k * CORES + c for k in range(self.chips)] for c in range(CORES)]

    def swap(self, blocks):
        return lax.all_to_all(
            blocks,
            "ep",
            split_axis=0,
            concat_axis=0,
            tiled=True,
            axis_index_groups=self.same_core(),
        )

    def scatter_core(self, terms, axis):
        mine = lax.dynamic_index_in_dim(terms, self.core, axis, keepdims=False)
        other = lax.dynamic_index_in_dim(terms, 1 - self.core, axis, keepdims=False)
        return mine.astype(f32) + self.hop(other, dc=1).astype(f32)

    def scatter_groups(self, terms):
        total = lax.dynamic_index_in_dim(terms, self.group, 0, keepdims=False).astype(f32)
        for shift in range(1, self.groups):
            there = (self.group + shift) % self.groups
            piece = lax.dynamic_index_in_dim(terms, there, 0, keepdims=False)
            total = total + self.cross(piece, shift).astype(f32)
        return total

    def scatter_row(self, terms):
        total = lax.dynamic_index_in_dim(terms, self.b, 1, keepdims=False).astype(f32)
        for db in range(1, self.nb):
            there = (self.b + db) % self.nb
            piece = lax.dynamic_index_in_dim(terms, there, 1, keepdims=False)
            total = total + self.hop(piece, db=db).astype(f32)
        return total.astype(terms.dtype)

    def scatter_line(self, terms):
        total = lax.dynamic_index_in_dim(terms, self.a, 0, keepdims=False).astype(f32)
        for da in range(1, self.na):
            there = (self.a + da) % self.na
            piece = lax.dynamic_index_in_dim(terms, there, 0, keepdims=False)
            total = total + self.hop(piece, da=da).astype(f32)
        return total

    def everywhere(self, small):
        parts = [small] + [self.cross(small, shift) for shift in range(1, self.groups)]
        level = yield jnp.stack(parts)
        parts = [level] + [self.hop(level, db=db) for db in range(1, self.nb)]
        level = yield jnp.stack(parts, axis=1)
        parts = [level] + [self.hop(level, da=da) for da in range(1, self.na)]
        level = yield jnp.stack(parts, axis=1)
        yield jnp.stack([level, self.hop(level, dc=1)], axis=3)


def turned_lanes(values):
    return pltpu.roll(values, HEAD_DIM // 2, 1)


def head_probabilities(query, key, length):
    scores = dot(query, key, ((1,), (1,))) / math.sqrt(HEAD_DIM)
    query_place = lax.broadcasted_iota(jnp.int32, scores.shape, 0)
    key_place = lax.broadcasted_iota(jnp.int32, scores.shape, 1)
    allowed = (key_place <= query_place) & (key_place < length)
    scores = jnp.where(allowed, scores, -1e30)
    exponent = jnp.exp(scores - jnp.max(scores, axis=1, keepdims=True))
    return exponent / jnp.sum(exponent, axis=1, keepdims=True)


def home_rows(here, sequence, sequences, rows):
    return pl.ds(pl.multiple_of(lax.rem(here[1] - sequence + sequences, sequences) * rows, rows), rows)


def attention_kernel(sequences, heads, here, raw, bias, cosine, signed_sine, low, context):
    rows = cosine.shape[0]
    width = heads * HEAD_DIM
    for sequence in range(sequences):
        at = slice(sequence * rows, (sequence + 1) * rows)
        home = home_rows(here, sequence, sequences, rows)
        length = here[2 + pl.program_id(0) * sequences + sequence]
        for head in range(heads):
            parts = []
            for part in range(3):
                low_lane = part * width + head * HEAD_DIM
                lanes = slice(low_lane, low_lane + HEAD_DIM)
                values = raw[at, lanes] + bias[:, lanes]
                if part < 2:
                    values = values * cosine[...] + turned_lanes(values) * signed_sine[...]
                values = values.astype(bf16)
                low[at, lanes] = values
                parts.append(values)
            probabilities = head_probabilities(parts[0], parts[1], length).astype(bf16)
            lanes = slice(head * HEAD_DIM, (head + 1) * HEAD_DIM)
            context[home, lanes] = dot(probabilities, parts[2], ((1,), (0,))).astype(bf16)


def attention_grad_kernel(
    sequences, heads, here, low, incoming, cosine, sine, sign, outgoing, bias_grad
):
    rows = cosine.shape[0]
    width = heads * HEAD_DIM
    root_size = math.sqrt(HEAD_DIM)

    @pl.when(pl.program_id(0) == 0)
    def _():
        bias_grad[...] = jnp.zeros_like(bias_grad)

    for sequence in range(sequences):
        at = slice(sequence * rows, (sequence + 1) * rows)
        home = home_rows(here, sequence, sequences, rows)
        length = here[2 + pl.program_id(0) * sequences + sequence]
        for head in range(heads):
            lanes = [
                slice(part * width + head * HEAD_DIM, part * width + (head + 1) * HEAD_DIM)
                for part in range(3)
            ]
            query, key, value = (low[at, part] for part in lanes)
            grad = incoming[home, lanes[0]]
            probabilities = head_probabilities(query, key, length)
            probs_grad = dot(grad, value, ((1,), (1,)))
            inner = jnp.sum(probabilities * probs_grad, axis=1, keepdims=True)
            score_grad = (probabilities * (probs_grad - inner)).astype(bf16)
            grads = [
                dot(score_grad, key, ((1,), (0,))) / root_size,
                dot(score_grad, query, ((0,), (0,))) / root_size,
                dot(probabilities.astype(bf16), grad, ((0,), (0,))),
            ]
            for part in range(3):
                values = grads[part]
                if part < 2:
                    values = values * cosine[...] - turned_lanes(values * sine[...]) * sign[...]
                values = values.astype(bf16)
                outgoing[at, lanes[part]] = values
                bias_grad[:, lanes[part]] += jnp.sum(values.astype(f32), axis=0, keepdims=True)


def rope_inputs(row_count):
    cosine, sine = (table[:, 0] for table in rope_tables(row_count, HEAD_DIM))
    sign = jnp.where(jnp.arange(HEAD_DIM) < HEAD_DIM // 2, -1.0, 1.0).astype(f32)[None]
    return cosine, sine, sign


def attention(here, raw, bias, rows, sequences, heads):
    tokens, width = raw.shape[0], heads * HEAD_DIM
    cosine, sine, sign = rope_inputs(rows)
    block = sequences * rows
    lines = tokens // block
    whole = lambda *shape: pl.BlockSpec(shape, lambda i, here: (0, 0))
    return pl.pallas_call(
        functools.partial(attention_kernel, sequences, heads),
        out_shape=[
            jax.ShapeDtypeStruct((tokens, 3 * width), bf16),
            jax.ShapeDtypeStruct((tokens, width), bf16),
        ],
        grid_spec=pltpu.PrefetchScalarGridSpec(
            num_scalar_prefetch=1,
            grid=(lines,),
            in_specs=[
                pl.BlockSpec((block, 3 * width), lambda i, here: (i, 0)),
                whole(1, 3 * width),
                whole(rows, HEAD_DIM),
                whole(rows, HEAD_DIM),
            ],
            out_specs=[
                pl.BlockSpec((block, 3 * width), lambda i, here: (i, 0)),
                pl.BlockSpec((block, width), lambda i, here: (lax.rem(here[0] - i + lines, lines), 0)),
            ],
        ),
        cost_estimate=pl.CostEstimate(
            flops=4 * tokens * rows * width, bytes_accessed=tokens * width * 20, transcendentals=0
        ),
    )(here, raw, bias, cosine, sine * sign)


def attention_grad(here, low, incoming, rows, sequences, heads):
    tokens, width = low.shape[0], heads * HEAD_DIM
    block = sequences * rows
    lines = tokens // block
    whole = lambda *shape: pl.BlockSpec(shape, lambda i, here: (0, 0))
    return pl.pallas_call(
        functools.partial(attention_grad_kernel, sequences, heads),
        out_shape=[
            jax.ShapeDtypeStruct((tokens, 3 * width), bf16),
            jax.ShapeDtypeStruct((1, 3 * width), f32),
        ],
        grid_spec=pltpu.PrefetchScalarGridSpec(
            num_scalar_prefetch=1,
            grid=(lines,),
            in_specs=[
                pl.BlockSpec((block, 3 * width), lambda i, here: (i, 0)),
                pl.BlockSpec((block, width), lambda i, here: (lax.rem(here[0] - i + lines, lines), 0)),
                whole(rows, HEAD_DIM),
                whole(rows, HEAD_DIM),
                whole(1, HEAD_DIM),
            ],
            out_specs=[
                pl.BlockSpec((block, 3 * width), lambda i, here: (i, 0)),
                whole(1, 3 * width),
            ],
        ),
        cost_estimate=pl.CostEstimate(
            flops=10 * tokens * rows * width, bytes_accessed=tokens * width * 14, transcendentals=0
        ),
    )(here, low, incoming, *rope_inputs(rows))


def pack_kernel(count, moves, blanks, order, *refs):
    sources, out, sem = refs[:count], refs[-2], refs[-1]
    copies = []
    for n, (source, low, size, to) in enumerate(moves):
        if to < 0:
            to = pl.multiple_of(order[-1 - to] * size, size)
        copies.append(
            pltpu.make_async_copy(
                sources[source].at[pl.ds(low, size), :], out.at[pl.ds(to, size), :], sem.at[n]
            )
        )
    for copy in copies:
        copy.start()
    for at, size in blanks:
        out[at : at + size, :] = jnp.zeros((size, out.shape[1]), out.dtype)
    for copy in copies:
        copy.wait()


def pack(pieces, step=1, size=None, order=None):
    moves, blanks, at = [], [], 0
    for n, piece in enumerate(pieces):
        rows = piece.shape[0]
        if order is None:
            moves.append((n, 0, rows, at))
        else:
            moves += [(n, low, size, -1 - len(moves) - low // size) for low in range(0, rows, size)]
        at += rows
        if at % step:
            blanks.append((at, -at % step))
            at += -at % step
    if order is None:
        order = jnp.zeros((1,), jnp.int32)
    return pl.pallas_call(
        functools.partial(pack_kernel, len(pieces), moves, blanks),
        out_shape=jax.ShapeDtypeStruct((at, pieces[0].shape[1]), pieces[0].dtype),
        in_specs=[pl.BlockSpec(memory_space=pltpu.SMEM)]
        + [pl.BlockSpec(memory_space=pl.ANY)] * len(pieces),
        out_specs=pl.BlockSpec(memory_space=pltpu.VMEM),
        scratch_shapes=[pltpu.SemaphoreType.DMA((len(moves),))],
        compiler_params=pltpu.CompilerParams(vmem_limit_bytes=VMEM),
        cost_estimate=pl.CostEstimate(
            flops=0, bytes_accessed=4 * at * pieces[0].shape[1], transcendentals=0
        ),
    )(order, *pieces)


def experts_kernel(blocks, start, expert, meta, vector, *refs):
    row_blocks, grad_blocks = refs[:blocks], refs[blocks : 2 * blocks]
    into_hbm, down_hbm = refs[2 * blocks : 2 * blocks + 2]
    refs = refs[2 * blocks + 2 :]
    unit_outs, refs = refs[:3], refs[3:]
    rest = blocks // CORES
    term_outs, vector_grad, refs = refs[: rest + 1], refs[rest + 1], refs[rest + 2 :]
    rows, grads, into, down, middle_all, gate_all, up_all = refs[:7]
    in_sem, weight_sem, out_sem, term_sem = refs[7:11]
    tokens, features = rows.shape
    units = down.shape[0]
    count = tokens // blocks
    tiles = [(low, min(low + TILE, units)) for low in range(0, units, TILE)]

    loads = [
        [
            pltpu.make_async_copy(
                block, held.at[pl.ds(n * count, count), :], in_sem.at[which, n]
            )
            for n, block in enumerate(arrived)
        ]
        for which, (arrived, held) in enumerate(((row_blocks, rows), (grad_blocks, grads)))
    ]
    weights = [
        [
            pltpu.make_async_copy(
                source.at[pl.ds(first + low, high - low), :],
                held.at[pl.ds(first + low, high - low), :],
                weight_sem.at[tile, which],
            )
            for which, (source, held, first) in enumerate(
                ((into_hbm, into, 0), (into_hbm, into, units), (down_hbm, down, 0))
            )
        ]
        for tile, (low, high) in enumerate(tiles)
    ]
    for copy in loads[0] + weights[0] + loads[1]:
        copy.start()
    for tile in weights[1:]:
        for copy in tile:
            copy.start()

    here = expert[0].astype(f32)
    columns = []
    for core in range(meta.shape[1]):
        for line in range(meta.shape[0]):
            told = meta[line, core]
            scale = jnp.zeros((1, count), f32)
            for k in range(TOP):
                hit = told[k : k + 1] == here
                scale = scale + jnp.where(hit, told[TOP + k : TOP + k + 1], 0.0)
            columns.append(jnp.transpose(jnp.broadcast_to(scale, (count, count)))[:, :1])
    routed_scale = jnp.concatenate(columns, axis=0)

    for copy in loads[0]:
        copy.wait()
    logit = jnp.sum(rows[...].astype(f32) * vector[...], axis=1, keepdims=True)
    shared_scale = jax.nn.sigmoid(logit)
    inner = jnp.zeros((tokens, 1), f32)
    stores = []
    for tile, (low, high) in enumerate(tiles):
        for copy in weights[tile]:
            copy.wait()
        gate = dot(rows[...], into[low:high, :], ((1,), (1,)))
        up = dot(rows[...], into[units + low : units + high, :], ((1,), (1,)))
        if tile == 0:
            for copy in loads[1]:
                copy.wait()
        back = dot(grads[...], down[low:high, :], ((1,), (1,)))
        gate_sigmoid = jax.nn.sigmoid(gate)
        silu = gate * gate_sigmoid
        middle = silu * up
        unit = lax.broadcasted_iota(jnp.int32, (1, high - low), 1) + low
        if high <= start:
            scale = routed_scale
        elif low >= start:
            scale = shared_scale
        else:
            scale = jnp.where(unit < start, routed_scale, shared_scale)
        if high > start:
            product = middle * back
            if low < start:
                product = jnp.where(unit < start, 0.0, product)
            inner = inner + jnp.sum(product, axis=1, keepdims=True)
        back = back * scale
        middle_all[:, low:high] = (middle * scale).astype(bf16)
        gate_all[:, low:high] = (back * up * (gate_sigmoid + silu * (1.0 - gate_sigmoid))).astype(
            bf16
        )
        up_all[:, low:high] = (back * silu).astype(bf16)
        for which, (held, out) in enumerate(zip((middle_all, gate_all, up_all), unit_outs)):
            lanes = pl.ds(low, high - low)
            copy = pltpu.make_async_copy(
                held.at[:, lanes], out.at[:, lanes], out_sem.at[tile, which]
            )
            copy.start()
            stores.append(copy)

    @pl.when(expert[1] == 1)
    def _():
        terms = refs[11]
        logit_grad = inner * shared_scale * (1.0 - shared_scale)
        for low in range(0, features, TILE):
            lanes = slice(low, low + TILE)
            value = dot(gate_all[...], into[:units, lanes], ((1,), (0,)))
            value = value + dot(up_all[...], into[units:, lanes], ((1,), (0,)))
            value = (value + logit_grad * vector[:, lanes]).astype(bf16)
            result = dot(middle_all[...], down[:, lanes], ((1,), (0,))).astype(bf16)
            for n in range(blocks):
                at = slice(n * count, (n + 1) * count)
                terms[2 * n * count : (2 * n + 1) * count, lanes] = value[at]
                terms[(2 * n + 1) * count : (2 * n + 2) * count, lanes] = result[at]
        at, copies = 0, []
        for n, out in enumerate(term_outs):
            copies.append(
                pltpu.make_async_copy(terms.at[pl.ds(at, out.shape[0]), :], out, term_sem.at[n])
            )
            at += out.shape[0]
        for copy in copies:
            copy.start()
        vector_grad[...] = jnp.sum(rows[...].astype(f32) * logit_grad, axis=0, keepdims=True)
        for copy in copies:
            copy.wait()

    for copy in stores:
        copy.wait()


def experts(expert, meta, vector, rows, grads, into, down, routed):
    blocks = len(rows)
    count, features = rows[0].shape
    tokens, units, rest = blocks * count, down.shape[0], blocks // CORES
    tiles = -(-units // TILE)
    anywhere = pl.BlockSpec(memory_space=pl.ANY)
    inside = pl.BlockSpec(memory_space=pltpu.VMEM)
    out_shape = [jax.ShapeDtypeStruct((tokens, units), bf16)] * 3
    out_specs = [anywhere] * 3
    scratch = [
        pltpu.VMEM((tokens, features), bf16),
        pltpu.VMEM((tokens, features), bf16),
        pltpu.VMEM(into.shape, bf16),
        pltpu.VMEM(down.shape, bf16),
        pltpu.VMEM((tokens, units), bf16),
        pltpu.VMEM((tokens, units), bf16),
        pltpu.VMEM((tokens, units), bf16),
        pltpu.SemaphoreType.DMA((2, blocks)),
        pltpu.SemaphoreType.DMA((tiles, 3)),
        pltpu.SemaphoreType.DMA((tiles, 3)),
        pltpu.SemaphoreType.DMA((rest + 1,)),
    ]
    out_shape += [jax.ShapeDtypeStruct((2 * count, features), bf16)] * rest
    out_shape += [jax.ShapeDtypeStruct((2 * (tokens - rest * count), features), bf16)]
    out_shape += [jax.ShapeDtypeStruct((1, features), f32)]
    out_specs += [anywhere] * (rest + 1) + [inside]
    scratch += [pltpu.VMEM((2 * tokens, features), bf16)]
    return pl.pallas_call(
        functools.partial(experts_kernel, blocks, routed + -routed % LANES),
        out_shape=out_shape,
        in_specs=[pl.BlockSpec(memory_space=pltpu.SMEM), inside, inside]
        + [anywhere] * (2 * blocks + 2),
        out_specs=out_specs,
        scratch_shapes=scratch,
        compiler_params=pltpu.CompilerParams(vmem_limit_bytes=VMEM),
        cost_estimate=pl.CostEstimate(
            flops=2 * tokens * features * units * 4,
            bytes_accessed=2 * (into.size + down.size + 4 * tokens * features),
            transcendentals=0,
        ),
    )(expert, meta, vector, *rows, *grads, into, down)


def weight_grad_kernel(unit_counts, row_counts, first, second, start, adds, *refs):
    some, pieces = len(unit_counts), len(unit_counts) + len(row_counts)
    units, rows = refs[:some], refs[some:pieces]
    before = refs[pieces : pieces + 2] if adds else (None, None)
    first_out, second_out, held, tiles, held_sem, tile_sem = refs[pieces + 2 * adds :]
    width = tiles.shape[-1]
    step = pl.program_id(0)
    slot = lax.rem(step, 2)
    unit_places, row_places = (
        [pl.ds(sum(counts[:n]), count) for n, count in enumerate(counts)]
        for counts in (unit_counts, row_counts)
    )

    def held_copies():
        return [
            pltpu.make_async_copy(units[n], held.at[at, :], held_sem.at[n])
            for n, at in enumerate(unit_places)
        ]

    def tile_copies(index, into):
        columns = pl.ds(pl.multiple_of(index * width, width), width)
        return [
            pltpu.make_async_copy(
                rows[n].at[:, columns], tiles.at[into, at, :], tile_sem.at[into, n]
            )
            for n, at in enumerate(row_places)
        ]

    @pl.when(step == 0)
    def _():
        for copy in held_copies() + tile_copies(0, 0):
            copy.start()
        for copy in held_copies():
            copy.wait()

    for copy in tile_copies(step, slot):
        copy.wait()

    @pl.when(step + 1 < pl.num_programs(0))
    def _():
        for copy in tile_copies(step + 1, 1 - slot):
            copy.start()

    for low, size, out, earlier in (
        (0, first, first_out, before[0]),
        (start, second, second_out, before[1]),
    ):
        value = dot(held[:, low : low + size], tiles[slot], ((0,), (0,)))
        out[...] = earlier[...] + value if adds else value


def weight_grad(units, rows, first, second, before=()):
    unit_counts = [piece.shape[0] for piece in units]
    row_counts = [piece.shape[0] for piece in rows]
    pieces, tokens = len(units) + len(rows), sum(row_counts)
    features, all_units = rows[0].shape[1], units[0].shape[1]
    start = first + -first % LANES
    adds = int(bool(before))
    anywhere = pl.BlockSpec(memory_space=pl.ANY)
    blocks = [pl.BlockSpec((size, TILE), lambda i: (0, i)) for size in (first, second)]
    return pl.pallas_call(
        functools.partial(weight_grad_kernel, unit_counts, row_counts, first, second, start, adds),
        grid=(features // TILE,),
        out_shape=[jax.ShapeDtypeStruct((size, features), f32) for size in (first, second)],
        in_specs=[anywhere] * pieces + blocks * adds,
        out_specs=blocks,
        scratch_shapes=[
            pltpu.VMEM((tokens, all_units), bf16),
            pltpu.VMEM((2, tokens, TILE), bf16),
            pltpu.SemaphoreType.DMA((len(units),)),
            pltpu.SemaphoreType.DMA((2, len(rows))),
        ],
        input_output_aliases={pieces: 0, pieces + 1: 1} if adds else {},
        compiler_params=pltpu.CompilerParams(vmem_limit_bytes=VMEM),
        cost_estimate=pl.CostEstimate(
            flops=2 * tokens * features * (first + second),
            bytes_accessed=tokens * (features + all_units) * 2
            + features * (first + second) * 4 * (1 + adds),
            transcendentals=0,
        ),
    )(*units, *rows, *before)


def local(
    layer_input,
    lengths,
    routes,
    route_weight,
    cotangent,
    norm_gain,
    w_qkv,
    b_qkv,
    w_out,
    post_gain,
    w_gate,
    w_up,
    w_down,
    shared_gate,
    shared_up,
    shared_down,
    shared_vector,
):
    grid = Grid()
    row_count, feature_count = layer_input.shape
    groups, owners, chips, na, nb = grid.groups, grid.owners, grid.chips, grid.na, grid.nb
    devices = groups * owners
    heads_here = HEADS // chips
    width = heads_here * HEAD_DIM
    own_rows = w_qkv.shape[0]
    sizes = (w_gate.shape[2], shared_gate.shape[1])
    positions = jnp.arange(row_count, dtype=jnp.int32)
    slots = range(na)
    two = groups == 2

    class Rounds:
        def __init__(self, block):
            self.far, self.blocks = [block], []

        def row(self):
            if len(self.blocks) < na:
                self.blocks.append(grid.row(self.far[len(self.blocks)]))

        def line(self):
            if len(self.far) < na:
                self.far.append(grid.hop(self.far[-1], da=1))

        def all(self):
            return [block for blocks in self.blocks for block in blocks]

    def tie_rounds(rounds, *values):
        state = [(r.far, r.blocks) for r in rounds]
        state, *values = tie(state, *values)
        for r, (far, blocks) in zip(rounds, state):
            r.far, r.blocks = far, blocks
        return values

    def place_of(da, db, dc, dg):
        group = (grid.group - dg) % groups
        chip = (grid.a - da) % na * nb + (grid.b - db) % nb
        return (group * chips + chip) * CORES + (grid.core + dc) % CORES

    def other_core(blocks):
        return [grid.hop(block, dc=1) for block in blocks]

    small = jnp.concatenate([norm_gain, post_gain, shared_vector, b_qkv]).astype(f32)
    small_count = small.shape[0]
    small = jnp.pad(small, (0, -small_count % row_count))
    meta = jnp.concatenate(
        [
            routes.T.astype(f32),
            route_weight.T.astype(f32),
            jnp.broadcast_to(lengths.astype(f32)[:, None], (1, row_count)),
            small.reshape(-1, row_count),
        ],
        axis=0,
    )
    telling = grid.everywhere(meta)

    x_rounds = Rounds(layer_input)
    x_rounds.line()
    x_rounds.row()
    sliced = jnp.transpose(w_qkv.reshape(own_rows, 3, chips, width), (2, 0, 1, 3))
    by_chip = grid.swap(sliced.reshape(chips, own_rows, 3 * width))
    level = next(telling)
    into_in = [w_gate, shared_gate, w_up, shared_up]
    down_in = [w_down, shared_down]
    level, w_out, into_in = tie_rounds([x_rounds], level, w_out, into_in)

    out_pairs, out_far = [jnp.concatenate(grid.row(w_out), axis=0)], []

    def out_line():
        if len(out_pairs) < na:
            out_pairs.append(grid.hop(out_pairs[-1], da=1))

    def out_cross():
        if len(out_far) < len(out_pairs):
            pair = out_pairs[len(out_far)]
            out_far.append([grid.cross(pair, shift) for shift in range(1, groups)])

    def tie_out(rounds, *values):
        nonlocal out_pairs, out_far
        out_pairs, out_far, *values = tie_rounds(rounds, out_pairs, out_far, *values)
        return values

    x_rounds.line()
    x_rounds.row()
    level = telling.send(level)
    into_rows = pack(
        [into_in[0][0].T, into_in[1].T, into_in[2][0].T, into_in[3].T], LANES
    )
    by_chip, level, into_rows, down_in = tie_out(
        [x_rounds], by_chip, level, into_rows, down_in
    )
    by_chip = by_chip.reshape(chips * own_rows, 3 * width)
    x_rounds.line()
    x_rounds.row()
    level = telling.send(level)
    by_group = [by_chip] + [grid.cross(by_chip, shift) for shift in range(1, groups)]
    down_rows = pack([down_in[0][0], down_in[1]], LANES)
    out_line()
    by_group, level, down_rows = tie_out([x_rounds], by_group, level, down_rows)
    weight_pieces, order = [], []
    for shift, piece in enumerate(by_group):
        for core in range(CORES):
            weight_pieces.append(grid.hop(piece, dc=1) if core else piece)
            for chip in range(chips):
                order.append(
                    ((grid.group - shift) % groups * chips + chip) * CORES
                    + (grid.core + core) % CORES
                )
    meta_all = telling.send(level)
    flat_meta = meta_all.reshape(devices, *meta.shape)
    index = jnp.arange(devices, dtype=jnp.int32)
    ig, ia, ib, ic = (
        index // owners,
        index // (nb * CORES) % na,
        index // CORES % nb,
        index % CORES,
    )
    from_here = (
        ((grid.group - ig) % groups * na + (grid.a - ia) % na) * nb + (grid.b - ib) % nb
    ) * CORES + (grid.core - ic) % CORES
    small_all = jnp.take(flat_meta[:, 2 * TOP + 1 :], from_here, axis=0).reshape(devices, -1)
    own_features = norm_gain.shape[0]
    gains_in = small_all[:, :own_features].reshape(-1)
    gains_post = small_all[:, own_features : 2 * own_features].reshape(-1)
    gate_vector = small_all[:, 2 * own_features : 3 * own_features].reshape(-1)
    qkv_bias = small_all[:, 3 * own_features : small_count].reshape(3, chips, width)
    bias_here = lax.dynamic_index_in_dim(qkv_bias, grid.chip, 1, keepdims=False).reshape(-1)
    plane_lengths = meta_all[0, :, :, 0, 2 * TOP, 0].reshape(chips).astype(jnp.int32)
    here = jnp.concatenate([jnp.stack([grid.a, grid.b]).astype(jnp.int32), plane_lengths])
    while len(x_rounds.blocks) < na:
        x_rounds.row()
    out_line()
    out_cross()
    heads_weight = pack(weight_pieces, size=own_rows, order=jnp.stack(order).astype(jnp.int32))
    normed_first = pack(
        [(unit_norm(block.astype(f32))[0] * gains_in).astype(bf16) for block in x_rounds.all()]
    )
    normed_first, heads_weight, bias_here, gains_in, cotangent, here = tie_out(
        [], normed_first, heads_weight, bias_here, gains_in, cotangent, here
    )

    valid_rows = positions < lengths[0]
    grad_rows = jnp.where(valid_rows[:, None], cotangent, jnp.zeros_like(cotangent))
    inputs = layer_input.astype(f32)
    grad_rounds = Rounds(grad_rows)
    while len(out_pairs) < na:
        out_line()
    out_cross()
    grad_rounds.line()
    grad_rounds.row()
    projected = dot(normed_first, heads_weight, ((1,), (0,)))
    low, sent = attention(here, projected, bias_here[None], row_count, nb, heads_here)
    low, sent = tie_out([grad_rounds], low, sent)

    grad_rounds.line()
    grad_rounds.row()
    while len(out_far) < na:
        out_cross()
    pieces, order = [], []
    for dc in range(CORES):
        for da in slots:
            for dg in range(groups):
                pair = out_far[da][dg - 1] if dg else out_pairs[da]
                pieces.append(grid.hop(pair, dc=1) if dc else pair)
                order += [place_of(da, db, dc, dg) for db in range(nb)]
    out_weight = pack(pieces, size=own_rows, order=jnp.stack(order).astype(jnp.int32))
    arrived = grid.swap(sent.reshape(chips, row_count, width))
    arrived, out_weight = tie_rounds([grad_rounds], arrived, out_weight)

    far_grads, far_rows = [], []
    crossings = [("grads", s) for s in slots] + [("rows", s) for s in slots]

    def cross_step():
        if crossings and two:
            what, s = crossings[0]
            source, goes = (
                (grad_rounds, far_grads) if what == "grads" else (second_rounds, far_rows)
            )
            if s < len(source.blocks):
                crossings.pop(0)
                goes.append([grid.cross(block, 1) for block in source.blocks[s]])

    grad_rounds.line()
    grad_rounds.row()
    context = jnp.transpose(arrived, (1, 0, 2)).reshape(row_count, feature_count)
    residual = inputs + dot(context, out_weight, ((1,), (0,)))
    unit_second, factor_second = unit_norm(residual)
    normed_second = (unit_second * gains_post).astype(bf16)

    expert = (lax.axis_index("ep") // HALVES).astype(jnp.int32)
    expert, far_expert = (jnp.stack([expert, jnp.int32(n)]) for n in (1, 0))
    vector_row = gate_vector[None]
    told = meta_all[..., : 2 * TOP, :]
    second_rounds = Rounds(normed_second)
    own = {"rows": [], "grads": [], "middle": [], "gate": [], "up": [], "vector": []}

    def work(s):
        own["rows"].append(second_rounds.blocks[s] + other_core(second_rounds.blocks[s]))
        own["grads"].append(grad_rounds.blocks[s] + other_core(grad_rounds.blocks[s]))
        middle, gate, up, *terms, vector = experts(
            expert, told[0, s], vector_row, own["rows"][s], own["grads"][s],
            into_rows, down_rows, sizes[0],
        )
        for name, value in (("middle", middle), ("gate", gate), ("up", up), ("vector", vector)):
            own[name].append(value)
        return terms

    def add_cores(terms):
        arriving = grid.hop(terms[-1], dc=1)
        return [
            (
                terms[t].astype(f32)
                + arriving[2 * t * row_count : 2 * (t + 1) * row_count].astype(f32)
            ).astype(bf16)
            for t in range(nb)
        ]

    def step_tie(*values):
        nonlocal own, far_grads, far_rows, into_rows, down_rows
        own, far_grads, far_rows, into_rows, down_rows, *values = tie_rounds(
            [grad_rounds, second_rounds], own, far_grads, far_rows, into_rows, down_rows, *values
        )
        return values

    def line_sum(rowed, sums, s):
        total = rowed[s] if sums is None else rowed[s] + sums.astype(f32)
        return grid.hop(total.astype(bf16), da=1) if s else total

    def far_work(shift, s):
        rows = far_rows[s] + other_core(far_rows[s])
        grads = far_grads[s] + other_core(far_grads[s])
        units = experts(
            far_expert, told[shift, s], vector_row, rows, grads,
            into_rows, down_rows, sizes[0],
        )
        return rows, grads, units[:3]

    def flat(lists):
        return [block for blocks in lists for block in blocks]

    rowed, terms, far = {}, {}, []
    sums = None
    second_rounds.line()
    second_rounds.row()
    cross_step()
    for s in slots:
        grad_rounds.line()
        grad_rounds.row()
        second_rounds.line()
        second_rounds.row()
        if s:
            cross_step()
            cross_step()
        if s >= 2:
            rowed[s - 1] = grid.row_sum(add_cores(terms[s - 1]))
        if s >= 3:
            sums = line_sum(rowed, sums, s - 2)
        terms[s] = work(s)
        rowed, terms, sums = step_tie(rowed, terms, sums)
    cross_step()
    rowed[na - 1] = grid.row_sum(add_cores(terms[na - 1]))
    if na > 2:
        sums = line_sum(rowed, sums, na - 2)
    own_gate = weight_grad(own["gate"], flat(own["rows"]), *sizes)
    rowed, terms, sums, own_gate = step_tie(rowed, terms, sums, own_gate)
    while crossings and two:
        cross_step()
    sums = line_sum(rowed, sums, na - 1)
    rowed[0] = grid.row_sum(add_cores(terms[0]))
    own_up = weight_grad(own["up"], flat(own["rows"]), *sizes)
    if two:
        far.append(far_work(1, 0))
    rowed, sums, own_up, far = step_tie(rowed, sums, own_up, far)

    both_sums = line_sum(rowed, sums, 0)
    second_grad = both_sums[:row_count]
    outs = residual + both_sums[row_count:]
    output = jnp.where(valid_rows[:, None], outs, 0.0).astype(bf16)
    grad_float = grad_rows.astype(f32)
    post_gain_grad = jnp.sum(second_grad * unit_second, axis=0)
    residual_grad = grad_float + norm_backward(
        second_grad, unit_second, factor_second, gains_post
    )
    attended_grad = residual_grad.astype(bf16)
    context_grad = dot(attended_grad, out_weight, ((1,), (1,))).astype(bf16)
    sent = jnp.transpose(context_grad.reshape(row_count, chips, width), (1, 0, 2))
    arrived = grid.swap(sent)
    own_down = weight_grad(own["middle"], flat(own["grads"]), *sizes)
    if two:
        far.append(far_work(1, 1))
    arrived, own_down, attended_grad, far = step_tie(arrived, own_down, attended_grad, far)

    def own_features_of(values, core, group):
        parts = values.reshape(row_count, groups, chips, CORES, own_rows)
        parts = lax.dynamic_index_in_dim(parts, core, 3, keepdims=False)
        parts = lax.dynamic_index_in_dim(parts, group, 1, keepdims=False)
        return parts.reshape(row_count, chips * own_rows)

    projected_grad, bias_here_grad = attention_grad(
        here, low, arrived.reshape(-1, width), row_count, nb, heads_here
    )
    first_terms = dot(projected_grad, heads_weight, ((1,), (1,))).astype(bf16)
    out_parts = []
    for shift in range(groups):
        group = (grid.group + shift) % groups
        mine, other = (
            dot(own_features_of(context, core, group), attended_grad, ((0,), (0,))).astype(bf16)
            for core in (grid.core, 1 - grid.core)
        )
        total = mine.astype(f32) + grid.hop(other, dc=1).astype(f32)
        out_parts.append(total.astype(bf16))
    first_terms, projected_grad, out_parts, far = step_tie(
        first_terms, projected_grad, out_parts, far
    )

    slot_first = first_terms.reshape(na, nb, row_count, feature_count)
    totals = [[own_gate, own_up, own_down]]

    def end_tie(*values):
        nonlocal far, far_rows, far_grads, into_rows, down_rows, own, totals
        far, far_rows, far_grads, into_rows, down_rows, own, totals, *values = tie(
            far, far_rows, far_grads, into_rows, down_rows, own, totals, *values
        )
        return values

    def far_grad(units, place):
        before = totals[0][units] if two else ()
        return weight_grad(
            [work[2][(1, 2, 0)[units]] for work in far], flat(work[place] for work in far),
            *sizes, before,
        )

    first_rowed = {s: grid.row_sum(slot_first[s]) for s in range(1, na - 1)}
    qkv_grad = dot(normed_first, projected_grad, ((0,), (0,))).astype(bf16)
    half = chips * own_rows // 2
    crossed = [[grid.cross(part[:half], n + 1)] for n, part in enumerate(out_parts[1:])]
    if two:
        far.append(far_work(1, 2))
    first_rowed, slot_first, qkv_grad, crossed, out_parts = end_tie(
        first_rowed, slot_first, qkv_grad, crossed, out_parts
    )
    for s in sorted({na - 1, 0}):
        first_rowed[s] = grid.row_sum(slot_first[s])
    first_sums = line_sum(first_rowed, None, 1)
    for n, part in enumerate(out_parts[1:]):
        crossed[n].append(grid.cross(part[half:], n + 1))
    qkv_grad = grid.scatter_core(qkv_grad.reshape(groups, chips, CORES, own_rows, 3 * width), 2)
    if two:
        far.append(far_work(1, 3 % na))
    first_rowed, qkv_grad, crossed, out_parts, first_sums = end_tie(
        first_rowed, qkv_grad.astype(bf16), crossed, out_parts, first_sums
    )
    for s in range(2, na):
        first_sums = line_sum(first_rowed, first_sums, s)
    qkv_grad = grid.scatter_groups(qkv_grad).astype(bf16)
    out_total = out_parts[0].astype(f32)
    for halves in crossed:
        out_total = out_total + jnp.concatenate(halves, axis=0).astype(f32)
    out_rowed = grid.scatter_row(
        out_total.astype(bf16).reshape(na, nb, own_rows, feature_count)
    )
    if two:
        gate_total = far_grad(0, 0)
        first_sums, qkv_grad, out_rowed, gate_total = end_tie(
            first_sums, qkv_grad, out_rowed, gate_total
        )
    first_grad = line_sum(first_rowed, first_sums, 0)
    unit_first, factor_first = unit_norm(inputs)
    input_part = norm_backward(first_grad, unit_first, factor_first, gains_in)
    layer_grad = (residual_grad + input_part).astype(bf16)
    out_weight_grad = grid.scatter_line(out_rowed)
    qkv_grad = grid.swap(qkv_grad).reshape(chips, own_rows, 3, width)
    if two:
        up_total = far_grad(1, 0)
        qkv_grad, out_weight_grad, up_total, layer_grad = end_tie(
            qkv_grad, out_weight_grad, up_total, layer_grad
        )
    qkv_weight_grad = jnp.transpose(qkv_grad, (1, 2, 0, 3)).reshape(own_rows, -1).astype(f32)
    if two:
        totals.append([gate_total, up_total, far_grad(2, 1)])
    else:
        second_blocks, grad_blocks = second_rounds.blocks, grad_rounds.blocks
        for shift in range(1, groups):
            totals, second_blocks, grad_blocks = tie(totals, second_blocks, grad_blocks)
            far_grads, far_rows = (
                [[grid.cross(block, shift) for block in blocks] for blocks in source]
                for source in (grad_blocks, second_blocks)
            )
            far = [far_work(shift, s) for s in slots]
            totals.append([far_grad(0, 0), far_grad(1, 0), far_grad(2, 1)])

        def ordered(*parts):
            total = 0.0
            for group in range(groups):
                far_by = (grid.group - group) % groups
                total = total + sum(
                    jnp.where(far_by == shift, part, 0.0) for shift, part in enumerate(parts)
                )
            return total

        totals.append(jax.tree.map(ordered, *totals))
    (
        (gate_grad, shared_gate_grad),
        (up_grad, shared_up_grad),
        (down_grad, shared_down_grad),
    ) = totals[-1]

    vector_grad = sum(own["vector"])[0]
    gain_grad = jnp.sum(first_terms.astype(f32) * normed_first.astype(f32), axis=0) / gains_in
    bias_grad = jnp.zeros((3, chips, width), f32)
    bias_grad = lax.dynamic_update_slice(
        bias_grad, bias_here_grad.reshape(3, 1, width), (0, grid.chip, 0)
    )
    vectors = jnp.concatenate(
        [
            gain_grad.reshape(devices, -1),
            post_gain_grad.reshape(devices, -1),
            vector_grad.reshape(devices, -1),
            bias_grad.reshape(devices, -1),
        ],
        axis=1,
    ).reshape(groups, na, nb, CORES, -1)
    vectors = grid.scatter_core(vectors, 3)
    vectors = grid.scatter_groups(vectors)
    vectors = grid.scatter_line(grid.scatter_row(vectors))
    return (
        output,
        layer_grad,
        vectors[:own_features],
        qkv_weight_grad,
        vectors[3 * own_features :],
        out_weight_grad,
        vectors[own_features : 2 * own_features],
        gate_grad.T[None],
        up_grad.T[None],
        down_grad[None],
        shared_gate_grad.T,
        shared_up_grad.T,
        shared_down_grad,
        vectors[2 * own_features : 3 * own_features],
    )


def solution(mesh):
    rows = P(("dp", "ep"), None)
    split = P(("dp", "ep"))
    parts = P("ep", None, None)
    return jax.shard_map(
        local,
        mesh=mesh,
        in_specs=(
            rows,
            split,
            rows,
            rows,
            rows,
            split,
            rows,
            split,
            rows,
            split,
            parts,
            parts,
            parts,
            P(None, "ep"),
            P(None, "ep"),
            P("ep", None),
            split,
        ),
        out_specs=(
            rows,
            rows,
            split,
            rows,
            split,
            rows,
            split,
            parts,
            parts,
            parts,
            P(None, "ep"),
            P(None, "ep"),
            P("ep", None),
            split,
        ),
        check_vma=False,
    )
```

```python
import functools
import math

import jax
import jax.numpy as jnp
from jax import lax
from jax.experimental import pallas as pl
from jax.experimental.pallas import tpu as pltpu
from jax.sharding import PartitionSpec as P

HEADS = 16
HEAD_DIM = 128
TOP = 4
HALVES = 2
CORES = 2
LINE = 4
LANES = 128
TILE = 512
VMEM = 56 << 20
EXTRA = 16


epsilon = 1e-06
rope_base = 1000000.0
bf16 = jnp.bfloat16
f32 = jnp.float32


def unit_norm(values):
    factor = lax.rsqrt(jnp.mean(values * values, axis=-1, keepdims=True) + epsilon)
    return (values * factor, factor)


def norm_backward(incoming, unit_rows, factor, gain_row):
    scaled = incoming * gain_row
    inner_mean = jnp.mean(scaled * unit_rows, axis=-1, keepdims=True)
    return factor * (scaled - unit_rows * inner_mean)


def rope_tables(row_count, head_size):
    inverse = rope_base ** (-jnp.arange(0, head_size, 2, dtype=f32) / head_size)
    angles = jnp.arange(row_count, dtype=f32)[:, None] * inverse[None, :]
    angles = jnp.concatenate([angles, angles], axis=-1)
    return (jnp.cos(angles)[:, None, :], jnp.sin(angles)[:, None, :])


def dot(left, right, dims):
    return lax.dot_general(left, right, (dims, ((), ())), preferred_element_type=f32)


def tie(*values):
    return lax.optimization_barrier(values)


class Grid:
    def __init__(self):
        self.groups = lax.axis_size("dp")
        self.owners = lax.axis_size("ep")
        self.chips = self.owners // CORES
        self.na = math.gcd(LINE, self.chips)
        self.nb = self.chips // self.na
        self.group = lax.axis_index("dp")
        me = lax.axis_index("ep")
        self.chip = me // CORES
        self.core = me % CORES
        self.a = self.chip // self.nb
        self.b = self.chip % self.nb

    def place(self, a, b, c):
        return ((a % self.na) * self.nb + b % self.nb) * CORES + c % CORES

    def hop(self, values, da=0, db=0, dc=0):
        pairs = [
            (self.place(a, b, c), self.place(a + da, b + db, c + dc))
            for a in range(self.na)
            for b in range(self.nb)
            for c in range(CORES)
        ]
        return lax.ppermute(values, "ep", pairs)

    def cross(self, values, shift):
        pairs = [(g, (g + shift) % self.groups) for g in range(self.groups)]
        return lax.ppermute(values, "dp", pairs)

    def row(self, block):
        return [block] + [self.hop(block, db=db) for db in range(1, self.nb)]

    def row_sum(self, terms):
        total = terms[0].astype(f32)
        for db in range(1, self.nb):
            total = total + self.hop(terms[db], db=-db).astype(f32)
        return total

    def core_sum(self, terms):
        return (terms[0].astype(f32) + self.hop(terms[1], dc=1).astype(f32)).astype(bf16)

    def same_core(self):
        return [[k * CORES + c for k in range(self.chips)] for c in range(CORES)]

    def swap(self, blocks):
        return lax.all_to_all(
            blocks,
            "ep",
            split_axis=0,
            concat_axis=0,
            tiled=True,
            axis_index_groups=self.same_core(),
        )

    def scatter_core(self, terms, axis):
        mine = lax.dynamic_index_in_dim(terms, self.core, axis, keepdims=False)
        other = lax.dynamic_index_in_dim(terms, 1 - self.core, axis, keepdims=False)
        return mine.astype(f32) + self.hop(other, dc=1).astype(f32)

    def scatter_groups(self, terms):
        total = lax.dynamic_index_in_dim(terms, self.group, 0, keepdims=False).astype(f32)
        for shift in range(1, self.groups):
            there = (self.group + shift) % self.groups
            piece = lax.dynamic_index_in_dim(terms, there, 0, keepdims=False)
            total = total + self.cross(piece, shift).astype(f32)
        return total

    def scatter_row(self, terms):
        total = lax.dynamic_index_in_dim(terms, self.b, 1, keepdims=False).astype(f32)
        for db in range(1, self.nb):
            there = (self.b + db) % self.nb
            piece = lax.dynamic_index_in_dim(terms, there, 1, keepdims=False)
            total = total + self.hop(piece, db=db).astype(f32)
        return total.astype(terms.dtype)

    def scatter_line(self, terms):
        total = lax.dynamic_index_in_dim(terms, self.a, 0, keepdims=False).astype(f32)
        for da in range(1, self.na):
            there = (self.a + da) % self.na
            piece = lax.dynamic_index_in_dim(terms, there, 0, keepdims=False)
            total = total + self.hop(piece, da=da).astype(f32)
        return total


def turned_lanes(values):
    return pltpu.roll(values, HEAD_DIM // 2, 1)


def head_probabilities(query, key, length):
    scores = dot(query, key, ((1,), (1,))) / math.sqrt(HEAD_DIM)
    query_place = lax.broadcasted_iota(jnp.int32, scores.shape, 0)
    key_place = lax.broadcasted_iota(jnp.int32, scores.shape, 1)
    allowed = (key_place <= query_place) & (key_place < length)
    scores = jnp.where(allowed, scores, -1e30)
    exponent = jnp.exp(scores - jnp.max(scores, axis=1, keepdims=True))
    return exponent / jnp.sum(exponent, axis=1, keepdims=True)


def home_rows(here, sequence, sequences, rows):
    return pl.ds(pl.multiple_of(lax.rem(here[1] - sequence + sequences, sequences) * rows, rows), rows)


def attention_kernel(sequences, heads, here, raw, bias, cosine, signed_sine, low, context):
    rows = cosine.shape[0]
    width = heads * HEAD_DIM
    for sequence in range(sequences):
        at = slice(sequence * rows, (sequence + 1) * rows)
        home = home_rows(here, sequence, sequences, rows)
        length = here[2 + pl.program_id(0) * sequences + sequence]
        for head in range(heads):
            parts = []
            for part in range(3):
                low_lane = part * width + head * HEAD_DIM
                lanes = slice(low_lane, low_lane + HEAD_DIM)
                values = raw[at, lanes] + bias[:, lanes]
                if part < 2:
                    values = values * cosine[...] + turned_lanes(values) * signed_sine[...]
                values = values.astype(bf16)
                low[at, lanes] = values
                parts.append(values)
            probabilities = head_probabilities(parts[0], parts[1], length).astype(bf16)
            lanes = slice(head * HEAD_DIM, (head + 1) * HEAD_DIM)
            context[home, lanes] = dot(probabilities, parts[2], ((1,), (0,))).astype(bf16)


def attention_grad_kernel(
    sequences, heads, here, low, incoming, cosine, sine, sign, outgoing, bias_grad
):
    rows = cosine.shape[0]
    width = heads * HEAD_DIM
    root_size = math.sqrt(HEAD_DIM)

    @pl.when(pl.program_id(0) == 0)
    def _():
        bias_grad[...] = jnp.zeros_like(bias_grad)

    for sequence in range(sequences):
        at = slice(sequence * rows, (sequence + 1) * rows)
        home = home_rows(here, sequence, sequences, rows)
        length = here[2 + pl.program_id(0) * sequences + sequence]
        for head in range(heads):
            lanes = [
                slice(part * width + head * HEAD_DIM, part * width + (head + 1) * HEAD_DIM)
                for part in range(3)
            ]
            query, key, value = (low[at, part] for part in lanes)
            grad = incoming[home, lanes[0]]
            probabilities = head_probabilities(query, key, length)
            probs_grad = dot(grad, value, ((1,), (1,)))
            inner = jnp.sum(probabilities * probs_grad, axis=1, keepdims=True)
            score_grad = (probabilities * (probs_grad - inner)).astype(bf16)
            grads = [
                dot(score_grad, key, ((1,), (0,))) / root_size,
                dot(score_grad, query, ((0,), (0,))) / root_size,
                dot(probabilities.astype(bf16), grad, ((0,), (0,))),
            ]
            for part in range(3):
                values = grads[part]
                if part < 2:
                    values = values * cosine[...] - turned_lanes(values * sine[...]) * sign[...]
                values = values.astype(bf16)
                outgoing[at, lanes[part]] = values
                bias_grad[:, lanes[part]] += jnp.sum(values.astype(f32), axis=0, keepdims=True)


def rope_inputs(row_count):
    cosine, sine = (table[:, 0] for table in rope_tables(row_count, HEAD_DIM))
    sign = jnp.where(jnp.arange(HEAD_DIM) < HEAD_DIM // 2, -1.0, 1.0).astype(f32)[None]
    return cosine, sine, sign


def attention(here, raw, bias, rows, sequences, heads):
    tokens, width = raw.shape[0], heads * HEAD_DIM
    cosine, sine, sign = rope_inputs(rows)
    block = sequences * rows
    lines = tokens // block
    whole = lambda *shape: pl.BlockSpec(shape, lambda i, here: (0, 0))
    return pl.pallas_call(
        functools.partial(attention_kernel, sequences, heads),
        out_shape=[
            jax.ShapeDtypeStruct((tokens, 3 * width), bf16),
            jax.ShapeDtypeStruct((tokens, width), bf16),
        ],
        grid_spec=pltpu.PrefetchScalarGridSpec(
            num_scalar_prefetch=1,
            grid=(lines,),
            in_specs=[
                pl.BlockSpec((block, 3 * width), lambda i, here: (i, 0)),
                whole(1, 3 * width),
                whole(rows, HEAD_DIM),
                whole(rows, HEAD_DIM),
            ],
            out_specs=[
                pl.BlockSpec((block, 3 * width), lambda i, here: (i, 0)),
                pl.BlockSpec((block, width), lambda i, here: (lax.rem(here[0] - i + lines, lines), 0)),
            ],
        ),
        cost_estimate=pl.CostEstimate(
            flops=4 * tokens * rows * width, bytes_accessed=tokens * width * 20, transcendentals=0
        ),
    )(here, raw, bias, cosine, sine * sign)


def attention_grad(here, low, incoming, rows, sequences, heads):
    tokens, width = low.shape[0], heads * HEAD_DIM
    block = sequences * rows
    lines = tokens // block
    whole = lambda *shape: pl.BlockSpec(shape, lambda i, here: (0, 0))
    return pl.pallas_call(
        functools.partial(attention_grad_kernel, sequences, heads),
        out_shape=[
            jax.ShapeDtypeStruct((tokens, 3 * width), bf16),
            jax.ShapeDtypeStruct((1, 3 * width), f32),
        ],
        grid_spec=pltpu.PrefetchScalarGridSpec(
            num_scalar_prefetch=1,
            grid=(lines,),
            in_specs=[
                pl.BlockSpec((block, 3 * width), lambda i, here: (i, 0)),
                pl.BlockSpec((block, width), lambda i, here: (lax.rem(here[0] - i + lines, lines), 0)),
                whole(rows, HEAD_DIM),
                whole(rows, HEAD_DIM),
                whole(1, HEAD_DIM),
            ],
            out_specs=[
                pl.BlockSpec((block, 3 * width), lambda i, here: (i, 0)),
                whole(1, 3 * width),
            ],
        ),
        cost_estimate=pl.CostEstimate(
            flops=10 * tokens * rows * width, bytes_accessed=tokens * width * 14, transcendentals=0
        ),
    )(here, low, incoming, *rope_inputs(rows))


def pack_kernel(count, moves, blanks, order, *refs):
    sources, out, sem = refs[:count], refs[-2], refs[-1]
    copies = []
    for n, (source, low, size, to) in enumerate(moves):
        if to < 0:
            to = pl.multiple_of(order[-1 - to] * size, size)
        copies.append(
            pltpu.make_async_copy(
                sources[source].at[pl.ds(low, size), :], out.at[pl.ds(to, size), :], sem.at[n]
            )
        )
    for copy in copies:
        copy.start()
    for at, size in blanks:
        out[at : at + size, :] = jnp.zeros((size, out.shape[1]), out.dtype)
    for copy in copies:
        copy.wait()


def pack(pieces, step=1, size=None, order=None):
    moves, blanks, at = [], [], 0
    for n, piece in enumerate(pieces):
        rows = piece.shape[0]
        if order is None:
            moves.append((n, 0, rows, at))
        else:
            moves += [(n, low, size, -1 - len(moves) - low // size) for low in range(0, rows, size)]
        at += rows
        if at % step:
            blanks.append((at, -at % step))
            at += -at % step
    if order is None:
        order = jnp.zeros((1,), jnp.int32)
    return pl.pallas_call(
        functools.partial(pack_kernel, len(pieces), moves, blanks),
        out_shape=jax.ShapeDtypeStruct((at, pieces[0].shape[1]), pieces[0].dtype),
        in_specs=[pl.BlockSpec(memory_space=pltpu.SMEM)]
        + [pl.BlockSpec(memory_space=pl.ANY)] * len(pieces),
        out_specs=pl.BlockSpec(memory_space=pltpu.VMEM),
        scratch_shapes=[pltpu.SemaphoreType.DMA((len(moves),))],
        compiler_params=pltpu.CompilerParams(vmem_limit_bytes=VMEM),
        cost_estimate=pl.CostEstimate(
            flops=0, bytes_accessed=4 * at * pieces[0].shape[1], transcendentals=0
        ),
    )(order, *pieces)


def project_kernel(counts, size, step, order, gain, *refs):
    blocks, pieces = refs[: counts[0]], refs[counts[0] : sum(counts)]
    normed_out, weight_out, raw, arrived, normed, weight, in_sem, weight_sem, out_sem = refs[
        sum(counts) :
    ]
    rows = blocks[0].shape[0]
    loads = [
        pltpu.make_async_copy(block, arrived.at[pl.ds(n * rows, rows), :], in_sem.at[n])
        for n, block in enumerate(blocks)
    ]
    parts = pieces[0].shape[0] // step
    moves = []
    for n, piece in enumerate(pieces):
        for part in range(parts):
            to = pl.multiple_of(order[n * parts + part] * size, size)
            moves.append(
                pltpu.make_async_copy(
                    piece.at[pl.ds(part * step, size), :],
                    weight.at[pl.ds(to, size), :],
                    weight_sem.at[n * parts + part],
                )
            )
    for copy in loads + moves:
        copy.start()
    stores = []
    for n, load in enumerate(loads):
        load.wait()
        at = slice(n * rows, (n + 1) * rows)
        values = arrived[at, :].astype(f32)
        mean = jnp.mean(values * values, axis=1, keepdims=True)
        normed[at, :] = (values * lax.rsqrt(mean + epsilon) * gain[...]).astype(bf16)
    stores.append(pltpu.make_async_copy(normed, normed_out, out_sem.at[0]))
    for copy in moves:
        copy.wait()
    stores.append(pltpu.make_async_copy(weight, weight_out, out_sem.at[1]))
    for copy in stores:
        copy.start()
    raw[...] = dot(normed[...], weight[...], ((1,), (0,)))
    for copy in stores:
        copy.wait()


def project(blocks, gain, pieces, size, step, order):
    tokens, features = sum(block.shape[0] for block in blocks), blocks[0].shape[1]
    weight_rows = sum(piece.shape[0] for piece in pieces) // step * size
    columns = pieces[0].shape[1]
    anywhere = pl.BlockSpec(memory_space=pl.ANY)
    inside = pl.BlockSpec(memory_space=pltpu.VMEM)
    return pl.pallas_call(
        functools.partial(project_kernel, (len(blocks), len(pieces)), size, step),
        out_shape=[
            jax.ShapeDtypeStruct((tokens, features), bf16),
            jax.ShapeDtypeStruct((weight_rows, columns), bf16),
            jax.ShapeDtypeStruct((tokens, columns), f32),
        ],
        in_specs=[pl.BlockSpec(memory_space=pltpu.SMEM), inside]
        + [anywhere] * (len(blocks) + len(pieces)),
        out_specs=[anywhere, anywhere, inside],
        scratch_shapes=[
            pltpu.VMEM((tokens, features), bf16),
            pltpu.VMEM((tokens, features), bf16),
            pltpu.VMEM((weight_rows, columns), bf16),
            pltpu.SemaphoreType.DMA((len(blocks),)),
            pltpu.SemaphoreType.DMA((weight_rows // size,)),
            pltpu.SemaphoreType.DMA((2,)),
        ],
        compiler_params=pltpu.CompilerParams(vmem_limit_bytes=VMEM),
        cost_estimate=pl.CostEstimate(
            flops=2 * tokens * features * columns,
            bytes_accessed=4 * (tokens * features + weight_rows * columns + tokens * columns),
            transcendentals=0,
        ),
    )(order, gain, *blocks, *pieces)


def experts_kernel(pieces, start, expert, meta, vector, *refs):
    row_pieces, grad_pieces = refs[:pieces], refs[pieces : 2 * pieces]
    into_hbm, down_hbm = refs[2 * pieces : 2 * pieces + 2]
    refs = refs[2 * pieces + 2 :]
    unit_outs, refs = refs[:3], refs[3:]
    rest, count = meta.shape[0], meta.shape[-1]
    blocks = rest * CORES
    term_outs, vector_grad, refs = refs[: rest + 1], refs[rest + 1], refs[rest + 2 :]
    rows, grads, into, down, middle_all, gate_all, up_all = refs[:7]
    in_sem, weight_sem, out_sem, term_sem, terms = refs[7:12]
    tokens, features = rows.shape
    units = down.shape[0]
    size = tokens // pieces
    parts = ((0, start), (start, units))

    loads = [
        [
            pltpu.make_async_copy(
                piece, held.at[pl.ds(n * size, size), :], in_sem.at[which, n]
            )
            for n, piece in enumerate(arrived)
        ]
        for which, (arrived, held) in enumerate(((row_pieces, rows), (grad_pieces, grads)))
    ]
    weights = [
        [
            pltpu.make_async_copy(
                source.at[pl.ds(first + low, high - low), :],
                held.at[pl.ds(first + low, high - low), :],
                weight_sem.at[part, which],
            )
            for which, (source, held, first) in enumerate(
                ((into_hbm, into, 0), (into_hbm, into, units), (down_hbm, down, 0))
            )
        ]
        for part, (low, high) in enumerate(parts)
    ]
    for copy in loads[0] + weights[0] + loads[1]:
        copy.start()

    @pl.when(expert[1] == 1)
    def _():
        for copy in weights[1]:
            copy.start()

    here = expert[0].astype(f32)
    columns = []
    for core in range(meta.shape[1]):
        for line in range(meta.shape[0]):
            told = meta[line, core]
            scale = jnp.zeros((1, count), f32)
            for k in range(TOP):
                hit = told[k : k + 1] == here
                scale = scale + jnp.where(hit, told[TOP + k : TOP + k + 1], 0.0)
            columns.append(jnp.transpose(jnp.broadcast_to(scale, (count, count)))[:, :1])
    routed_scale = jnp.concatenate(columns, axis=0)

    def work(part, scale):
        low, high = parts[part]
        gate = dot(rows[...], into[low:high, :], ((1,), (1,)))
        up = dot(rows[...], into[units + low : units + high, :], ((1,), (1,)))
        back = dot(grads[...], down[low:high, :], ((1,), (1,)))
        gate_sigmoid = jax.nn.sigmoid(gate)
        silu = gate * gate_sigmoid
        middle = silu * up
        inner = jnp.sum(middle * back, axis=1, keepdims=True) if part else None
        back = back * scale
        middle_all[:, low:high] = (middle * scale).astype(bf16)
        gate_all[:, low:high] = (back * up * (gate_sigmoid + silu * (1.0 - gate_sigmoid))).astype(
            bf16
        )
        up_all[:, low:high] = (back * silu).astype(bf16)
        lanes = pl.ds(low, high - low)
        copies = [
            pltpu.make_async_copy(held.at[:, lanes], out.at[:, lanes], out_sem.at[part, which])
            for which, (held, out) in enumerate(zip((middle_all, gate_all, up_all), unit_outs))
        ]
        for copy in copies:
            copy.start()
        return inner, copies

    for copy in loads[0] + weights[0] + loads[1]:
        copy.wait()
    _, stores = work(0, routed_scale)

    @pl.when(expert[1] == 1)
    def _():
        for copy in weights[1]:
            copy.wait()
        logit = jnp.sum(rows[...].astype(f32) * vector[...], axis=1, keepdims=True)
        shared_scale = jax.nn.sigmoid(logit)
        inner, copies = work(1, shared_scale)
        logit_grad = inner * shared_scale * (1.0 - shared_scale)
        for low in range(0, features, TILE):
            lanes = slice(low, low + TILE)
            value = dot(gate_all[...], into[:units, lanes], ((1,), (0,)))
            value = value + dot(up_all[...], into[units:, lanes], ((1,), (0,)))
            value = (value + logit_grad * vector[:, lanes]).astype(bf16)
            result = dot(middle_all[...], down[:, lanes], ((1,), (0,))).astype(bf16)
            for n in range(blocks):
                at = slice(n * count, (n + 1) * count)
                terms[2 * n * count : (2 * n + 1) * count, lanes] = value[at]
                terms[(2 * n + 1) * count : (2 * n + 2) * count, lanes] = result[at]
        at = 0
        for n, out in enumerate(term_outs):
            copy = pltpu.make_async_copy(
                terms.at[pl.ds(at, out.shape[0]), :], out, term_sem.at[n]
            )
            copy.start()
            copies.append(copy)
            at += out.shape[0]
        vector_grad[...] = jnp.sum(rows[...].astype(f32) * logit_grad, axis=0, keepdims=True)
        for copy in copies:
            copy.wait()

    for copy in stores:
        copy.wait()


def experts(expert, meta, vector, rows, grads, into, down, routed):
    pieces, features = len(rows), rows[0].shape[1]
    tokens, units = sum(piece.shape[0] for piece in rows), down.shape[0]
    rest, count = meta.shape[0], meta.shape[-1]
    anywhere = pl.BlockSpec(memory_space=pl.ANY)
    inside = pl.BlockSpec(memory_space=pltpu.VMEM)
    out_shape = [jax.ShapeDtypeStruct((tokens, units), bf16)] * 3
    out_specs = [anywhere] * 3
    scratch = [
        pltpu.VMEM((tokens, features), bf16),
        pltpu.VMEM((tokens, features), bf16),
        pltpu.VMEM(into.shape, bf16),
        pltpu.VMEM(down.shape, bf16),
        pltpu.VMEM((tokens, units), bf16),
        pltpu.VMEM((tokens, units), bf16),
        pltpu.VMEM((tokens, units), bf16),
        pltpu.SemaphoreType.DMA((2, pieces)),
        pltpu.SemaphoreType.DMA((2, 3)),
        pltpu.SemaphoreType.DMA((2, 3)),
        pltpu.SemaphoreType.DMA((rest + 1,)),
    ]
    out_shape += [jax.ShapeDtypeStruct((2 * count, features), bf16)] * rest
    out_shape += [jax.ShapeDtypeStruct((2 * (tokens - rest * count), features), bf16)]
    out_shape += [jax.ShapeDtypeStruct((1, features), f32)]
    out_specs += [anywhere] * (rest + 1) + [inside]
    scratch += [pltpu.VMEM((2 * tokens, features), bf16)]
    return pl.pallas_call(
        functools.partial(experts_kernel, pieces, routed + -routed % LANES),
        out_shape=out_shape,
        in_specs=[pl.BlockSpec(memory_space=pltpu.SMEM), inside, inside]
        + [anywhere] * (2 * pieces + 2),
        out_specs=out_specs,
        scratch_shapes=scratch,
        compiler_params=pltpu.CompilerParams(vmem_limit_bytes=VMEM),
        cost_estimate=pl.CostEstimate(
            flops=2 * tokens * features * units * 4,
            bytes_accessed=2 * (into.size + down.size + 4 * tokens * features),
            transcendentals=0,
        ),
    )(expert, meta, vector, *rows, *grads, into, down)


def weight_grad_kernel(unit_counts, row_counts, parts, adds, *refs):
    some, pieces = len(unit_counts), len(unit_counts) + len(row_counts)
    units, rows = refs[:some], refs[some:pieces]
    before, refs = refs[pieces : pieces + adds * len(parts)], refs[pieces + adds * len(parts) :]
    outs, (held, tiles, held_sem, tile_sem) = refs[: len(parts)], refs[len(parts) :]
    width = tiles.shape[-1]
    step = pl.program_id(0)
    slot = lax.rem(step, 2)
    used = pl.ds(0, held.shape[1])
    unit_places, row_places = (
        [pl.ds(sum(counts[:n]), count) for n, count in enumerate(counts)]
        for counts in (unit_counts, row_counts)
    )

    def held_copies():
        return [
            pltpu.make_async_copy(units[n].at[:, used], held.at[at, :], held_sem.at[n])
            for n, at in enumerate(unit_places)
        ]

    def tile_copies(index, into):
        columns = pl.ds(pl.multiple_of(index * width, width), width)
        return [
            pltpu.make_async_copy(
                rows[n].at[:, columns], tiles.at[into, at, :], tile_sem.at[into, n]
            )
            for n, at in enumerate(row_places)
        ]

    @pl.when(step == 0)
    def _():
        for copy in held_copies() + tile_copies(0, 0):
            copy.start()
        for copy in held_copies():
            copy.wait()

    for copy in tile_copies(step, slot):
        copy.wait()

    @pl.when(step + 1 < pl.num_programs(0))
    def _():
        for copy in tile_copies(step + 1, 1 - slot):
            copy.start()

    for n, (low, size) in enumerate(parts):
        value = dot(held[:, low : low + size], tiles[slot], ((0,), (0,)))
        outs[n][...] = before[n][...] + value if adds else value.astype(outs[n].dtype)


def weight_grad(units, rows, sizes, before=()):
    unit_counts = [piece.shape[0] for piece in units]
    row_counts = [piece.shape[0] for piece in rows]
    pieces, tokens = len(units) + len(rows), sum(row_counts)
    features = rows[0].shape[1]
    parts, used = [], 0
    for size in sizes:
        parts.append((used, size))
        used += size + -size % LANES
    adds = int(bool(before))
    anywhere = pl.BlockSpec(memory_space=pl.ANY)
    blocks = [pl.BlockSpec((size, TILE), lambda i: (0, i)) for size in sizes]
    return pl.pallas_call(
        functools.partial(weight_grad_kernel, unit_counts, row_counts, parts, adds),
        grid=(features // TILE,),
        out_shape=[
            jax.ShapeDtypeStruct((size, features), bf16 if n else f32)
            for n, size in enumerate(sizes)
        ],
        in_specs=[anywhere] * pieces + blocks * adds,
        out_specs=blocks,
        scratch_shapes=[
            pltpu.VMEM((tokens, used), bf16),
            pltpu.VMEM((2, tokens, TILE), bf16),
            pltpu.SemaphoreType.DMA((len(units),)),
            pltpu.SemaphoreType.DMA((2, len(rows))),
        ],
        input_output_aliases={pieces + n: n for n in range(len(sizes))} if adds else {},
        compiler_params=pltpu.CompilerParams(vmem_limit_bytes=VMEM),
        cost_estimate=pl.CostEstimate(
            flops=2 * tokens * features * sum(sizes),
            bytes_accessed=tokens * (features + used) * 2
            + features * sum(sizes) * 4 * (1 + adds),
            transcendentals=0,
        ),
    )(*units, *rows, *before)


def local(
    layer_input,
    lengths,
    routes,
    route_weight,
    cotangent,
    norm_gain,
    w_qkv,
    b_qkv,
    w_out,
    post_gain,
    w_gate,
    w_up,
    w_down,
    shared_gate,
    shared_up,
    shared_down,
    shared_vector,
):
    grid = Grid()
    row_count, feature_count = layer_input.shape
    groups, owners, chips, na, nb = grid.groups, grid.owners, grid.chips, grid.na, grid.nb
    devices = groups * owners
    heads_here = HEADS // chips
    width = heads_here * HEAD_DIM
    own_rows = w_qkv.shape[0]
    sizes = (w_gate.shape[2], shared_gate.shape[1])
    positions = jnp.arange(row_count, dtype=jnp.int32)
    slots = range(na)
    two = groups == 2

    class Rounds:
        def __init__(self, block):
            self.far, self.blocks = [block], []

        def row(self):
            if len(self.blocks) < na:
                self.blocks.append(grid.row(self.far[len(self.blocks)]))

        def line(self):
            if len(self.far) < na:
                self.far.append(grid.hop(self.far[-1], da=1))

        def all(self):
            return [block for blocks in self.blocks for block in blocks]

    class RowRounds(Rounds):
        def row(self):
            if len(self.blocks) < len(self.far):
                blocks = grid.row(self.far[len(self.blocks)])
                self.blocks.append(jnp.concatenate(blocks, axis=0))

        def rest(self):
            left = self.far[len(self.blocks) :]
            if left:
                blocks = grid.row(jnp.concatenate(left, axis=0))
                for n in range(len(left)):
                    part = slice(n * row_count, (n + 1) * row_count)
                    self.blocks.append(jnp.concatenate([b[part] for b in blocks], axis=0))

    class PairRounds:
        def __init__(self, block):
            self.far, self.blocks = [], [jnp.concatenate(grid.row(block), axis=0)]

        def line(self):
            if len(self.blocks) < na:
                self.blocks.append(grid.hop(self.blocks[-1], da=1))

    def tie_rounds(rounds, *values):
        state = [(r.far, r.blocks) for r in rounds]
        state, *values = tie(state, *values)
        for r, (far, blocks) in zip(rounds, state):
            r.far, r.blocks = far, blocks
        return values

    def place_of(da, db, dc, dg):
        group = (grid.group - dg) % groups
        chip = (grid.a - da) % na * nb + (grid.b - db) % nb
        return (group * chips + chip) * CORES + (grid.core + dc) % CORES

    def with_other(rows):
        return [rows, grid.hop(rows, dc=1)]

    small = jnp.concatenate([norm_gain, post_gain, shared_vector, b_qkv]).astype(f32)
    small_count = small.shape[0]
    small = jnp.pad(small, (0, -small_count % row_count))
    meta = jnp.concatenate(
        [
            routes.T.astype(f32),
            route_weight.T.astype(f32),
            jnp.broadcast_to(lengths.astype(f32)[:, None], (1, row_count)),
            small.reshape(-1, row_count),
        ],
        axis=0,
    )
    meta_rows = meta.shape[0]

    x_rounds = Rounds(layer_input)
    x_rounds.line()
    x_rounds.row()
    sliced = jnp.transpose(w_qkv.reshape(own_rows, 3, chips, width), (2, 0, 1, 3))
    sliced = sliced.reshape(chips, own_rows, 3 * width)
    extra = jnp.pad(meta.astype(bf16).reshape(-1), (0, EXTRA * 3 * width - meta.size))
    extra = jnp.broadcast_to(extra.reshape(1, EXTRA, 3 * width), (chips, EXTRA, 3 * width))
    sliced = jnp.concatenate([sliced, extra], axis=1)
    out_rounds = RowRounds(w_out)
    out_rounds.line()
    into_in = [w_gate, shared_gate, w_up, shared_up]
    down_in = [w_down, shared_down]
    out_far = []

    def out_cross():
        if len(out_far) < len(out_rounds.blocks):
            pair = out_rounds.blocks[len(out_far)]
            out_far.append([grid.cross(pair, shift) for shift in range(1, groups)])

    def tie_out(rounds, *values):
        nonlocal out_far
        out_far, *values = tie_rounds([out_rounds] + rounds, out_far, *values)
        return values

    into_in, sliced = tie_out([x_rounds], into_in, sliced)
    x_rounds.line()
    x_rounds.row()
    by_chip = grid.swap(sliced)
    out_rounds.row()
    into_rows = pack(
        [into_in[0][0].T, into_in[1].T, into_in[2][0].T, into_in[3].T], LANES
    )
    by_chip, into_rows, down_in = tie_out([x_rounds], by_chip, into_rows, down_in)
    part_rows = own_rows + EXTRA
    by_chip = by_chip.reshape(chips * part_rows, 3 * width)
    x_rounds.line()
    x_rounds.row()
    out_rounds.line()
    out_rounds.row()
    by_group = [by_chip] + [grid.cross(by_chip, shift) for shift in range(1, groups)]
    down_rows = pack([down_in[0][0], down_in[1]], LANES)
    by_group, down_rows, cotangent = tie_out([x_rounds], by_group, down_rows, cotangent)
    weight_pieces, order = [], []
    for shift, piece in enumerate(by_group):
        for core in range(CORES):
            weight_pieces.append(grid.hop(piece, dc=1) if core else piece)
            for chip in range(chips):
                order.append(
                    ((grid.group - shift) % groups * chips + chip) * CORES
                    + (grid.core + core) % CORES
                )
    used = -(-meta.size // (3 * width))
    meta_all = jnp.stack(
        [
            piece.reshape(chips, part_rows, 3 * width)[:, own_rows : own_rows + used]
            for piece in weight_pieces
        ]
    ).reshape(devices, -1)
    meta_all = meta_all[:, : meta.size].astype(f32).reshape(devices, meta_rows, row_count)

    def told_by(dg, chip, dc):
        return (dg * CORES + dc) * chips + chip

    by_place = jnp.stack(
        [
            told_by((grid.group - g) % groups, jnp.int32(chip), (grid.core - c) % CORES)
            for g in range(groups)
            for chip in range(chips)
            for c in range(CORES)
        ]
    )
    small_all = jnp.take(meta_all[:, 2 * TOP + 1 :], by_place, axis=0).reshape(devices, -1)
    own_features = norm_gain.shape[0]
    gains_in = small_all[:, :own_features].reshape(-1)
    gains_post = small_all[:, own_features : 2 * own_features].reshape(-1)
    gate_vector = small_all[:, 2 * own_features : 3 * own_features].reshape(-1)
    qkv_bias = small_all[:, 3 * own_features : small_count].reshape(3, chips, width)
    bias_here = lax.dynamic_index_in_dim(qkv_bias, grid.chip, 1, keepdims=False).reshape(-1)
    offsets = [
        told_by(dg, (grid.a - da) % na * nb + (grid.b - db) % nb, dc)
        for dg in range(groups)
        for da in slots
        for dc in range(CORES)
        for db in range(nb)
    ]
    told = jnp.take(meta_all[:, : 2 * TOP + 1], jnp.stack(offsets), axis=0)
    told = told.reshape(groups, na, CORES, nb, 2 * TOP + 1, row_count)
    plane_lengths = told[0, :, 0, :, 2 * TOP, 0].reshape(chips).astype(jnp.int32)
    here = jnp.concatenate([jnp.stack([grid.a, grid.b]).astype(jnp.int32), plane_lengths])
    valid_rows = positions < lengths[0]
    grad_rows = jnp.where(valid_rows[:, None], cotangent, jnp.zeros_like(cotangent))
    grad_rounds = RowRounds(grad_rows)
    while len(x_rounds.blocks) < na:
        x_rounds.row()
    out_rounds.line()
    out_rounds.row()
    out_cross()
    x_blocks, weight_pieces, bias_here, gains_in, here = tie_out(
        [grad_rounds], x_rounds.all(), weight_pieces, bias_here, gains_in, here
    )

    inputs = layer_input.astype(f32)
    out_rounds.row()
    out_cross()
    out_cross()
    grad_rounds.line()
    grad_rounds.row()
    normed_first, heads_weight, raw = project(
        x_blocks, gains_in[None], weight_pieces, own_rows, part_rows,
        jnp.stack(order).astype(jnp.int32),
    )
    low, sent = attention(here, raw, bias_here[None], row_count, nb, heads_here)
    low, sent = tie_out([], low, sent)

    while len(out_far) < na:
        out_cross()
    grad_rounds.line()
    pieces, order = [], []
    for dc in range(CORES):
        for da in slots:
            for dg in range(groups):
                pair = out_far[da][dg - 1] if dg else out_rounds.blocks[da]
                pieces.append(grid.hop(pair, dc=1) if dc else pair)
                order += [place_of(da, db, dc, dg) for db in range(nb)]
    out_weight = pack(pieces, size=own_rows, order=jnp.stack(order).astype(jnp.int32))
    arrived = grid.swap(sent.reshape(chips, row_count, width))
    arrived, out_weight = tie(arrived, out_weight)

    far_grads, far_rows, flying = [], [], []
    crossings = [("grads", s) for s in slots] + [("rows", s) for s in slots]

    def cross_step():
        if crossings and two:
            what, s = crossings[0]
            source, goes = (
                (grad_rounds, far_grads) if what == "grads" else (second_rounds, far_rows)
            )
            if s < len(source.blocks):
                crossings.pop(0)
                flying.append((goes, grid.cross(source.blocks[s], 1)))

    grad_rounds.line()
    grad_rounds.row()
    cross_step()
    context = jnp.transpose(arrived, (1, 0, 2)).reshape(row_count, feature_count)
    residual = inputs + dot(context, out_weight, ((1,), (0,)))
    unit_second, factor_second = unit_norm(residual)
    normed_second = (unit_second * gains_post).astype(bf16)

    expert = (lax.axis_index("ep") // HALVES).astype(jnp.int32)
    expert, far_expert = (jnp.stack([expert, jnp.int32(n)]) for n in (1, 0))
    vector_row = gate_vector[None]
    told = jnp.swapaxes(told[..., : 2 * TOP, :], 2, 3)
    second_rounds = PairRounds(normed_second)
    own = {"rows": [], "grads": [], "middle": [], "gate": [], "up": [], "vector": []}

    def work(s):
        own["rows"].append(with_other(second_rounds.blocks[s]))
        own["grads"].append(with_other(grad_rounds.blocks[s]))
        middle, gate, up, *terms, vector = experts(
            expert, told[0, s], vector_row, own["rows"][s], own["grads"][s],
            into_rows, down_rows, sizes[0],
        )
        for name, value in (("middle", middle), ("gate", gate), ("up", up), ("vector", vector)):
            own[name].append(value)
        return terms

    def add_cores(terms):
        arriving = grid.hop(terms[-1], dc=1)
        return [
            (
                terms[t].astype(f32)
                + arriving[2 * t * row_count : 2 * (t + 1) * row_count].astype(f32)
            ).astype(bf16)
            for t in range(nb)
        ]

    def step_tie(*values):
        nonlocal own, into_rows, down_rows, flying
        arrivals = [rows for _, rows in flying]
        own, arrivals, into_rows, down_rows, *values = tie_rounds(
            [grad_rounds, second_rounds], own, arrivals, into_rows, down_rows, *values
        )
        for (goes, _), rows in zip(flying, arrivals):
            goes.append(rows)
        flying = []
        return values

    def line_sum(rowed, sums, s):
        total = rowed[s] if sums is None else rowed[s] + sums.astype(f32)
        return grid.hop(total.astype(bf16), da=1) if s else total

    def far_work(shift, s):
        rows, grads = with_other(far_rows[s]), with_other(far_grads[s])
        units = experts(
            far_expert, told[shift, s], vector_row, rows, grads,
            into_rows, down_rows, sizes[0],
        )
        return rows, grads, units[:3]

    def flat(lists):
        return [block for blocks in lists for block in blocks]

    rowed, terms, far = {}, {}, []
    sums = None
    for s in slots:
        second_rounds.line()
        if s:
            grad_rounds.rest()
        cross_step()
        if s >= 2:
            rowed[s - 1] = grid.row_sum(add_cores(terms[s - 1]))
        if s >= 3:
            sums = line_sum(rowed, sums, s - 2)
        terms[s] = work(s)
        rowed, terms, sums = step_tie(rowed, terms, sums)
    cross_step()
    rowed[na - 1] = grid.row_sum(add_cores(terms[na - 1]))
    if na > 2:
        sums = line_sum(rowed, sums, na - 2)
    own_gate = weight_grad(own["gate"], flat(own["rows"]), sizes)
    rowed, terms, sums, own_gate = step_tie(rowed, terms, sums, own_gate)
    cross_step()
    sums = line_sum(rowed, sums, na - 1)
    rowed[0] = grid.row_sum(add_cores(terms[0]))
    own_up = weight_grad(own["up"], flat(own["rows"]), sizes)
    own_down = weight_grad(own["middle"], flat(own["grads"]), sizes)
    rowed, sums, own_up, own_down = step_tie(rowed, sums, own_up, own_down)

    both_sums = line_sum(rowed, sums, 0)
    second_grad = both_sums[:row_count]
    outs = residual + both_sums[row_count:]
    output = jnp.where(valid_rows[:, None], outs, 0.0).astype(bf16)
    grad_float = grad_rows.astype(f32)
    post_gain_grad = jnp.sum(second_grad * unit_second, axis=0)
    residual_grad = grad_float + norm_backward(
        second_grad, unit_second, factor_second, gains_post
    )
    attended_grad = residual_grad.astype(bf16)
    context_grad = dot(attended_grad, out_weight, ((1,), (1,))).astype(bf16)
    sent = jnp.transpose(context_grad.reshape(row_count, chips, width), (1, 0, 2))
    arrived = grid.swap(sent)
    cross_step()
    if two:
        far.append(far_work(1, 0))
    totals = [[own_gate[0], own_up[0], own_down[0]]]
    shared = [part[1] for part in (own_gate, own_up, own_down)]
    arrived, attended_grad, far, shared, totals = step_tie(
        arrived, attended_grad, far, shared, totals
    )

    def own_features_of(values, core, group):
        parts = values.reshape(row_count, groups, chips, CORES, own_rows)
        parts = lax.dynamic_index_in_dim(parts, core, 3, keepdims=False)
        parts = lax.dynamic_index_in_dim(parts, group, 1, keepdims=False)
        return parts.reshape(row_count, chips * own_rows)

    projected_grad, bias_here_grad = attention_grad(
        here, low, arrived.reshape(-1, width), row_count, nb, heads_here
    )
    first_terms = dot(projected_grad, heads_weight, ((1,), (1,))).astype(bf16)
    out_parts = []
    for shift in range(groups):
        group = (grid.group + shift) % groups
        mine, other = (
            dot(own_features_of(context, core, group), attended_grad, ((0,), (0,))).astype(bf16)
            for core in (grid.core, 1 - grid.core)
        )
        total = mine.astype(f32) + grid.hop(other, dc=1).astype(f32)
        out_parts.append(total.astype(bf16))
    while crossings and two:
        cross_step()
    shared_far = [
        [grid.cross(part, shift) for shift in range(1, groups)] for part in shared[:1]
    ]
    first_terms, projected_grad, out_parts, far, shared_far = step_tie(
        first_terms, projected_grad, out_parts, far, shared_far
    )

    def in_order(*parts):
        parts = [part.astype(f32) for part in parts]
        if two:
            return parts[0] + parts[1]
        total = 0.0
        for group in range(groups):
            far_by = (grid.group - group) % groups
            total = total + sum(
                jnp.where(far_by == shift, part, 0.0) for shift, part in enumerate(parts)
            )
        return total

    slot_first = first_terms.reshape(na, nb * row_count, feature_count)

    def end_tie(*values):
        nonlocal far, into_rows, down_rows
        far, into_rows, down_rows, *values = tie(far, into_rows, down_rows, *values)
        return values

    def far_grad(units, place):
        before = [totals[0][units]] if two else ()
        return weight_grad(
            [work[2][(1, 2, 0)[units]] for work in far], flat(work[place] for work in far),
            sizes[:1], before,
        )[0]

    qkv_grad = dot(normed_first, projected_grad, ((0,), (0,))).astype(bf16)
    half = chips * own_rows // 2
    first_sums = line_sum(slot_first, None, 1) if na > 1 else None
    crossed = [[grid.cross(part[:half], n + 1)] for n, part in enumerate(out_parts[1:])]
    if two:
        far.append(far_work(1, 1))
    slot_first, qkv_grad, crossed, out_parts, first_sums = end_tie(
        slot_first, qkv_grad, crossed, out_parts, first_sums
    )
    if na > 2:
        first_sums = line_sum(slot_first, first_sums, 2)
    for n, part in enumerate(out_parts[1:]):
        crossed[n].append(grid.cross(part[half:], n + 1))
    qkv_grad = grid.scatter_core(qkv_grad.reshape(groups, chips, CORES, own_rows, 3 * width), 2)
    if two:
        far.append(far_work(1, 2 % na))
    slot_first, qkv_grad, crossed, out_parts, first_sums, shared = end_tie(
        slot_first, qkv_grad.astype(bf16), crossed, out_parts, first_sums, shared
    )
    for s in range(3, na):
        first_sums = line_sum(slot_first, first_sums, s)
    qkv_grad = grid.scatter_groups(qkv_grad).astype(bf16)
    out_total = out_parts[0].astype(f32)
    for halves in crossed:
        out_total = out_total + jnp.concatenate(halves, axis=0).astype(f32)
    out_rowed = grid.scatter_row(
        out_total.astype(bf16).reshape(na, nb, own_rows, feature_count)
    )
    shared_far.append([grid.cross(shared[1], shift) for shift in range(1, groups)])
    if two:
        if na > 3:
            far.append(far_work(1, 3))
        slot_first, first_sums, qkv_grad, out_rowed, shared = end_tie(
            slot_first, first_sums, qkv_grad, out_rowed, shared
        )
    first_terms_here = slot_first[0] if first_sums is None else line_sum(slot_first, first_sums, 0)
    first_grad = grid.row_sum(
        first_terms_here.astype(bf16).reshape(nb, row_count, feature_count)
    )
    qkv_grad = grid.swap(qkv_grad).reshape(chips, own_rows, 3, width)
    if two:
        gate_total = far_grad(0, 0)
        gate_total, first_grad, shared_far, shared, qkv_grad, out_rowed = end_tie(
            gate_total, first_grad, shared_far, shared, qkv_grad, out_rowed
        )
    out_weight_grad = grid.scatter_line(out_rowed)
    shared_far.append([grid.cross(shared[2], shift) for shift in range(1, groups)])
    unit_first, factor_first = unit_norm(inputs)
    input_part = norm_backward(first_grad, unit_first, factor_first, gains_in)
    layer_grad = (residual_grad + input_part).astype(bf16)
    qkv_weight_grad = jnp.transpose(qkv_grad, (1, 2, 0, 3)).reshape(own_rows, -1).astype(f32)
    if two:
        gate_grad, up_grad, down_grad = gate_total, far_grad(1, 0), far_grad(2, 1)
    else:
        second_blocks, grad_blocks = second_rounds.blocks, grad_rounds.blocks
        for shift in range(1, groups):
            totals, second_blocks, grad_blocks = tie(totals, second_blocks, grad_blocks)
            far_grads, far_rows = (
                [grid.cross(rows, shift) for rows in source]
                for source in (grad_blocks, second_blocks)
            )
            far = [far_work(shift, s) for s in slots]
            totals.append([far_grad(0, 0), far_grad(1, 0), far_grad(2, 1)])
        gate_grad, up_grad, down_grad = (in_order(*parts) for parts in zip(*totals))
    shared_gate_grad, shared_up_grad, shared_down_grad = (
        in_order(here_part, *parts) for here_part, parts in zip(shared, shared_far)
    )

    vector_grad = sum(own["vector"])[0]
    gain_grad = jnp.sum(first_terms.astype(f32) * normed_first.astype(f32), axis=0) / gains_in
    bias_grad = jnp.zeros((3, chips, width), f32)
    bias_grad = lax.dynamic_update_slice(
        bias_grad, bias_here_grad.reshape(3, 1, width), (0, grid.chip, 0)
    )
    vectors = jnp.concatenate(
        [
            gain_grad.reshape(devices, -1),
            post_gain_grad.reshape(devices, -1),
            vector_grad.reshape(devices, -1),
            bias_grad.reshape(devices, -1),
        ],
        axis=1,
    ).reshape(groups, na, nb, CORES, -1)
    vectors = grid.scatter_core(vectors, 3)
    vectors = grid.scatter_groups(vectors)
    vectors = grid.scatter_line(grid.scatter_row(vectors))
    return (
        output,
        layer_grad,
        vectors[:own_features],
        qkv_weight_grad,
        vectors[3 * own_features :],
        out_weight_grad,
        vectors[own_features : 2 * own_features],
        gate_grad.T[None],
        up_grad.T[None],
        down_grad[None],
        shared_gate_grad.T,
        shared_up_grad.T,
        shared_down_grad,
        vectors[2 * own_features : 3 * own_features],
    )


def solution(mesh):
    rows = P(("dp", "ep"), None)
    split = P(("dp", "ep"))
    parts = P("ep", None, None)
    return jax.shard_map(
        local,
        mesh=mesh,
        in_specs=(
            rows,
            split,
            rows,
            rows,
            rows,
            split,
            rows,
            split,
            rows,
            split,
            parts,
            parts,
            parts,
            P(None, "ep"),
            P(None, "ep"),
            P("ep", None),
            split,
        ),
        out_specs=(
            rows,
            rows,
            split,
            rows,
            split,
            rows,
            split,
            parts,
            parts,
            parts,
            P(None, "ep"),
            P(None, "ep"),
            P("ep", None),
            split,
        ),
        check_vma=False,
    )
```

```python
import functools
import math

import jax
import jax.numpy as jnp
from jax import lax
from jax.experimental import pallas as pl
from jax.experimental.pallas import tpu as pltpu
from jax.sharding import PartitionSpec as P

HEADS = 16
HEAD_DIM = 128
TOP = 4
HALVES = 2
CORES = 2
LINE = 4
LANES = 128
TILE = 512
VMEM = 56 << 20
EXTRA = 16


epsilon = 1e-06
rope_base = 1000000.0
bf16 = jnp.bfloat16
f32 = jnp.float32


def unit_norm(values):
    factor = lax.rsqrt(jnp.mean(values * values, axis=-1, keepdims=True) + epsilon)
    return (values * factor, factor)


def norm_backward(incoming, unit_rows, factor, gain_row):
    scaled = incoming * gain_row
    inner_mean = jnp.mean(scaled * unit_rows, axis=-1, keepdims=True)
    return factor * (scaled - unit_rows * inner_mean)


def rope_tables(row_count, head_size):
    inverse = rope_base ** (-jnp.arange(0, head_size, 2, dtype=f32) / head_size)
    angles = jnp.arange(row_count, dtype=f32)[:, None] * inverse[None, :]
    angles = jnp.concatenate([angles, angles], axis=-1)
    return (jnp.cos(angles)[:, None, :], jnp.sin(angles)[:, None, :])


def dot(left, right, dims):
    return lax.dot_general(left, right, (dims, ((), ())), preferred_element_type=f32)


def tie(*values):
    return lax.optimization_barrier(values)


class Grid:
    def __init__(self):
        self.groups = lax.axis_size("dp")
        self.owners = lax.axis_size("ep")
        self.chips = self.owners // CORES
        self.na = math.gcd(LINE, self.chips)
        self.nb = self.chips // self.na
        self.group = lax.axis_index("dp")
        me = lax.axis_index("ep")
        self.chip = me // CORES
        self.core = me % CORES
        self.a = self.chip // self.nb
        self.b = self.chip % self.nb

    def place(self, a, b, c):
        return ((a % self.na) * self.nb + b % self.nb) * CORES + c % CORES

    def hop(self, values, da=0, db=0, dc=0):
        pairs = [
            (self.place(a, b, c), self.place(a + da, b + db, c + dc))
            for a in range(self.na)
            for b in range(self.nb)
            for c in range(CORES)
        ]
        return lax.ppermute(values, "ep", pairs)

    def cross(self, values, shift):
        pairs = [(g, (g + shift) % self.groups) for g in range(self.groups)]
        return lax.ppermute(values, "dp", pairs)

    def row(self, block):
        return [block] + [self.hop(block, db=db) for db in range(1, self.nb)]

    def row_sum(self, terms):
        total = terms[0].astype(f32)
        for db in range(1, self.nb):
            total = total + self.hop(terms[db], db=-db).astype(f32)
        return total

    def core_sum(self, terms):
        return (terms[0].astype(f32) + self.hop(terms[1], dc=1).astype(f32)).astype(bf16)

    def same_core(self):
        return [[k * CORES + c for k in range(self.chips)] for c in range(CORES)]

    def swap(self, blocks):
        return lax.all_to_all(
            blocks,
            "ep",
            split_axis=0,
            concat_axis=0,
            tiled=True,
            axis_index_groups=self.same_core(),
        )

    def scatter_core(self, terms, axis):
        mine = lax.dynamic_index_in_dim(terms, self.core, axis, keepdims=False)
        other = lax.dynamic_index_in_dim(terms, 1 - self.core, axis, keepdims=False)
        return mine.astype(f32) + self.hop(other, dc=1).astype(f32)

    def scatter_groups(self, terms):
        total = lax.dynamic_index_in_dim(terms, self.group, 0, keepdims=False).astype(f32)
        for shift in range(1, self.groups):
            there = (self.group + shift) % self.groups
            piece = lax.dynamic_index_in_dim(terms, there, 0, keepdims=False)
            total = total + self.cross(piece, shift).astype(f32)
        return total

    def scatter_row(self, terms):
        total = lax.dynamic_index_in_dim(terms, self.b, 1, keepdims=False).astype(f32)
        for db in range(1, self.nb):
            there = (self.b + db) % self.nb
            piece = lax.dynamic_index_in_dim(terms, there, 1, keepdims=False)
            total = total + self.hop(piece, db=db).astype(f32)
        return total.astype(terms.dtype)

    def scatter_line(self, terms):
        total = lax.dynamic_index_in_dim(terms, self.a, 0, keepdims=False).astype(f32)
        for da in range(1, self.na):
            there = (self.a + da) % self.na
            piece = lax.dynamic_index_in_dim(terms, there, 0, keepdims=False)
            total = total + self.hop(piece, da=da).astype(f32)
        return total


def turned_lanes(values):
    return pltpu.roll(values, HEAD_DIM // 2, 1)


def head_probabilities(query, key, length):
    scores = dot(query, key, ((1,), (1,))) / math.sqrt(HEAD_DIM)
    query_place = lax.broadcasted_iota(jnp.int32, scores.shape, 0)
    key_place = lax.broadcasted_iota(jnp.int32, scores.shape, 1)
    allowed = (key_place <= query_place) & (key_place < length)
    scores = jnp.where(allowed, scores, -1e30)
    exponent = jnp.exp(scores - jnp.max(scores, axis=1, keepdims=True))
    return exponent / jnp.sum(exponent, axis=1, keepdims=True)


def home_rows(here, sequence, sequences, rows):
    return pl.ds(pl.multiple_of(lax.rem(here[1] - sequence + sequences, sequences) * rows, rows), rows)


def attention_kernel(sequences, heads, here, raw, bias, cosine, signed_sine, low, context):
    rows = cosine.shape[0]
    width = heads * HEAD_DIM
    for sequence in range(sequences):
        at = slice(sequence * rows, (sequence + 1) * rows)
        home = home_rows(here, sequence, sequences, rows)
        length = here[2 + pl.program_id(0) * sequences + sequence]
        for head in range(heads):
            parts = []
            for part in range(3):
                low_lane = part * width + head * HEAD_DIM
                lanes = slice(low_lane, low_lane + HEAD_DIM)
                values = raw[at, lanes] + bias[:, lanes]
                if part < 2:
                    values = values * cosine[...] + turned_lanes(values) * signed_sine[...]
                values = values.astype(bf16)
                low[at, lanes] = values
                parts.append(values)
            probabilities = head_probabilities(parts[0], parts[1], length).astype(bf16)
            lanes = slice(head * HEAD_DIM, (head + 1) * HEAD_DIM)
            context[home, lanes] = dot(probabilities, parts[2], ((1,), (0,))).astype(bf16)


def attention_grad_kernel(
    sequences, heads, here, low, incoming, cosine, sine, sign, outgoing, bias_grad
):
    rows = cosine.shape[0]
    width = heads * HEAD_DIM
    root_size = math.sqrt(HEAD_DIM)

    @pl.when(pl.program_id(0) == 0)
    def _():
        bias_grad[...] = jnp.zeros_like(bias_grad)

    for sequence in range(sequences):
        at = slice(sequence * rows, (sequence + 1) * rows)
        home = home_rows(here, sequence, sequences, rows)
        length = here[2 + pl.program_id(0) * sequences + sequence]
        for head in range(heads):
            lanes = [
                slice(part * width + head * HEAD_DIM, part * width + (head + 1) * HEAD_DIM)
                for part in range(3)
            ]
            query, key, value = (low[at, part] for part in lanes)
            grad = incoming[home, lanes[0]]
            probabilities = head_probabilities(query, key, length)
            probs_grad = dot(grad, value, ((1,), (1,)))
            inner = jnp.sum(probabilities * probs_grad, axis=1, keepdims=True)
            score_grad = (probabilities * (probs_grad - inner)).astype(bf16)
            grads = [
                dot(score_grad, key, ((1,), (0,))) / root_size,
                dot(score_grad, query, ((0,), (0,))) / root_size,
                dot(probabilities.astype(bf16), grad, ((0,), (0,))),
            ]
            for part in range(3):
                values = grads[part]
                if part < 2:
                    values = values * cosine[...] - turned_lanes(values * sine[...]) * sign[...]
                values = values.astype(bf16)
                outgoing[at, lanes[part]] = values
                bias_grad[:, lanes[part]] += jnp.sum(values.astype(f32), axis=0, keepdims=True)


def rope_inputs(row_count):
    cosine, sine = (table[:, 0] for table in rope_tables(row_count, HEAD_DIM))
    sign = jnp.where(jnp.arange(HEAD_DIM) < HEAD_DIM // 2, -1.0, 1.0).astype(f32)[None]
    return cosine, sine, sign


def attention(here, raw, bias, rows, sequences, heads):
    tokens, width = raw.shape[0], heads * HEAD_DIM
    cosine, sine, sign = rope_inputs(rows)
    block = sequences * rows
    lines = tokens // block
    whole = lambda *shape: pl.BlockSpec(shape, lambda i, here: (0, 0))
    return pl.pallas_call(
        functools.partial(attention_kernel, sequences, heads),
        out_shape=[
            jax.ShapeDtypeStruct((tokens, 3 * width), bf16),
            jax.ShapeDtypeStruct((tokens, width), bf16),
        ],
        grid_spec=pltpu.PrefetchScalarGridSpec(
            num_scalar_prefetch=1,
            grid=(lines,),
            in_specs=[
                pl.BlockSpec((block, 3 * width), lambda i, here: (i, 0)),
                whole(1, 3 * width),
                whole(rows, HEAD_DIM),
                whole(rows, HEAD_DIM),
            ],
            out_specs=[
                pl.BlockSpec((block, 3 * width), lambda i, here: (i, 0)),
                pl.BlockSpec((block, width), lambda i, here: (lax.rem(here[0] - i + lines, lines), 0)),
            ],
        ),
        cost_estimate=pl.CostEstimate(
            flops=300 * tokens * rows * width, bytes_accessed=tokens * width * 20, transcendentals=0
        ),
    )(here, raw, bias, cosine, sine * sign)


def attention_grad(here, low, incoming, rows, sequences, heads):
    tokens, width = low.shape[0], heads * HEAD_DIM
    block = sequences * rows
    lines = tokens // block
    whole = lambda *shape: pl.BlockSpec(shape, lambda i, here: (0, 0))
    return pl.pallas_call(
        functools.partial(attention_grad_kernel, sequences, heads),
        out_shape=[
            jax.ShapeDtypeStruct((tokens, 3 * width), bf16),
            jax.ShapeDtypeStruct((1, 3 * width), f32),
        ],
        grid_spec=pltpu.PrefetchScalarGridSpec(
            num_scalar_prefetch=1,
            grid=(lines,),
            in_specs=[
                pl.BlockSpec((block, 3 * width), lambda i, here: (i, 0)),
                pl.BlockSpec((block, width), lambda i, here: (lax.rem(here[0] - i + lines, lines), 0)),
                whole(rows, HEAD_DIM),
                whole(rows, HEAD_DIM),
                whole(1, HEAD_DIM),
            ],
            out_specs=[
                pl.BlockSpec((block, 3 * width), lambda i, here: (i, 0)),
                whole(1, 3 * width),
            ],
        ),
        cost_estimate=pl.CostEstimate(
            flops=370 * tokens * rows * width, bytes_accessed=tokens * width * 14, transcendentals=0
        ),
    )(here, low, incoming, *rope_inputs(rows))


def pack_kernel(count, moves, blanks, order, *refs):
    sources, out, sem = refs[:count], refs[-2], refs[-1]
    copies = []
    for n, (source, low, size, to) in enumerate(moves):
        if to < 0:
            to = pl.multiple_of(order[-1 - to] * size, size)
        copies.append(
            pltpu.make_async_copy(
                sources[source].at[pl.ds(low, size), :], out.at[pl.ds(to, size), :], sem.at[n]
            )
        )
    for copy in copies:
        copy.start()
    for at, size in blanks:
        out[at : at + size, :] = jnp.zeros((size, out.shape[1]), out.dtype)
    for copy in copies:
        copy.wait()


def pack(pieces, step=1, size=None, order=None):
    moves, blanks, at = [], [], 0
    for n, piece in enumerate(pieces):
        rows = piece.shape[0]
        if order is None:
            moves.append((n, 0, rows, at))
        else:
            moves += [(n, low, size, -1 - len(moves) - low // size) for low in range(0, rows, size)]
        at += rows
        if at % step:
            blanks.append((at, -at % step))
            at += -at % step
    if order is None:
        order = jnp.zeros((1,), jnp.int32)
    return pl.pallas_call(
        functools.partial(pack_kernel, len(pieces), moves, blanks),
        out_shape=jax.ShapeDtypeStruct((at, pieces[0].shape[1]), pieces[0].dtype),
        in_specs=[pl.BlockSpec(memory_space=pltpu.SMEM)]
        + [pl.BlockSpec(memory_space=pl.ANY)] * len(pieces),
        out_specs=pl.BlockSpec(memory_space=pltpu.VMEM),
        scratch_shapes=[pltpu.SemaphoreType.DMA((len(moves),))],
        compiler_params=pltpu.CompilerParams(vmem_limit_bytes=VMEM),
        cost_estimate=pl.CostEstimate(
            flops=0, bytes_accessed=4 * at * pieces[0].shape[1], transcendentals=0
        ),
    )(order, *pieces)


def project_kernel(counts, size, step, order, gain, *refs):
    blocks, pieces = refs[: counts[0]], refs[counts[0] : sum(counts)]
    normed_out, weight_out, raw, arrived, normed, weight, in_sem, weight_sem, out_sem = refs[
        sum(counts) :
    ]
    rows = blocks[0].shape[0]
    loads = [
        pltpu.make_async_copy(block, arrived.at[pl.ds(n * rows, rows), :], in_sem.at[n])
        for n, block in enumerate(blocks)
    ]
    parts = pieces[0].shape[0] // step
    moves = []
    for n, piece in enumerate(pieces):
        for part in range(parts):
            to = pl.multiple_of(order[n * parts + part] * size, size)
            moves.append(
                pltpu.make_async_copy(
                    piece.at[pl.ds(part * step, size), :],
                    weight.at[pl.ds(to, size), :],
                    weight_sem.at[n * parts + part],
                )
            )
    for copy in loads + moves:
        copy.start()
    stores = []
    for n, load in enumerate(loads):
        load.wait()
        at = slice(n * rows, (n + 1) * rows)
        values = arrived[at, :].astype(f32)
        mean = jnp.mean(values * values, axis=1, keepdims=True)
        normed[at, :] = (values * lax.rsqrt(mean + epsilon) * gain[...]).astype(bf16)
    stores.append(pltpu.make_async_copy(normed, normed_out, out_sem.at[0]))
    for copy in moves:
        copy.wait()
    stores.append(pltpu.make_async_copy(weight, weight_out, out_sem.at[1]))
    for copy in stores:
        copy.start()
    raw[...] = dot(normed[...], weight[...], ((1,), (0,)))
    for copy in stores:
        copy.wait()


def project(blocks, gain, pieces, size, step, order):
    tokens, features = sum(block.shape[0] for block in blocks), blocks[0].shape[1]
    weight_rows = sum(piece.shape[0] for piece in pieces) // step * size
    columns = pieces[0].shape[1]
    anywhere = pl.BlockSpec(memory_space=pl.ANY)
    inside = pl.BlockSpec(memory_space=pltpu.VMEM)
    return pl.pallas_call(
        functools.partial(project_kernel, (len(blocks), len(pieces)), size, step),
        out_shape=[
            jax.ShapeDtypeStruct((tokens, features), bf16),
            jax.ShapeDtypeStruct((weight_rows, columns), bf16),
            jax.ShapeDtypeStruct((tokens, columns), f32),
        ],
        in_specs=[pl.BlockSpec(memory_space=pltpu.SMEM), inside]
        + [anywhere] * (len(blocks) + len(pieces)),
        out_specs=[anywhere, anywhere, inside],
        scratch_shapes=[
            pltpu.VMEM((tokens, features), bf16),
            pltpu.VMEM((tokens, features), bf16),
            pltpu.VMEM((weight_rows, columns), bf16),
            pltpu.SemaphoreType.DMA((len(blocks),)),
            pltpu.SemaphoreType.DMA((weight_rows // size,)),
            pltpu.SemaphoreType.DMA((2,)),
        ],
        compiler_params=pltpu.CompilerParams(vmem_limit_bytes=VMEM),
        cost_estimate=pl.CostEstimate(
            flops=7 * tokens * features * columns,
            bytes_accessed=4 * (tokens * features + weight_rows * columns + tokens * columns),
            transcendentals=0,
        ),
    )(order, gain, *blocks, *pieces)


def experts_kernel(pieces, start, expert, meta, vector, *refs):
    row_pieces, grad_pieces = refs[:pieces], refs[pieces : 2 * pieces]
    into_hbm, down_hbm = refs[2 * pieces : 2 * pieces + 2]
    refs = refs[2 * pieces + 2 :]
    unit_outs, refs = refs[:3], refs[3:]
    rest, count = meta.shape[0], meta.shape[-1]
    blocks = rest * CORES
    term_outs, vector_grad, refs = refs[: rest + 1], refs[rest + 1], refs[rest + 2 :]
    rows, grads, into, down, middle_all, gate_all, up_all = refs[:7]
    in_sem, weight_sem, out_sem, term_sem, terms = refs[7:12]
    tokens, features = rows.shape
    units = down.shape[0]
    size = tokens // pieces
    parts = ((0, start), (start, units))

    loads = [
        [
            pltpu.make_async_copy(
                piece, held.at[pl.ds(n * size, size), :], in_sem.at[which, n]
            )
            for n, piece in enumerate(arrived)
        ]
        for which, (arrived, held) in enumerate(((row_pieces, rows), (grad_pieces, grads)))
    ]
    weights = [
        [
            pltpu.make_async_copy(
                source.at[pl.ds(first + low, high - low), :],
                held.at[pl.ds(first + low, high - low), :],
                weight_sem.at[part, which],
            )
            for which, (source, held, first) in enumerate(
                ((into_hbm, into, 0), (into_hbm, into, units), (down_hbm, down, 0))
            )
        ]
        for part, (low, high) in enumerate(parts)
    ]
    for copy in loads[0] + weights[0] + loads[1]:
        copy.start()

    @pl.when(expert[1] == 1)
    def _():
        for copy in weights[1]:
            copy.start()

    here = expert[0].astype(f32)
    columns = []
    for core in range(meta.shape[1]):
        for line in range(meta.shape[0]):
            told = meta[line, core]
            scale = jnp.zeros((1, count), f32)
            for k in range(TOP):
                hit = told[k : k + 1] == here
                scale = scale + jnp.where(hit, told[TOP + k : TOP + k + 1], 0.0)
            columns.append(jnp.transpose(jnp.broadcast_to(scale, (count, count)))[:, :1])
    routed_scale = jnp.concatenate(columns, axis=0)

    def work(part, scale):
        low, high = parts[part]
        gate = dot(rows[...], into[low:high, :], ((1,), (1,)))
        up = dot(rows[...], into[units + low : units + high, :], ((1,), (1,)))
        back = dot(grads[...], down[low:high, :], ((1,), (1,)))
        gate_sigmoid = jax.nn.sigmoid(gate)
        silu = gate * gate_sigmoid
        middle = silu * up
        inner = jnp.sum(middle * back, axis=1, keepdims=True) if part else None
        back = back * scale
        middle_all[:, low:high] = (middle * scale).astype(bf16)
        gate_all[:, low:high] = (back * up * (gate_sigmoid + silu * (1.0 - gate_sigmoid))).astype(
            bf16
        )
        up_all[:, low:high] = (back * silu).astype(bf16)
        lanes = pl.ds(low, high - low)
        copies = [
            pltpu.make_async_copy(held.at[:, lanes], out.at[:, lanes], out_sem.at[part, which])
            for which, (held, out) in enumerate(zip((middle_all, gate_all, up_all), unit_outs))
        ]
        for copy in copies:
            copy.start()
        return inner, copies

    for copy in loads[0] + weights[0] + loads[1]:
        copy.wait()
    _, stores = work(0, routed_scale)

    @pl.when(expert[1] == 1)
    def _():
        for copy in weights[1]:
            copy.wait()
        logit = jnp.sum(rows[...].astype(f32) * vector[...], axis=1, keepdims=True)
        shared_scale = jax.nn.sigmoid(logit)
        inner, copies = work(1, shared_scale)
        logit_grad = inner * shared_scale * (1.0 - shared_scale)
        for low in range(0, features, TILE):
            lanes = slice(low, low + TILE)
            value = dot(gate_all[...], into[:units, lanes], ((1,), (0,)))
            value = value + dot(up_all[...], into[units:, lanes], ((1,), (0,)))
            value = (value + logit_grad * vector[:, lanes]).astype(bf16)
            result = dot(middle_all[...], down[:, lanes], ((1,), (0,))).astype(bf16)
            for n in range(blocks):
                at = slice(n * count, (n + 1) * count)
                terms[2 * n * count : (2 * n + 1) * count, lanes] = value[at]
                terms[(2 * n + 1) * count : (2 * n + 2) * count, lanes] = result[at]
        at = 0
        for n, out in enumerate(term_outs):
            copy = pltpu.make_async_copy(
                terms.at[pl.ds(at, out.shape[0]), :], out, term_sem.at[n]
            )
            copy.start()
            copies.append(copy)
            at += out.shape[0]
        vector_grad[...] = jnp.sum(rows[...].astype(f32) * logit_grad, axis=0, keepdims=True)
        for copy in copies:
            copy.wait()

    for copy in stores:
        copy.wait()


def experts(expert, meta, vector, rows, grads, into, down, routed, terms_too):
    pieces, features = len(rows), rows[0].shape[1]
    tokens, units = sum(piece.shape[0] for piece in rows), down.shape[0]
    rest, count = meta.shape[0], meta.shape[-1]
    anywhere = pl.BlockSpec(memory_space=pl.ANY)
    inside = pl.BlockSpec(memory_space=pltpu.VMEM)
    out_shape = [jax.ShapeDtypeStruct((tokens, units), bf16)] * 3
    out_specs = [anywhere] * 3
    scratch = [
        pltpu.VMEM((tokens, features), bf16),
        pltpu.VMEM((tokens, features), bf16),
        pltpu.VMEM(into.shape, bf16),
        pltpu.VMEM(down.shape, bf16),
        pltpu.VMEM((tokens, units), bf16),
        pltpu.VMEM((tokens, units), bf16),
        pltpu.VMEM((tokens, units), bf16),
        pltpu.SemaphoreType.DMA((2, pieces)),
        pltpu.SemaphoreType.DMA((2, 3)),
        pltpu.SemaphoreType.DMA((2, 3)),
        pltpu.SemaphoreType.DMA((rest + 1,)),
    ]
    out_shape += [jax.ShapeDtypeStruct((2 * count, features), bf16)] * rest
    out_shape += [jax.ShapeDtypeStruct((2 * (tokens - rest * count), features), bf16)]
    out_shape += [jax.ShapeDtypeStruct((1, features), f32)]
    out_specs += [anywhere] * (rest + 1) + [inside]
    scratch += [pltpu.VMEM((2 * tokens, features), bf16)]
    return pl.pallas_call(
        functools.partial(experts_kernel, pieces, routed + -routed % LANES),
        out_shape=out_shape,
        in_specs=[pl.BlockSpec(memory_space=pltpu.SMEM), inside, inside]
        + [anywhere] * (2 * pieces + 2),
        out_specs=out_specs,
        scratch_shapes=scratch,
        compiler_params=pltpu.CompilerParams(vmem_limit_bytes=VMEM),
        cost_estimate=pl.CostEstimate(
            flops=2 * tokens * features * units * (12 if terms_too else 6),
            bytes_accessed=2 * (into.size + down.size + 4 * tokens * features),
            transcendentals=0,
        ),
    )(expert, meta, vector, *rows, *grads, into, down)


def weight_grad_kernel(unit_counts, row_counts, parts, adds, *refs):
    some, pieces = len(unit_counts), len(unit_counts) + len(row_counts)
    units, rows = refs[:some], refs[some:pieces]
    before, refs = refs[pieces : pieces + adds * len(parts)], refs[pieces + adds * len(parts) :]
    outs, (held, tiles, held_sem, tile_sem) = refs[: len(parts)], refs[len(parts) :]
    width = tiles.shape[-1]
    step = pl.program_id(0)
    slot = lax.rem(step, 2)
    used = pl.ds(0, held.shape[1])
    unit_places, row_places = (
        [pl.ds(sum(counts[:n]), count) for n, count in enumerate(counts)]
        for counts in (unit_counts, row_counts)
    )

    def held_copies():
        return [
            pltpu.make_async_copy(units[n].at[:, used], held.at[at, :], held_sem.at[n])
            for n, at in enumerate(unit_places)
        ]

    def tile_copies(index, into):
        columns = pl.ds(pl.multiple_of(index * width, width), width)
        return [
            pltpu.make_async_copy(
                rows[n].at[:, columns], tiles.at[into, at, :], tile_sem.at[into, n]
            )
            for n, at in enumerate(row_places)
        ]

    @pl.when(step == 0)
    def _():
        for copy in held_copies() + tile_copies(0, 0):
            copy.start()
        for copy in held_copies():
            copy.wait()

    for copy in tile_copies(step, slot):
        copy.wait()

    @pl.when(step + 1 < pl.num_programs(0))
    def _():
        for copy in tile_copies(step + 1, 1 - slot):
            copy.start()

    for n, (low, size) in enumerate(parts):
        value = dot(held[:, low : low + size], tiles[slot], ((0,), (0,)))
        outs[n][...] = before[n][...] + value if adds else value.astype(outs[n].dtype)


def weight_grad(units, rows, sizes, before=()):
    unit_counts = [piece.shape[0] for piece in units]
    row_counts = [piece.shape[0] for piece in rows]
    pieces, tokens = len(units) + len(rows), sum(row_counts)
    features = rows[0].shape[1]
    parts, used = [], 0
    for size in sizes:
        parts.append((used, size))
        used += size + -size % LANES
    adds = int(bool(before))
    anywhere = pl.BlockSpec(memory_space=pl.ANY)
    blocks = [pl.BlockSpec((size, TILE), lambda i: (0, i)) for size in sizes]
    return pl.pallas_call(
        functools.partial(weight_grad_kernel, unit_counts, row_counts, parts, adds),
        grid=(features // TILE,),
        out_shape=[
            jax.ShapeDtypeStruct((size, features), bf16 if n else f32)
            for n, size in enumerate(sizes)
        ],
        in_specs=[anywhere] * pieces + blocks * adds,
        out_specs=blocks,
        scratch_shapes=[
            pltpu.VMEM((tokens, used), bf16),
            pltpu.VMEM((2, tokens, TILE), bf16),
            pltpu.SemaphoreType.DMA((len(units),)),
            pltpu.SemaphoreType.DMA((2, len(rows))),
        ],
        input_output_aliases={pieces + n: n for n in range(len(sizes))} if adds else {},
        compiler_params=pltpu.CompilerParams(vmem_limit_bytes=VMEM),
        cost_estimate=pl.CostEstimate(
            flops=4 * tokens * features * sum(sizes),
            bytes_accessed=tokens * (features + used) * 2
            + features * sum(sizes) * 4 * (1 + adds),
            transcendentals=0,
        ),
    )(*units, *rows, *before)


def local(
    layer_input,
    lengths,
    routes,
    route_weight,
    cotangent,
    norm_gain,
    w_qkv,
    b_qkv,
    w_out,
    post_gain,
    w_gate,
    w_up,
    w_down,
    shared_gate,
    shared_up,
    shared_down,
    shared_vector,
):
    grid = Grid()
    row_count, feature_count = layer_input.shape
    groups, owners, chips, na, nb = grid.groups, grid.owners, grid.chips, grid.na, grid.nb
    devices = groups * owners
    heads_here = HEADS // chips
    width = heads_here * HEAD_DIM
    own_rows = w_qkv.shape[0]
    sizes = (w_gate.shape[2], shared_gate.shape[1])
    positions = jnp.arange(row_count, dtype=jnp.int32)
    slots = range(na)
    two = groups == 2

    class Rounds:
        def __init__(self, block):
            self.far, self.blocks = [block], []

        def row(self):
            if len(self.blocks) < na:
                self.blocks.append(grid.row(self.far[len(self.blocks)]))

        def line(self):
            if len(self.far) < na:
                self.far.append(grid.hop(self.far[-1], da=1))

        def all(self):
            return [block for blocks in self.blocks for block in blocks]

    class RowRounds(Rounds):
        def row(self):
            if len(self.blocks) < len(self.far):
                blocks = grid.row(self.far[len(self.blocks)])
                self.blocks.append(jnp.concatenate(blocks, axis=0))

        def rest(self):
            left = self.far[len(self.blocks) :]
            if left:
                blocks = grid.row(jnp.concatenate(left, axis=0))
                for n in range(len(left)):
                    part = slice(n * row_count, (n + 1) * row_count)
                    self.blocks.append(jnp.concatenate([b[part] for b in blocks], axis=0))

    class PairRounds:
        def __init__(self, block):
            self.far, self.blocks = [], [jnp.concatenate(grid.row(block), axis=0)]

        def line(self):
            if len(self.blocks) < na:
                self.blocks.append(grid.hop(self.blocks[-1], da=1))

    def tie_rounds(rounds, *values):
        state = [(r.far, r.blocks) for r in rounds]
        state, *values = tie(state, *values)
        for r, (far, blocks) in zip(rounds, state):
            r.far, r.blocks = far, blocks
        return values

    def place_of(da, db, dc, dg):
        group = (grid.group - dg) % groups
        chip = (grid.a - da) % na * nb + (grid.b - db) % nb
        return (group * chips + chip) * CORES + (grid.core + dc) % CORES

    def with_other(rows):
        return [rows, grid.hop(rows, dc=1)]

    small = jnp.concatenate([norm_gain, post_gain, shared_vector, b_qkv]).astype(f32)
    small_count = small.shape[0]
    small = jnp.pad(small, (0, -small_count % row_count))
    meta = jnp.concatenate(
        [
            routes.T.astype(f32),
            route_weight.T.astype(f32),
            jnp.broadcast_to(lengths.astype(f32)[:, None], (1, row_count)),
            small.reshape(-1, row_count),
        ],
        axis=0,
    )
    meta_rows = meta.shape[0]

    x_rounds = Rounds(layer_input)
    x_rounds.line()
    x_rounds.row()
    sliced = jnp.transpose(w_qkv.reshape(own_rows, 3, chips, width), (2, 0, 1, 3))
    sliced = sliced.reshape(chips, own_rows, 3 * width)
    extra = jnp.pad(meta.astype(bf16).reshape(-1), (0, EXTRA * 3 * width - meta.size))
    extra = jnp.broadcast_to(extra.reshape(1, EXTRA, 3 * width), (chips, EXTRA, 3 * width))
    sliced = jnp.concatenate([sliced, extra], axis=1)
    out_rounds = RowRounds(w_out)
    out_rounds.line()
    into_in = [w_gate, shared_gate, w_up, shared_up]
    down_in = [w_down, shared_down]
    out_far = []

    def out_cross():
        if len(out_far) < len(out_rounds.blocks):
            pair = out_rounds.blocks[len(out_far)]
            out_far.append([grid.cross(pair, shift) for shift in range(1, groups)])

    def tie_out(rounds, *values):
        nonlocal out_far
        out_far, *values = tie_rounds([out_rounds] + rounds, out_far, *values)
        return values

    into_in, sliced = tie_out([x_rounds], into_in, sliced)
    x_rounds.line()
    x_rounds.row()
    by_chip = grid.swap(sliced)
    out_rounds.row()
    into_rows = pack(
        [into_in[0][0].T, into_in[1].T, into_in[2][0].T, into_in[3].T], LANES
    )
    by_chip, into_rows, down_in = tie_out([x_rounds], by_chip, into_rows, down_in)
    part_rows = own_rows + EXTRA
    by_chip = by_chip.reshape(chips * part_rows, 3 * width)
    x_rounds.line()
    x_rounds.row()
    out_rounds.line()
    out_rounds.row()
    by_group = [by_chip] + [grid.cross(by_chip, shift) for shift in range(1, groups)]
    down_rows = pack([down_in[0][0], down_in[1]], LANES)
    by_group, down_rows, cotangent = tie_out([x_rounds], by_group, down_rows, cotangent)
    weight_pieces, order = [], []
    for shift, piece in enumerate(by_group):
        for core in range(CORES):
            weight_pieces.append(grid.hop(piece, dc=1) if core else piece)
            for chip in range(chips):
                order.append(
                    ((grid.group - shift) % groups * chips + chip) * CORES
                    + (grid.core + core) % CORES
                )
    used = -(-meta.size // (3 * width))
    meta_all = jnp.stack(
        [
            piece.reshape(chips, part_rows, 3 * width)[:, own_rows : own_rows + used]
            for piece in weight_pieces
        ]
    ).reshape(devices, -1)
    meta_all = meta_all[:, : meta.size].astype(f32).reshape(devices, meta_rows, row_count)

    def told_by(dg, chip, dc):
        return (dg * CORES + dc) * chips + chip

    by_place = jnp.stack(
        [
            told_by((grid.group - g) % groups, jnp.int32(chip), (grid.core - c) % CORES)
            for g in range(groups)
            for chip in range(chips)
            for c in range(CORES)
        ]
    )
    small_all = jnp.take(meta_all[:, 2 * TOP + 1 :], by_place, axis=0).reshape(devices, -1)
    own_features = norm_gain.shape[0]
    gains_in = small_all[:, :own_features].reshape(-1)
    gains_post = small_all[:, own_features : 2 * own_features].reshape(-1)
    gate_vector = small_all[:, 2 * own_features : 3 * own_features].reshape(-1)
    qkv_bias = small_all[:, 3 * own_features : small_count].reshape(3, chips, width)
    bias_here = lax.dynamic_index_in_dim(qkv_bias, grid.chip, 1, keepdims=False).reshape(-1)
    offsets = [
        told_by(dg, (grid.a - da) % na * nb + (grid.b - db) % nb, dc)
        for dg in range(groups)
        for da in slots
        for dc in range(CORES)
        for db in range(nb)
    ]
    told = jnp.take(meta_all[:, : 2 * TOP + 1], jnp.stack(offsets), axis=0)
    told = told.reshape(groups, na, CORES, nb, 2 * TOP + 1, row_count)
    plane_lengths = told[0, :, 0, :, 2 * TOP, 0].reshape(chips).astype(jnp.int32)
    here = jnp.concatenate([jnp.stack([grid.a, grid.b]).astype(jnp.int32), plane_lengths])
    valid_rows = positions < lengths[0]
    grad_rows = jnp.where(valid_rows[:, None], cotangent, jnp.zeros_like(cotangent))
    grad_rounds = RowRounds(grad_rows)
    while len(x_rounds.blocks) < na:
        x_rounds.row()
    out_rounds.line()
    out_rounds.row()
    out_cross()
    x_blocks, weight_pieces, bias_here, gains_in, here = tie_out(
        [grad_rounds], x_rounds.all(), weight_pieces, bias_here, gains_in, here
    )

    inputs = layer_input.astype(f32)
    out_rounds.row()
    out_cross()
    out_cross()
    grad_rounds.line()
    grad_rounds.row()
    normed_first, heads_weight, raw = project(
        x_blocks, gains_in[None], weight_pieces, own_rows, part_rows,
        jnp.stack(order).astype(jnp.int32),
    )
    low, sent = attention(here, raw, bias_here[None], row_count, nb, heads_here)
    low, sent = tie_out([], low, sent)

    while len(out_far) < na:
        out_cross()
    grad_rounds.line()
    pieces, order = [], []
    for dc in range(CORES):
        for da in slots:
            for dg in range(groups):
                pair = out_far[da][dg - 1] if dg else out_rounds.blocks[da]
                pieces.append(grid.hop(pair, dc=1) if dc else pair)
                order += [place_of(da, db, dc, dg) for db in range(nb)]
    out_weight = pack(pieces, size=own_rows, order=jnp.stack(order).astype(jnp.int32))
    arrived = grid.swap(sent.reshape(chips, row_count, width))
    arrived, out_weight = tie(arrived, out_weight)

    far_grads, far_rows, flying = [], [], []
    crossings = [(what, s) for s in slots for what in ("grads", "rows")]

    def cross_step():
        if crossings and two:
            what, s = crossings[0]
            source, goes = (
                (grad_rounds, far_grads) if what == "grads" else (second_rounds, far_rows)
            )
            if s < len(source.blocks):
                crossings.pop(0)
                flying.append((goes, grid.cross(source.blocks[s], 1)))

    grad_rounds.line()
    grad_rounds.row()
    cross_step()
    context = jnp.transpose(arrived, (1, 0, 2)).reshape(row_count, feature_count)
    residual = inputs + dot(context, out_weight, ((1,), (0,)))
    unit_second, factor_second = unit_norm(residual)
    normed_second = (unit_second * gains_post).astype(bf16)

    expert = (lax.axis_index("ep") // HALVES).astype(jnp.int32)
    expert, far_expert = (jnp.stack([expert, jnp.int32(n)]) for n in (1, 0))
    vector_row = gate_vector[None]
    told = jnp.swapaxes(told[..., : 2 * TOP, :], 2, 3)
    second_rounds = PairRounds(normed_second)
    own = {"rows": [], "grads": [], "middle": [], "gate": [], "up": [], "vector": []}

    def work(s):
        own["rows"].append(with_other(second_rounds.blocks[s]))
        own["grads"].append(with_other(grad_rounds.blocks[s]))
        middle, gate, up, *terms, vector = experts(
            expert, told[0, s], vector_row, own["rows"][s], own["grads"][s],
            into_rows, down_rows, sizes[0], True,
        )
        for name, value in (("middle", middle), ("gate", gate), ("up", up), ("vector", vector)):
            own[name].append(value)
        return terms

    def add_cores(terms):
        arriving = grid.hop(terms[-1], dc=1)
        return [
            (
                terms[t].astype(f32)
                + arriving[2 * t * row_count : 2 * (t + 1) * row_count].astype(f32)
            ).astype(bf16)
            for t in range(nb)
        ]

    def step_tie(*values):
        nonlocal own, into_rows, down_rows, flying
        arrivals = [rows for _, rows in flying]
        own, arrivals, into_rows, down_rows, *values = tie_rounds(
            [grad_rounds, second_rounds], own, arrivals, into_rows, down_rows, *values
        )
        for (goes, _), rows in zip(flying, arrivals):
            goes.append(rows)
        flying = []
        return values

    def line_sum(rowed, sums, s):
        total = rowed[s] if sums is None else rowed[s] + sums.astype(f32)
        return grid.hop(total.astype(bf16), da=1) if s else total

    def far_work(shift, s):
        rows, grads = with_other(far_rows[s]), with_other(far_grads[s])
        units = experts(
            far_expert, told[shift, s], vector_row, rows, grads,
            into_rows, down_rows, sizes[0], False,
        )
        return rows, grads, units[:3]

    def flat(lists):
        return [block for blocks in lists for block in blocks]

    rowed, terms, far = {}, {}, []
    sums = None
    for s in slots:
        second_rounds.line()
        cross_step()
        if s:
            grad_rounds.rest()
        if s >= 2:
            rowed[s - 1] = grid.row_sum(add_cores(terms[s - 1]))
        if s >= 3:
            sums = line_sum(rowed, sums, s - 2)
        terms[s] = work(s)
        rowed, terms, sums = step_tie(rowed, terms, sums)
    cross_step()
    rowed[na - 1] = grid.row_sum(add_cores(terms[na - 1]))
    if na > 2:
        sums = line_sum(rowed, sums, na - 2)
    own_gate = weight_grad(own["gate"], flat(own["rows"]), sizes)
    rowed, terms, sums, own_gate = step_tie(rowed, terms, sums, own_gate)
    cross_step()
    sums = line_sum(rowed, sums, na - 1)
    rowed[0] = grid.row_sum(add_cores(terms[0]))
    own_up = weight_grad(own["up"], flat(own["rows"]), sizes)
    own_down = weight_grad(own["middle"], flat(own["grads"]), sizes)
    rowed, sums, own_up, own_down = step_tie(rowed, sums, own_up, own_down)

    both_sums = line_sum(rowed, sums, 0)
    second_grad = both_sums[:row_count]
    outs = residual + both_sums[row_count:]
    output = jnp.where(valid_rows[:, None], outs, 0.0).astype(bf16)
    grad_float = grad_rows.astype(f32)
    post_gain_grad = jnp.sum(second_grad * unit_second, axis=0)
    residual_grad = grad_float + norm_backward(
        second_grad, unit_second, factor_second, gains_post
    )
    attended_grad = residual_grad.astype(bf16)
    context_grad = dot(attended_grad, out_weight, ((1,), (1,))).astype(bf16)
    sent = jnp.transpose(context_grad.reshape(row_count, chips, width), (1, 0, 2))
    arrived = grid.swap(sent)
    cross_step()
    if two:
        far.append(far_work(1, 0))
    totals = [[own_gate[0], own_up[0], own_down[0]]]
    shared = [part[1] for part in (own_gate, own_up, own_down)]
    arrived, attended_grad, far, shared, totals = step_tie(
        arrived, attended_grad, far, shared, totals
    )

    def own_features_of(values, core, group):
        parts = values.reshape(row_count, groups, chips, CORES, own_rows)
        parts = lax.dynamic_index_in_dim(parts, core, 3, keepdims=False)
        parts = lax.dynamic_index_in_dim(parts, group, 1, keepdims=False)
        return parts.reshape(row_count, chips * own_rows)

    projected_grad, bias_here_grad = attention_grad(
        here, low, arrived.reshape(-1, width), row_count, nb, heads_here
    )
    first_terms = dot(projected_grad, heads_weight, ((1,), (1,))).astype(bf16)
    out_parts = []
    for shift in range(groups):
        group = (grid.group + shift) % groups
        mine, other = (
            dot(own_features_of(context, core, group), attended_grad, ((0,), (0,))).astype(bf16)
            for core in (grid.core, 1 - grid.core)
        )
        total = mine.astype(f32) + grid.hop(other, dc=1).astype(f32)
        out_parts.append(total.astype(bf16))
    while crossings and two:
        cross_step()
    shared_far = [
        [grid.cross(part, shift) for shift in range(1, groups)] for part in shared[:1]
    ]
    first_terms, projected_grad, out_parts, far, shared_far = step_tie(
        first_terms, projected_grad, out_parts, far, shared_far
    )

    def in_order(*parts):
        parts = [part.astype(f32) for part in parts]
        if two:
            return parts[0] + parts[1]
        total = 0.0
        for group in range(groups):
            far_by = (grid.group - group) % groups
            total = total + sum(
                jnp.where(far_by == shift, part, 0.0) for shift, part in enumerate(parts)
            )
        return total

    slot_first = first_terms.reshape(na, nb * row_count, feature_count)

    def end_tie(*values):
        nonlocal far, into_rows, down_rows
        far, into_rows, down_rows, *values = tie(far, into_rows, down_rows, *values)
        return values

    def far_grad(units, place):
        before = [totals[0][units]] if two else ()
        return weight_grad(
            [work[2][(1, 2, 0)[units]] for work in far], flat(work[place] for work in far),
            sizes[:1], before,
        )[0]

    qkv_grad = dot(normed_first, projected_grad, ((0,), (0,))).astype(bf16)
    half = chips * own_rows // 2
    first_sums = line_sum(slot_first, None, 1) if na > 1 else None
    crossed = [[grid.cross(part[:half], n + 1)] for n, part in enumerate(out_parts[1:])]
    if two:
        far.append(far_work(1, 1))
    slot_first, qkv_grad, crossed, out_parts, first_sums = end_tie(
        slot_first, qkv_grad, crossed, out_parts, first_sums
    )
    if na > 2:
        first_sums = line_sum(slot_first, first_sums, 2)
    for n, part in enumerate(out_parts[1:]):
        crossed[n].append(grid.cross(part[half:], n + 1))
    qkv_grad = grid.scatter_core(qkv_grad.reshape(groups, chips, CORES, own_rows, 3 * width), 2)
    if two:
        far.append(far_work(1, 2 % na))
    slot_first, qkv_grad, crossed, out_parts, first_sums, shared = end_tie(
        slot_first, qkv_grad.astype(bf16), crossed, out_parts, first_sums, shared
    )
    for s in range(3, na):
        first_sums = line_sum(slot_first, first_sums, s)
    qkv_grad = grid.scatter_groups(qkv_grad).astype(bf16)
    out_total = out_parts[0].astype(f32)
    for halves in crossed:
        out_total = out_total + jnp.concatenate(halves, axis=0).astype(f32)
    out_rowed = grid.scatter_row(
        out_total.astype(bf16).reshape(na, nb, own_rows, feature_count)
    )
    shared_far.append([grid.cross(shared[1], shift) for shift in range(1, groups)])
    if two:
        if na > 3:
            far.append(far_work(1, 3))
        slot_first, first_sums, qkv_grad, out_rowed, shared = end_tie(
            slot_first, first_sums, qkv_grad, out_rowed, shared
        )
    first_terms_here = slot_first[0] if first_sums is None else line_sum(slot_first, first_sums, 0)
    first_grad = grid.row_sum(
        first_terms_here.astype(bf16).reshape(nb, row_count, feature_count)
    )
    qkv_grad = grid.swap(qkv_grad).reshape(chips, own_rows, 3, width)
    if two:
        gate_total = far_grad(0, 0)
        gate_total, first_grad, shared_far, shared, qkv_grad, out_rowed = end_tie(
            gate_total, first_grad, shared_far, shared, qkv_grad, out_rowed
        )
    out_weight_grad = grid.scatter_line(out_rowed)
    shared_far.append([grid.cross(shared[2], shift) for shift in range(1, groups)])
    unit_first, factor_first = unit_norm(inputs)
    input_part = norm_backward(first_grad, unit_first, factor_first, gains_in)
    layer_grad = (residual_grad + input_part).astype(bf16)
    qkv_weight_grad = jnp.transpose(qkv_grad, (1, 2, 0, 3)).reshape(own_rows, -1).astype(f32)
    if two:
        gate_grad, up_grad, down_grad = gate_total, far_grad(1, 0), far_grad(2, 1)
    else:
        second_blocks, grad_blocks = second_rounds.blocks, grad_rounds.blocks
        for shift in range(1, groups):
            totals, second_blocks, grad_blocks = tie(totals, second_blocks, grad_blocks)
            far_grads, far_rows = (
                [grid.cross(rows, shift) for rows in source]
                for source in (grad_blocks, second_blocks)
            )
            far = [far_work(shift, s) for s in slots]
            totals.append([far_grad(0, 0), far_grad(1, 0), far_grad(2, 1)])
        gate_grad, up_grad, down_grad = (in_order(*parts) for parts in zip(*totals))
    shared_gate_grad, shared_up_grad, shared_down_grad = (
        in_order(here_part, *parts) for here_part, parts in zip(shared, shared_far)
    )

    vector_grad = sum(own["vector"])[0]
    gain_grad = jnp.sum(first_terms.astype(f32) * normed_first.astype(f32), axis=0) / gains_in
    bias_grad = jnp.zeros((3, chips, width), f32)
    bias_grad = lax.dynamic_update_slice(
        bias_grad, bias_here_grad.reshape(3, 1, width), (0, grid.chip, 0)
    )
    vectors = jnp.concatenate(
        [
            gain_grad.reshape(devices, -1),
            post_gain_grad.reshape(devices, -1),
            vector_grad.reshape(devices, -1),
            bias_grad.reshape(devices, -1),
        ],
        axis=1,
    ).reshape(groups, na, nb, CORES, -1)
    vectors = grid.scatter_core(vectors, 3)
    vectors = grid.scatter_groups(vectors)
    vectors = grid.scatter_line(grid.scatter_row(vectors))
    return (
        output,
        layer_grad,
        vectors[:own_features],
        qkv_weight_grad,
        vectors[3 * own_features :],
        out_weight_grad,
        vectors[own_features : 2 * own_features],
        gate_grad.T[None],
        up_grad.T[None],
        down_grad[None],
        shared_gate_grad.T,
        shared_up_grad.T,
        shared_down_grad,
        vectors[2 * own_features : 3 * own_features],
    )


def solution(mesh):
    rows = P(("dp", "ep"), None)
    split = P(("dp", "ep"))
    parts = P("ep", None, None)
    return jax.shard_map(
        local,
        mesh=mesh,
        in_specs=(
            rows,
            split,
            rows,
            rows,
            rows,
            split,
            rows,
            split,
            rows,
            split,
            parts,
            parts,
            parts,
            P(None, "ep"),
            P(None, "ep"),
            P("ep", None),
            split,
        ),
        out_specs=(
            rows,
            rows,
            split,
            rows,
            split,
            rows,
            split,
            parts,
            parts,
            parts,
            P(None, "ep"),
            P(None, "ep"),
            P("ep", None),
            split,
        ),
        check_vma=False,
    )
```

```python
import functools
import math

import jax
import jax.numpy as jnp
from jax import lax
from jax.experimental import pallas as pl
from jax.experimental.pallas import tpu as pltpu
from jax.sharding import PartitionSpec as P

HEADS = 16
HEAD_DIM = 128
TOP = 4
HALVES = 2
CORES = 2
LINE = 4
LANES = 128
TILE = 512
VMEM = 56 << 20
EXTRA = 16


epsilon = 1e-06
rope_base = 1000000.0
bf16 = jnp.bfloat16
f32 = jnp.float32


def unit_norm(values):
    factor = lax.rsqrt(jnp.mean(values * values, axis=-1, keepdims=True) + epsilon)
    return (values * factor, factor)


def norm_backward(incoming, unit_rows, factor, gain_row):
    scaled = incoming * gain_row
    inner_mean = jnp.mean(scaled * unit_rows, axis=-1, keepdims=True)
    return factor * (scaled - unit_rows * inner_mean)


def rope_tables(row_count, head_size):
    inverse = rope_base ** (-jnp.arange(0, head_size, 2, dtype=f32) / head_size)
    angles = jnp.arange(row_count, dtype=f32)[:, None] * inverse[None, :]
    angles = jnp.concatenate([angles, angles], axis=-1)
    return (jnp.cos(angles)[:, None, :], jnp.sin(angles)[:, None, :])


def dot(left, right, dims):
    return lax.dot_general(left, right, (dims, ((), ())), preferred_element_type=f32)


def tie(*values):
    return lax.optimization_barrier(values)


class Grid:
    def __init__(self):
        self.groups = lax.axis_size("dp")
        self.owners = lax.axis_size("ep")
        self.chips = self.owners // CORES
        self.na = math.gcd(LINE, self.chips)
        self.nb = self.chips // self.na
        self.group = lax.axis_index("dp")
        me = lax.axis_index("ep")
        self.chip = me // CORES
        self.core = me % CORES
        self.a = self.chip // self.nb
        self.b = self.chip % self.nb

    def place(self, a, b, c):
        return ((a % self.na) * self.nb + b % self.nb) * CORES + c % CORES

    def hop(self, values, da=0, db=0, dc=0):
        pairs = [
            (self.place(a, b, c), self.place(a + da, b + db, c + dc))
            for a in range(self.na)
            for b in range(self.nb)
            for c in range(CORES)
        ]
        return lax.ppermute(values, "ep", pairs)

    def cross(self, values, shift):
        pairs = [(g, (g + shift) % self.groups) for g in range(self.groups)]
        return lax.ppermute(values, "dp", pairs)

    def row(self, block):
        return [block] + [self.hop(block, db=db) for db in range(1, self.nb)]

    def row_sum(self, terms):
        total = terms[0].astype(f32)
        for db in range(1, self.nb):
            total = total + self.hop(terms[db], db=-db).astype(f32)
        return total

    def core_sum(self, terms):
        return (terms[0].astype(f32) + self.hop(terms[1], dc=1).astype(f32)).astype(bf16)

    def same_core(self):
        return [[k * CORES + c for k in range(self.chips)] for c in range(CORES)]

    def swap(self, blocks):
        return lax.all_to_all(
            blocks,
            "ep",
            split_axis=0,
            concat_axis=0,
            tiled=True,
            axis_index_groups=self.same_core(),
        )

    def scatter_core(self, terms, axis):
        mine = lax.dynamic_index_in_dim(terms, self.core, axis, keepdims=False)
        other = lax.dynamic_index_in_dim(terms, 1 - self.core, axis, keepdims=False)
        return mine.astype(f32) + self.hop(other, dc=1).astype(f32)

    def scatter_groups(self, terms):
        total = lax.dynamic_index_in_dim(terms, self.group, 0, keepdims=False).astype(f32)
        for shift in range(1, self.groups):
            there = (self.group + shift) % self.groups
            piece = lax.dynamic_index_in_dim(terms, there, 0, keepdims=False)
            total = total + self.cross(piece, shift).astype(f32)
        return total

    def scatter_row(self, terms):
        total = lax.dynamic_index_in_dim(terms, self.b, 1, keepdims=False).astype(f32)
        for db in range(1, self.nb):
            there = (self.b + db) % self.nb
            piece = lax.dynamic_index_in_dim(terms, there, 1, keepdims=False)
            total = total + self.hop(piece, db=db).astype(f32)
        return total.astype(terms.dtype)

    def scatter_line(self, terms):
        total = lax.dynamic_index_in_dim(terms, self.a, 0, keepdims=False).astype(f32)
        for da in range(1, self.na):
            there = (self.a + da) % self.na
            piece = lax.dynamic_index_in_dim(terms, there, 0, keepdims=False)
            total = total + self.hop(piece, da=da).astype(f32)
        return total


def turned_lanes(values):
    return pltpu.roll(values, HEAD_DIM // 2, 1)


def head_probabilities(query, key, length):
    scores = dot(query, key, ((1,), (1,))) / math.sqrt(HEAD_DIM)
    query_place = lax.broadcasted_iota(jnp.int32, scores.shape, 0)
    key_place = lax.broadcasted_iota(jnp.int32, scores.shape, 1)
    allowed = (key_place <= query_place) & (key_place < length)
    scores = jnp.where(allowed, scores, -1e30)
    exponent = jnp.exp(scores - jnp.max(scores, axis=1, keepdims=True))
    return exponent / jnp.sum(exponent, axis=1, keepdims=True)


def home_rows(here, sequence, sequences, rows):
    return pl.ds(pl.multiple_of(lax.rem(here[1] - sequence + sequences, sequences) * rows, rows), rows)


def attention_kernel(sequences, heads, here, raw, bias, cosine, signed_sine, low, context):
    rows = cosine.shape[0]
    width = heads * HEAD_DIM
    for sequence in range(sequences):
        at = slice(sequence * rows, (sequence + 1) * rows)
        home = home_rows(here, sequence, sequences, rows)
        length = here[2 + pl.program_id(0) * sequences + sequence]
        for head in range(heads):
            parts = []
            for part in range(3):
                low_lane = part * width + head * HEAD_DIM
                lanes = slice(low_lane, low_lane + HEAD_DIM)
                values = raw[at, lanes] + bias[:, lanes]
                if part < 2:
                    values = values * cosine[...] + turned_lanes(values) * signed_sine[...]
                values = values.astype(bf16)
                low[at, lanes] = values
                parts.append(values)
            probabilities = head_probabilities(parts[0], parts[1], length).astype(bf16)
            lanes = slice(head * HEAD_DIM, (head + 1) * HEAD_DIM)
            context[home, lanes] = dot(probabilities, parts[2], ((1,), (0,))).astype(bf16)


def attention_grad_kernel(
    sequences, heads, here, low, incoming, cosine, sine, sign, outgoing, bias_grad
):
    rows = cosine.shape[0]
    width = heads * HEAD_DIM
    root_size = math.sqrt(HEAD_DIM)

    @pl.when(pl.program_id(0) == 0)
    def _():
        bias_grad[...] = jnp.zeros_like(bias_grad)

    for sequence in range(sequences):
        at = slice(sequence * rows, (sequence + 1) * rows)
        home = home_rows(here, sequence, sequences, rows)
        length = here[2 + pl.program_id(0) * sequences + sequence]
        for head in range(heads):
            lanes = [
                slice(part * width + head * HEAD_DIM, part * width + (head + 1) * HEAD_DIM)
                for part in range(3)
            ]
            query, key, value = (low[at, part] for part in lanes)
            grad = incoming[home, lanes[0]]
            probabilities = head_probabilities(query, key, length)
            probs_grad = dot(grad, value, ((1,), (1,)))
            inner = jnp.sum(probabilities * probs_grad, axis=1, keepdims=True)
            score_grad = (probabilities * (probs_grad - inner)).astype(bf16)
            grads = [
                dot(score_grad, key, ((1,), (0,))) / root_size,
                dot(score_grad, query, ((0,), (0,))) / root_size,
                dot(probabilities.astype(bf16), grad, ((0,), (0,))),
            ]
            for part in range(3):
                values = grads[part]
                if part < 2:
                    values = values * cosine[...] - turned_lanes(values * sine[...]) * sign[...]
                values = values.astype(bf16)
                outgoing[at, lanes[part]] = values
                bias_grad[:, lanes[part]] += jnp.sum(values.astype(f32), axis=0, keepdims=True)


def rope_inputs(row_count):
    cosine, sine = (table[:, 0] for table in rope_tables(row_count, HEAD_DIM))
    sign = jnp.where(jnp.arange(HEAD_DIM) < HEAD_DIM // 2, -1.0, 1.0).astype(f32)[None]
    return cosine, sine, sign


def attention(here, raw, bias, rows, sequences, heads):
    tokens, width = raw.shape[0], heads * HEAD_DIM
    cosine, sine, sign = rope_inputs(rows)
    block = sequences * rows
    lines = tokens // block
    whole = lambda *shape: pl.BlockSpec(shape, lambda i, here: (0, 0))
    return pl.pallas_call(
        functools.partial(attention_kernel, sequences, heads),
        out_shape=[
            jax.ShapeDtypeStruct((tokens, 3 * width), bf16),
            jax.ShapeDtypeStruct((tokens, width), bf16),
        ],
        grid_spec=pltpu.PrefetchScalarGridSpec(
            num_scalar_prefetch=1,
            grid=(lines,),
            in_specs=[
                pl.BlockSpec((block, 3 * width), lambda i, here: (i, 0)),
                whole(1, 3 * width),
                whole(rows, HEAD_DIM),
                whole(rows, HEAD_DIM),
            ],
            out_specs=[
                pl.BlockSpec((block, 3 * width), lambda i, here: (i, 0)),
                pl.BlockSpec((block, width), lambda i, here: (lax.rem(here[0] - i + lines, lines), 0)),
            ],
        ),
        cost_estimate=pl.CostEstimate(
            flops=300 * tokens * rows * width, bytes_accessed=tokens * width * 20, transcendentals=0
        ),
    )(here, raw, bias, cosine, sine * sign)


def attention_grad(here, low, incoming, rows, sequences, heads):
    tokens, width = low.shape[0], heads * HEAD_DIM
    block = sequences * rows
    lines = tokens // block
    whole = lambda *shape: pl.BlockSpec(shape, lambda i, here: (0, 0))
    return pl.pallas_call(
        functools.partial(attention_grad_kernel, sequences, heads),
        out_shape=[
            jax.ShapeDtypeStruct((tokens, 3 * width), bf16),
            jax.ShapeDtypeStruct((1, 3 * width), f32),
        ],
        grid_spec=pltpu.PrefetchScalarGridSpec(
            num_scalar_prefetch=1,
            grid=(lines,),
            in_specs=[
                pl.BlockSpec((block, 3 * width), lambda i, here: (i, 0)),
                pl.BlockSpec((block, width), lambda i, here: (lax.rem(here[0] - i + lines, lines), 0)),
                whole(rows, HEAD_DIM),
                whole(rows, HEAD_DIM),
                whole(1, HEAD_DIM),
            ],
            out_specs=[
                pl.BlockSpec((block, 3 * width), lambda i, here: (i, 0)),
                whole(1, 3 * width),
            ],
        ),
        cost_estimate=pl.CostEstimate(
            flops=370 * tokens * rows * width, bytes_accessed=tokens * width * 14, transcendentals=0
        ),
    )(here, low, incoming, *rope_inputs(rows))


def pack_kernel(count, moves, blanks, order, *refs):
    sources, out, sem = refs[:count], refs[-2], refs[-1]
    copies = []
    for n, (source, low, size, to) in enumerate(moves):
        if to < 0:
            to = pl.multiple_of(order[-1 - to] * size, size)
        copies.append(
            pltpu.make_async_copy(
                sources[source].at[pl.ds(low, size), :], out.at[pl.ds(to, size), :], sem.at[n]
            )
        )
    for copy in copies:
        copy.start()
    for at, size in blanks:
        out[at : at + size, :] = jnp.zeros((size, out.shape[1]), out.dtype)
    for copy in copies:
        copy.wait()


def pack(pieces, step=1, size=None, order=None):
    moves, blanks, at = [], [], 0
    for n, piece in enumerate(pieces):
        rows = piece.shape[0]
        if order is None:
            moves.append((n, 0, rows, at))
        else:
            moves += [(n, low, size, -1 - len(moves) - low // size) for low in range(0, rows, size)]
        at += rows
        if at % step:
            blanks.append((at, -at % step))
            at += -at % step
    if order is None:
        order = jnp.zeros((1,), jnp.int32)
    return pl.pallas_call(
        functools.partial(pack_kernel, len(pieces), moves, blanks),
        out_shape=jax.ShapeDtypeStruct((at, pieces[0].shape[1]), pieces[0].dtype),
        in_specs=[pl.BlockSpec(memory_space=pltpu.SMEM)]
        + [pl.BlockSpec(memory_space=pl.ANY)] * len(pieces),
        out_specs=pl.BlockSpec(memory_space=pltpu.VMEM),
        scratch_shapes=[pltpu.SemaphoreType.DMA((len(moves),))],
        compiler_params=pltpu.CompilerParams(vmem_limit_bytes=VMEM),
        cost_estimate=pl.CostEstimate(
            flops=0, bytes_accessed=4 * at * pieces[0].shape[1], transcendentals=0
        ),
    )(order, *pieces)


def project_kernel(counts, size, step, order, gain, *refs):
    blocks, pieces = refs[: counts[0]], refs[counts[0] : sum(counts)]
    normed_out, weight_out, raw, arrived, normed, weight, in_sem, weight_sem, out_sem = refs[
        sum(counts) :
    ]
    rows = blocks[0].shape[0]
    loads = [
        pltpu.make_async_copy(block, arrived.at[pl.ds(n * rows, rows), :], in_sem.at[n])
        for n, block in enumerate(blocks)
    ]
    parts = pieces[0].shape[0] // step
    moves = []
    for n, piece in enumerate(pieces):
        for part in range(parts):
            to = pl.multiple_of(order[n * parts + part] * size, size)
            moves.append(
                pltpu.make_async_copy(
                    piece.at[pl.ds(part * step, size), :],
                    weight.at[pl.ds(to, size), :],
                    weight_sem.at[n * parts + part],
                )
            )
    for copy in loads + moves:
        copy.start()
    stores = []
    for n, load in enumerate(loads):
        load.wait()
        at = slice(n * rows, (n + 1) * rows)
        values = arrived[at, :].astype(f32)
        mean = jnp.mean(values * values, axis=1, keepdims=True)
        normed[at, :] = (values * lax.rsqrt(mean + epsilon) * gain[...]).astype(bf16)
    stores.append(pltpu.make_async_copy(normed, normed_out, out_sem.at[0]))
    for copy in moves:
        copy.wait()
    stores.append(pltpu.make_async_copy(weight, weight_out, out_sem.at[1]))
    for copy in stores:
        copy.start()
    raw[...] = dot(normed[...], weight[...], ((1,), (0,)))
    for copy in stores:
        copy.wait()


def project(blocks, gain, pieces, size, step, order):
    tokens, features = sum(block.shape[0] for block in blocks), blocks[0].shape[1]
    weight_rows = sum(piece.shape[0] for piece in pieces) // step * size
    columns = pieces[0].shape[1]
    anywhere = pl.BlockSpec(memory_space=pl.ANY)
    inside = pl.BlockSpec(memory_space=pltpu.VMEM)
    return pl.pallas_call(
        functools.partial(project_kernel, (len(blocks), len(pieces)), size, step),
        out_shape=[
            jax.ShapeDtypeStruct((tokens, features), bf16),
            jax.ShapeDtypeStruct((weight_rows, columns), bf16),
            jax.ShapeDtypeStruct((tokens, columns), f32),
        ],
        in_specs=[pl.BlockSpec(memory_space=pltpu.SMEM), inside]
        + [anywhere] * (len(blocks) + len(pieces)),
        out_specs=[anywhere, anywhere, inside],
        scratch_shapes=[
            pltpu.VMEM((tokens, features), bf16),
            pltpu.VMEM((tokens, features), bf16),
            pltpu.VMEM((weight_rows, columns), bf16),
            pltpu.SemaphoreType.DMA((len(blocks),)),
            pltpu.SemaphoreType.DMA((weight_rows // size,)),
            pltpu.SemaphoreType.DMA((2,)),
        ],
        compiler_params=pltpu.CompilerParams(vmem_limit_bytes=VMEM),
        cost_estimate=pl.CostEstimate(
            flops=7 * tokens * features * columns,
            bytes_accessed=4 * (tokens * features + weight_rows * columns + tokens * columns),
            transcendentals=0,
        ),
    )(order, gain, *blocks, *pieces)


def experts_kernel(pieces, start, expert, meta, vector, *refs):
    row_pieces, grad_pieces = refs[:pieces], refs[pieces : 2 * pieces]
    into_hbm, down_hbm = refs[2 * pieces : 2 * pieces + 2]
    refs = refs[2 * pieces + 2 :]
    unit_outs, refs = refs[:3], refs[3:]
    rest, count = meta.shape[0], meta.shape[-1]
    blocks = rest * CORES
    term_outs, vector_grad, refs = refs[: rest + 1], refs[rest + 1], refs[rest + 2 :]
    rows, grads, into, down, middle_all, gate_all, up_all = refs[:7]
    in_sem, weight_sem, out_sem, term_sem, terms = refs[7:12]
    tokens, features = rows.shape
    units = down.shape[0]
    size = tokens // pieces
    parts = ((0, start), (start, units))

    loads = [
        [
            pltpu.make_async_copy(
                piece, held.at[pl.ds(n * size, size), :], in_sem.at[which, n]
            )
            for n, piece in enumerate(arrived)
        ]
        for which, (arrived, held) in enumerate(((row_pieces, rows), (grad_pieces, grads)))
    ]
    weights = [
        [
            pltpu.make_async_copy(
                source.at[pl.ds(first + low, high - low), :],
                held.at[pl.ds(first + low, high - low), :],
                weight_sem.at[part, which],
            )
            for which, (source, held, first) in enumerate(
                ((into_hbm, into, 0), (into_hbm, into, units), (down_hbm, down, 0))
            )
        ]
        for part, (low, high) in enumerate(parts)
    ]
    arrivals = (loads[0] + weights[0][:1], weights[0][1:2], loads[1] + weights[0][2:])
    for copy in arrivals[0] + arrivals[1] + arrivals[2]:
        copy.start()

    @pl.when(expert[1] == 1)
    def _():
        for copy in weights[1]:
            copy.start()

    here = expert[0].astype(f32)
    columns = []
    for core in range(meta.shape[1]):
        for line in range(meta.shape[0]):
            told = meta[line, core]
            scale = jnp.zeros((1, count), f32)
            for k in range(TOP):
                hit = told[k : k + 1] == here
                scale = scale + jnp.where(hit, told[TOP + k : TOP + k + 1], 0.0)
            columns.append(jnp.transpose(jnp.broadcast_to(scale, (count, count)))[:, :1])
    routed_scale = jnp.concatenate(columns, axis=0)

    def work(part, scale):
        low, high = parts[part]
        waits = arrivals if part == 0 else ((), (), ())
        for copy in waits[0]:
            copy.wait()
        gate = dot(rows[...], into[low:high, :], ((1,), (1,)))
        for copy in waits[1]:
            copy.wait()
        up = dot(rows[...], into[units + low : units + high, :], ((1,), (1,)))
        for copy in waits[2]:
            copy.wait()
        back = dot(grads[...], down[low:high, :], ((1,), (1,)))
        gate_sigmoid = jax.nn.sigmoid(gate)
        silu = gate * gate_sigmoid
        middle = silu * up
        inner = jnp.sum(middle * back, axis=1, keepdims=True) if part else None
        back = back * scale
        middle_all[:, low:high] = (middle * scale).astype(bf16)
        gate_all[:, low:high] = (back * up * (gate_sigmoid + silu * (1.0 - gate_sigmoid))).astype(
            bf16
        )
        up_all[:, low:high] = (back * silu).astype(bf16)
        lanes = pl.ds(low, high - low)
        copies = [
            pltpu.make_async_copy(held.at[:, lanes], out.at[:, lanes], out_sem.at[part, which])
            for which, (held, out) in enumerate(zip((middle_all, gate_all, up_all), unit_outs))
        ]
        for copy in copies:
            copy.start()
        return inner, copies

    _, stores = work(0, routed_scale)

    @pl.when(expert[1] == 1)
    def _():
        for copy in weights[1]:
            copy.wait()
        logit = jnp.sum(rows[...].astype(f32) * vector[...], axis=1, keepdims=True)
        shared_scale = jax.nn.sigmoid(logit)
        inner, copies = work(1, shared_scale)
        logit_grad = inner * shared_scale * (1.0 - shared_scale)
        for low in range(0, features, TILE):
            lanes = slice(low, low + TILE)
            value = dot(gate_all[...], into[:units, lanes], ((1,), (0,)))
            value = value + dot(up_all[...], into[units:, lanes], ((1,), (0,)))
            value = (value + logit_grad * vector[:, lanes]).astype(bf16)
            result = dot(middle_all[...], down[:, lanes], ((1,), (0,))).astype(bf16)
            for n in range(blocks):
                at = slice(n * count, (n + 1) * count)
                terms[2 * n * count : (2 * n + 1) * count, lanes] = value[at]
                terms[(2 * n + 1) * count : (2 * n + 2) * count, lanes] = result[at]
        at = 0
        for n, out in enumerate(term_outs):
            copy = pltpu.make_async_copy(
                terms.at[pl.ds(at, out.shape[0]), :], out, term_sem.at[n]
            )
            copy.start()
            copies.append(copy)
            at += out.shape[0]
        vector_grad[...] = jnp.sum(rows[...].astype(f32) * logit_grad, axis=0, keepdims=True)
        for copy in copies:
            copy.wait()

    for copy in stores:
        copy.wait()


def experts(expert, meta, vector, rows, grads, into, down, routed, terms_too):
    pieces, features = len(rows), rows[0].shape[1]
    tokens, units = sum(piece.shape[0] for piece in rows), down.shape[0]
    rest, count = meta.shape[0], meta.shape[-1]
    anywhere = pl.BlockSpec(memory_space=pl.ANY)
    inside = pl.BlockSpec(memory_space=pltpu.VMEM)
    out_shape = [jax.ShapeDtypeStruct((tokens, units), bf16)] * 3
    out_specs = [anywhere] * 3
    scratch = [
        pltpu.VMEM((tokens, features), bf16),
        pltpu.VMEM((tokens, features), bf16),
        pltpu.VMEM(into.shape, bf16),
        pltpu.VMEM(down.shape, bf16),
        pltpu.VMEM((tokens, units), bf16),
        pltpu.VMEM((tokens, units), bf16),
        pltpu.VMEM((tokens, units), bf16),
        pltpu.SemaphoreType.DMA((2, pieces)),
        pltpu.SemaphoreType.DMA((2, 3)),
        pltpu.SemaphoreType.DMA((2, 3)),
        pltpu.SemaphoreType.DMA((rest + 1,)),
    ]
    out_shape += [jax.ShapeDtypeStruct((2 * count, features), bf16)] * rest
    out_shape += [jax.ShapeDtypeStruct((2 * (tokens - rest * count), features), bf16)]
    out_shape += [jax.ShapeDtypeStruct((1, features), f32)]
    out_specs += [anywhere] * (rest + 1) + [inside]
    scratch += [pltpu.VMEM((2 * tokens, features), bf16)]
    return pl.pallas_call(
        functools.partial(experts_kernel, pieces, routed + -routed % LANES),
        out_shape=out_shape,
        in_specs=[pl.BlockSpec(memory_space=pltpu.SMEM), inside, inside]
        + [anywhere] * (2 * pieces + 2),
        out_specs=out_specs,
        scratch_shapes=scratch,
        compiler_params=pltpu.CompilerParams(vmem_limit_bytes=VMEM),
        cost_estimate=pl.CostEstimate(
            flops=2 * tokens * features * units * (12 if terms_too else 6),
            bytes_accessed=2 * (into.size + down.size + 4 * tokens * features),
            transcendentals=0,
        ),
    )(expert, meta, vector, *rows, *grads, into, down)


def weight_grad_kernel(unit_counts, row_counts, parts, adds, *refs):
    some, pieces = len(unit_counts), len(unit_counts) + len(row_counts)
    units, rows = refs[:some], refs[some:pieces]
    before, refs = refs[pieces : pieces + adds * len(parts)], refs[pieces + adds * len(parts) :]
    outs, (held, tiles, held_sem, tile_sem) = refs[: len(parts)], refs[len(parts) :]
    width = tiles.shape[-1]
    step = pl.program_id(0)
    slot = lax.rem(step, 2)
    used = pl.ds(0, held.shape[1])
    unit_places, row_places = (
        [pl.ds(sum(counts[:n]), count) for n, count in enumerate(counts)]
        for counts in (unit_counts, row_counts)
    )

    def held_copies():
        return [
            pltpu.make_async_copy(units[n].at[:, used], held.at[at, :], held_sem.at[n])
            for n, at in enumerate(unit_places)
        ]

    def tile_copies(index, into):
        columns = pl.ds(pl.multiple_of(index * width, width), width)
        return [
            pltpu.make_async_copy(
                rows[n].at[:, columns], tiles.at[into, at, :], tile_sem.at[into, n]
            )
            for n, at in enumerate(row_places)
        ]

    @pl.when(step == 0)
    def _():
        for copy in held_copies() + tile_copies(0, 0):
            copy.start()
        for copy in held_copies():
            copy.wait()

    for copy in tile_copies(step, slot):
        copy.wait()

    @pl.when(step + 1 < pl.num_programs(0))
    def _():
        for copy in tile_copies(step + 1, 1 - slot):
            copy.start()

    for n, (low, size) in enumerate(parts):
        value = dot(held[:, low : low + size], tiles[slot], ((0,), (0,)))
        outs[n][...] = before[n][...] + value if adds else value.astype(outs[n].dtype)


def weight_grad(units, rows, sizes, before=()):
    unit_counts = [piece.shape[0] for piece in units]
    row_counts = [piece.shape[0] for piece in rows]
    pieces, tokens = len(units) + len(rows), sum(row_counts)
    features = rows[0].shape[1]
    parts, used = [], 0
    for size in sizes:
        parts.append((used, size))
        used += size + -size % LANES
    adds = int(bool(before))
    anywhere = pl.BlockSpec(memory_space=pl.ANY)
    blocks = [pl.BlockSpec((size, TILE), lambda i: (0, i)) for size in sizes]
    return pl.pallas_call(
        functools.partial(weight_grad_kernel, unit_counts, row_counts, parts, adds),
        grid=(features // TILE,),
        out_shape=[
            jax.ShapeDtypeStruct((size, features), bf16 if n else f32)
            for n, size in enumerate(sizes)
        ],
        in_specs=[anywhere] * pieces + blocks * adds,
        out_specs=blocks,
        scratch_shapes=[
            pltpu.VMEM((tokens, used), bf16),
            pltpu.VMEM((2, tokens, TILE), bf16),
            pltpu.SemaphoreType.DMA((len(units),)),
            pltpu.SemaphoreType.DMA((2, len(rows))),
        ],
        input_output_aliases={pieces + n: n for n in range(len(sizes))} if adds else {},
        compiler_params=pltpu.CompilerParams(vmem_limit_bytes=VMEM),
        cost_estimate=pl.CostEstimate(
            flops=4 * tokens * features * sum(sizes),
            bytes_accessed=tokens * (features + used) * 2
            + features * sum(sizes) * 4 * (1 + adds),
            transcendentals=0,
        ),
    )(*units, *rows, *before)


def local(
    layer_input,
    lengths,
    routes,
    route_weight,
    cotangent,
    norm_gain,
    w_qkv,
    b_qkv,
    w_out,
    post_gain,
    w_gate,
    w_up,
    w_down,
    shared_gate,
    shared_up,
    shared_down,
    shared_vector,
):
    grid = Grid()
    row_count, feature_count = layer_input.shape
    groups, owners, chips, na, nb = grid.groups, grid.owners, grid.chips, grid.na, grid.nb
    devices = groups * owners
    heads_here = HEADS // chips
    width = heads_here * HEAD_DIM
    own_rows = w_qkv.shape[0]
    sizes = (w_gate.shape[2], shared_gate.shape[1])
    positions = jnp.arange(row_count, dtype=jnp.int32)
    slots = range(na)
    two = groups == 2

    class Rounds:
        def __init__(self, block):
            self.far, self.blocks = [block], []

        def row(self):
            if len(self.blocks) < na:
                self.blocks.append(grid.row(self.far[len(self.blocks)]))

        def line(self):
            if len(self.far) < na:
                self.far.append(grid.hop(self.far[-1], da=1))

        def all(self):
            return [block for blocks in self.blocks for block in blocks]

    class RowRounds(Rounds):
        def row(self):
            if len(self.blocks) < len(self.far):
                blocks = grid.row(self.far[len(self.blocks)])
                self.blocks.append(jnp.concatenate(blocks, axis=0))

        def rest(self):
            left = self.far[len(self.blocks) :]
            if left:
                blocks = grid.row(jnp.concatenate(left, axis=0))
                for n in range(len(left)):
                    part = slice(n * row_count, (n + 1) * row_count)
                    self.blocks.append(jnp.concatenate([b[part] for b in blocks], axis=0))

    class PairRounds:
        def __init__(self, block):
            self.far, self.blocks = [], [jnp.concatenate(grid.row(block), axis=0)]

        def line(self):
            if len(self.blocks) < na:
                self.blocks.append(grid.hop(self.blocks[-1], da=1))

    def tie_rounds(rounds, *values):
        state = [(r.far, r.blocks) for r in rounds]
        state, *values = tie(state, *values)
        for r, (far, blocks) in zip(rounds, state):
            r.far, r.blocks = far, blocks
        return values

    def place_of(da, db, dc, dg):
        group = (grid.group - dg) % groups
        chip = (grid.a - da) % na * nb + (grid.b - db) % nb
        return (group * chips + chip) * CORES + (grid.core + dc) % CORES

    def with_other(rows):
        return [rows, grid.hop(rows, dc=1)]

    small = jnp.concatenate([norm_gain, post_gain, shared_vector, b_qkv]).astype(f32)
    small_count = small.shape[0]
    small = jnp.pad(small, (0, -small_count % row_count))
    meta = jnp.concatenate(
        [
            routes.T.astype(f32),
            route_weight.T.astype(f32),
            jnp.broadcast_to(lengths.astype(f32)[:, None], (1, row_count)),
            small.reshape(-1, row_count),
        ],
        axis=0,
    )
    meta_rows = meta.shape[0]

    x_rounds = Rounds(layer_input)
    x_rounds.line()
    x_rounds.row()
    sliced = jnp.transpose(w_qkv.reshape(own_rows, 3, chips, width), (2, 0, 1, 3))
    sliced = sliced.reshape(chips, own_rows, 3 * width)
    extra = jnp.pad(meta.astype(bf16).reshape(-1), (0, EXTRA * 3 * width - meta.size))
    extra = jnp.broadcast_to(extra.reshape(1, EXTRA, 3 * width), (chips, EXTRA, 3 * width))
    sliced = jnp.concatenate([sliced, extra], axis=1)
    out_rounds = RowRounds(w_out)
    out_rounds.line()
    into_in = [w_gate, shared_gate, w_up, shared_up]
    down_in = [w_down, shared_down]
    out_far = []

    def out_cross():
        if len(out_far) < len(out_rounds.blocks):
            pair = out_rounds.blocks[len(out_far)]
            out_far.append([grid.cross(pair, shift) for shift in range(1, groups)])

    def tie_out(rounds, *values):
        nonlocal out_far
        out_far, *values = tie_rounds([out_rounds] + rounds, out_far, *values)
        return values

    into_in, sliced = tie_out([x_rounds], into_in, sliced)
    x_rounds.line()
    x_rounds.row()
    by_chip = grid.swap(sliced)
    out_rounds.row()
    into_rows = pack(
        [into_in[0][0].T, into_in[1].T, into_in[2][0].T, into_in[3].T], LANES
    )
    by_chip, into_rows, down_in = tie_out([x_rounds], by_chip, into_rows, down_in)
    part_rows = own_rows + EXTRA
    by_chip = by_chip.reshape(chips * part_rows, 3 * width)
    x_rounds.line()
    x_rounds.row()
    out_rounds.line()
    out_rounds.row()
    by_group = [by_chip] + [grid.cross(by_chip, shift) for shift in range(1, groups)]
    down_rows = pack([down_in[0][0], down_in[1]], LANES)
    by_group, down_rows, cotangent = tie_out([x_rounds], by_group, down_rows, cotangent)
    weight_pieces, order = [], []
    for shift, piece in enumerate(by_group):
        for core in range(CORES):
            weight_pieces.append(grid.hop(piece, dc=1) if core else piece)
            for chip in range(chips):
                order.append(
                    ((grid.group - shift) % groups * chips + chip) * CORES
                    + (grid.core + core) % CORES
                )
    used = -(-meta.size // (3 * width))
    meta_all = jnp.stack(
        [
            piece.reshape(chips, part_rows, 3 * width)[:, own_rows : own_rows + used]
            for piece in weight_pieces
        ]
    ).reshape(devices, -1)
    meta_all = meta_all[:, : meta.size].astype(f32).reshape(devices, meta_rows, row_count)

    def told_by(dg, chip, dc):
        return (dg * CORES + dc) * chips + chip

    by_place = jnp.stack(
        [
            told_by((grid.group - g) % groups, jnp.int32(chip), (grid.core - c) % CORES)
            for g in range(groups)
            for chip in range(chips)
            for c in range(CORES)
        ]
    )
    small_all = jnp.take(meta_all[:, 2 * TOP + 1 :], by_place, axis=0).reshape(devices, -1)
    own_features = norm_gain.shape[0]
    gains_in = small_all[:, :own_features].reshape(-1)
    gains_post = small_all[:, own_features : 2 * own_features].reshape(-1)
    gate_vector = small_all[:, 2 * own_features : 3 * own_features].reshape(-1)
    qkv_bias = small_all[:, 3 * own_features : small_count].reshape(3, chips, width)
    bias_here = lax.dynamic_index_in_dim(qkv_bias, grid.chip, 1, keepdims=False).reshape(-1)
    offsets = [
        told_by(dg, (grid.a - da) % na * nb + (grid.b - db) % nb, dc)
        for dg in range(groups)
        for da in slots
        for dc in range(CORES)
        for db in range(nb)
    ]
    told = jnp.take(meta_all[:, : 2 * TOP + 1], jnp.stack(offsets), axis=0)
    told = told.reshape(groups, na, CORES, nb, 2 * TOP + 1, row_count)
    plane_lengths = told[0, :, 0, :, 2 * TOP, 0].reshape(chips).astype(jnp.int32)
    here = jnp.concatenate([jnp.stack([grid.a, grid.b]).astype(jnp.int32), plane_lengths])
    valid_rows = positions < lengths[0]
    grad_rows = jnp.where(valid_rows[:, None], cotangent, jnp.zeros_like(cotangent))
    grad_rounds = RowRounds(grad_rows)
    while len(x_rounds.blocks) < na:
        x_rounds.row()
    out_rounds.line()
    out_rounds.row()
    out_cross()
    x_blocks, weight_pieces, bias_here, gains_in, here = tie_out(
        [grad_rounds], x_rounds.all(), weight_pieces, bias_here, gains_in, here
    )

    inputs = layer_input.astype(f32)
    out_rounds.row()
    out_cross()
    out_cross()
    grad_rounds.line()
    grad_rounds.row()
    normed_first, heads_weight, raw = project(
        x_blocks, gains_in[None], weight_pieces, own_rows, part_rows,
        jnp.stack(order).astype(jnp.int32),
    )
    low, sent = attention(here, raw, bias_here[None], row_count, nb, heads_here)
    low, sent = tie_out([], low, sent)

    while len(out_far) < na:
        out_cross()
    grad_rounds.line()
    pieces, order = [], []
    for dc in range(CORES):
        for da in slots:
            for dg in range(groups):
                pair = out_far[da][dg - 1] if dg else out_rounds.blocks[da]
                pieces.append(grid.hop(pair, dc=1) if dc else pair)
                order += [place_of(da, db, dc, dg) for db in range(nb)]
    out_weight = pack(pieces, size=own_rows, order=jnp.stack(order).astype(jnp.int32))
    arrived = grid.swap(sent.reshape(chips, row_count, width))
    arrived, out_weight = tie(arrived, out_weight)

    far_grads, far_rows, flying = [], [], []
    crossings = [(what, s) for s in slots for what in ("grads", "rows")]

    def cross_step():
        if crossings and two:
            what, s = crossings[0]
            source, goes = (
                (grad_rounds, far_grads) if what == "grads" else (second_rounds, far_rows)
            )
            if s < len(source.blocks):
                crossings.pop(0)
                flying.append((goes, grid.cross(source.blocks[s], 1)))

    grad_rounds.line()
    grad_rounds.row()
    cross_step()
    context = jnp.transpose(arrived, (1, 0, 2)).reshape(row_count, feature_count)
    residual = inputs + dot(context, out_weight, ((1,), (0,)))
    unit_second, factor_second = unit_norm(residual)
    normed_second = (unit_second * gains_post).astype(bf16)

    expert = (lax.axis_index("ep") // HALVES).astype(jnp.int32)
    expert, far_expert = (jnp.stack([expert, jnp.int32(n)]) for n in (1, 0))
    vector_row = gate_vector[None]
    told = jnp.swapaxes(told[..., : 2 * TOP, :], 2, 3)
    second_rounds = PairRounds(normed_second)
    own = {"rows": [], "grads": [], "middle": [], "gate": [], "up": [], "vector": []}

    def work(s):
        own["rows"].append(with_other(second_rounds.blocks[s]))
        own["grads"].append(with_other(grad_rounds.blocks[s]))
        middle, gate, up, *terms, vector = experts(
            expert, told[0, s], vector_row, own["rows"][s], own["grads"][s],
            into_rows, down_rows, sizes[0], True,
        )
        for name, value in (("middle", middle), ("gate", gate), ("up", up), ("vector", vector)):
            own[name].append(value)
        return terms

    def add_cores(terms):
        arriving = grid.hop(terms[-1], dc=1)
        return [
            (
                terms[t].astype(f32)
                + arriving[2 * t * row_count : 2 * (t + 1) * row_count].astype(f32)
            ).astype(bf16)
            for t in range(nb)
        ]

    def step_tie(*values):
        nonlocal own, into_rows, down_rows, flying
        arrivals = [rows for _, rows in flying]
        own, arrivals, into_rows, down_rows, *values = tie_rounds(
            [grad_rounds, second_rounds], own, arrivals, into_rows, down_rows, *values
        )
        for (goes, _), rows in zip(flying, arrivals):
            goes.append(rows)
        flying = []
        return values

    def line_sum(rowed, sums, s):
        total = rowed[s] if sums is None else rowed[s] + sums.astype(f32)
        return grid.hop(total.astype(bf16), da=1) if s else total

    def far_work(shift, s):
        rows, grads = with_other(far_rows[s]), with_other(far_grads[s])
        units = experts(
            far_expert, told[shift, s], vector_row, rows, grads,
            into_rows, down_rows, sizes[0], False,
        )
        return rows, grads, units[:3]

    def flat(lists):
        return [block for blocks in lists for block in blocks]

    rowed, terms, far = {}, {}, []
    sums = None
    for s in slots:
        second_rounds.line()
        cross_step()
        if s:
            grad_rounds.rest()
        if s >= 2:
            rowed[s - 1] = grid.row_sum(add_cores(terms[s - 1]))
        if s >= 3:
            sums = line_sum(rowed, sums, s - 2)
        terms[s] = work(s)
        rowed, terms, sums = step_tie(rowed, terms, sums)
    cross_step()
    rowed[na - 1] = grid.row_sum(add_cores(terms[na - 1]))
    if na > 2:
        sums = line_sum(rowed, sums, na - 2)
    own_gate = weight_grad(own["gate"], flat(own["rows"]), sizes)
    rowed, terms, sums, own_gate = step_tie(rowed, terms, sums, own_gate)
    cross_step()
    sums = line_sum(rowed, sums, na - 1)
    rowed[0] = grid.row_sum(add_cores(terms[0]))
    own_up = weight_grad(own["up"], flat(own["rows"]), sizes)
    own_down = weight_grad(own["middle"], flat(own["grads"]), sizes)
    rowed, sums, own_up, own_down = step_tie(rowed, sums, own_up, own_down)

    both_sums = line_sum(rowed, sums, 0)
    second_grad = both_sums[:row_count]
    outs = residual + both_sums[row_count:]
    output = jnp.where(valid_rows[:, None], outs, 0.0).astype(bf16)
    grad_float = grad_rows.astype(f32)
    post_gain_grad = jnp.sum(second_grad * unit_second, axis=0)
    residual_grad = grad_float + norm_backward(
        second_grad, unit_second, factor_second, gains_post
    )
    attended_grad = residual_grad.astype(bf16)
    context_grad = dot(attended_grad, out_weight, ((1,), (1,))).astype(bf16)
    sent = jnp.transpose(context_grad.reshape(row_count, chips, width), (1, 0, 2))
    arrived = grid.swap(sent)
    cross_step()
    if two:
        far.append(far_work(1, 0))
    totals = [[own_gate[0], own_up[0], own_down[0]]]
    shared = [part[1] for part in (own_gate, own_up, own_down)]
    arrived, attended_grad, far, shared, totals = step_tie(
        arrived, attended_grad, far, shared, totals
    )

    def own_features_of(values, core, group):
        parts = values.reshape(row_count, groups, chips, CORES, own_rows)
        parts = lax.dynamic_index_in_dim(parts, core, 3, keepdims=False)
        parts = lax.dynamic_index_in_dim(parts, group, 1, keepdims=False)
        return parts.reshape(row_count, chips * own_rows)

    projected_grad, bias_here_grad = attention_grad(
        here, low, arrived.reshape(-1, width), row_count, nb, heads_here
    )
    first_terms = dot(projected_grad, heads_weight, ((1,), (1,))).astype(bf16)
    out_parts = []
    for shift in range(groups):
        group = (grid.group + shift) % groups
        mine, other = (
            dot(own_features_of(context, core, group), attended_grad, ((0,), (0,))).astype(bf16)
            for core in (grid.core, 1 - grid.core)
        )
        total = mine.astype(f32) + grid.hop(other, dc=1).astype(f32)
        out_parts.append(total.astype(bf16))
    while crossings and two:
        cross_step()
    shared_far = [
        [grid.cross(part, shift) for shift in range(1, groups)] for part in shared[:1]
    ]
    first_terms, projected_grad, out_parts, far, shared_far = step_tie(
        first_terms, projected_grad, out_parts, far, shared_far
    )

    def in_order(*parts):
        parts = [part.astype(f32) for part in parts]
        if two:
            return parts[0] + parts[1]
        total = 0.0
        for group in range(groups):
            far_by = (grid.group - group) % groups
            total = total + sum(
                jnp.where(far_by == shift, part, 0.0) for shift, part in enumerate(parts)
            )
        return total

    slot_first = first_terms.reshape(na, nb * row_count, feature_count)

    def end_tie(*values):
        nonlocal far, into_rows, down_rows
        far, into_rows, down_rows, *values = tie(far, into_rows, down_rows, *values)
        return values

    def far_grad(units, place):
        before = [totals[0][units]] if two else ()
        return weight_grad(
            [work[2][(1, 2, 0)[units]] for work in far], flat(work[place] for work in far),
            sizes[:1], before,
        )[0]

    qkv_grad = dot(normed_first, projected_grad, ((0,), (0,))).astype(bf16)
    half = chips * own_rows // 2
    first_sums = line_sum(slot_first, None, 1) if na > 1 else None
    crossed = [[grid.cross(part[:half], n + 1)] for n, part in enumerate(out_parts[1:])]
    if two:
        far.append(far_work(1, 1))
    slot_first, qkv_grad, crossed, out_parts, first_sums = end_tie(
        slot_first, qkv_grad, crossed, out_parts, first_sums
    )
    if na > 2:
        first_sums = line_sum(slot_first, first_sums, 2)
    for n, part in enumerate(out_parts[1:]):
        crossed[n].append(grid.cross(part[half:], n + 1))
    qkv_grad = grid.scatter_core(qkv_grad.reshape(groups, chips, CORES, own_rows, 3 * width), 2)
    if two:
        far.append(far_work(1, 2 % na))
    slot_first, qkv_grad, crossed, out_parts, first_sums, shared = end_tie(
        slot_first, qkv_grad.astype(bf16), crossed, out_parts, first_sums, shared
    )
    for s in range(3, na):
        first_sums = line_sum(slot_first, first_sums, s)
    qkv_grad = grid.scatter_groups(qkv_grad).astype(bf16)
    out_total = out_parts[0].astype(f32)
    for halves in crossed:
        out_total = out_total + jnp.concatenate(halves, axis=0).astype(f32)
    out_rowed = grid.scatter_row(
        out_total.astype(bf16).reshape(na, nb, own_rows, feature_count)
    )
    shared_far.append([grid.cross(shared[1], shift) for shift in range(1, groups)])
    if two:
        if na > 3:
            far.append(far_work(1, 3))
        slot_first, first_sums, qkv_grad, out_rowed, shared = end_tie(
            slot_first, first_sums, qkv_grad, out_rowed, shared
        )
    first_terms_here = slot_first[0] if first_sums is None else line_sum(slot_first, first_sums, 0)
    first_grad = grid.row_sum(
        first_terms_here.astype(bf16).reshape(nb, row_count, feature_count)
    )
    qkv_grad = grid.swap(qkv_grad).reshape(chips, own_rows, 3, width)
    if two:
        gate_total = far_grad(0, 0)
        gate_total, first_grad, shared_far, shared, qkv_grad, out_rowed = end_tie(
            gate_total, first_grad, shared_far, shared, qkv_grad, out_rowed
        )
    out_weight_grad = grid.scatter_line(out_rowed)
    shared_far.append([grid.cross(shared[2], shift) for shift in range(1, groups)])
    unit_first, factor_first = unit_norm(inputs)
    input_part = norm_backward(first_grad, unit_first, factor_first, gains_in)
    layer_grad = (residual_grad + input_part).astype(bf16)
    qkv_weight_grad = jnp.transpose(qkv_grad, (1, 2, 0, 3)).reshape(own_rows, -1).astype(f32)
    if two:
        gate_grad, up_grad, down_grad = gate_total, far_grad(1, 0), far_grad(2, 1)
    else:
        second_blocks, grad_blocks = second_rounds.blocks, grad_rounds.blocks
        for shift in range(1, groups):
            totals, second_blocks, grad_blocks = tie(totals, second_blocks, grad_blocks)
            far_grads, far_rows = (
                [grid.cross(rows, shift) for rows in source]
                for source in (grad_blocks, second_blocks)
            )
            far = [far_work(shift, s) for s in slots]
            totals.append([far_grad(0, 0), far_grad(1, 0), far_grad(2, 1)])
        gate_grad, up_grad, down_grad = (in_order(*parts) for parts in zip(*totals))
    shared_gate_grad, shared_up_grad, shared_down_grad = (
        in_order(here_part, *parts) for here_part, parts in zip(shared, shared_far)
    )

    vector_grad = sum(own["vector"])[0]
    gain_grad = jnp.sum(first_terms.astype(f32) * normed_first.astype(f32), axis=0) / gains_in
    bias_grad = jnp.zeros((3, chips, width), f32)
    bias_grad = lax.dynamic_update_slice(
        bias_grad, bias_here_grad.reshape(3, 1, width), (0, grid.chip, 0)
    )
    vectors = jnp.concatenate(
        [
            gain_grad.reshape(devices, -1),
            post_gain_grad.reshape(devices, -1),
            vector_grad.reshape(devices, -1),
            bias_grad.reshape(devices, -1),
        ],
        axis=1,
    ).reshape(groups, na, nb, CORES, -1)
    vectors = grid.scatter_core(vectors, 3)
    vectors = grid.scatter_groups(vectors)
    vectors = grid.scatter_line(grid.scatter_row(vectors))
    return (
        output,
        layer_grad,
        vectors[:own_features],
        qkv_weight_grad,
        vectors[3 * own_features :],
        out_weight_grad,
        vectors[own_features : 2 * own_features],
        gate_grad.T[None],
        up_grad.T[None],
        down_grad[None],
        shared_gate_grad.T,
        shared_up_grad.T,
        shared_down_grad,
        vectors[2 * own_features : 3 * own_features],
    )


def solution(mesh):
    rows = P(("dp", "ep"), None)
    split = P(("dp", "ep"))
    parts = P("ep", None, None)
    return jax.shard_map(
        local,
        mesh=mesh,
        in_specs=(
            rows,
            split,
            rows,
            rows,
            rows,
            split,
            rows,
            split,
            rows,
            split,
            parts,
            parts,
            parts,
            P(None, "ep"),
            P(None, "ep"),
            P("ep", None),
            split,
        ),
        out_specs=(
            rows,
            rows,
            split,
            rows,
            split,
            rows,
            split,
            parts,
            parts,
            parts,
            P(None, "ep"),
            P(None, "ep"),
            P("ep", None),
            split,
        ),
        check_vma=False,
    )
```
